32 devices in a mesh: expert: 8 (over z, y), tensor: 4 (over x, core).
Axes of the slice: x: 2, y: 2, z: 4, core: 2. Of those that a mesh axis runs over, the one named last changes fastest.
Arguments:
- tokens: bfloat16 [1024, 5120], P('expert', 'tensor'), may hold values from -6 to 6
- out_grad: bfloat16 [1024, 5120], P('expert', 'tensor'), may hold values from -6 to 6
- expert_ids: int32 [1024, 6], P('expert'), may hold values from 0 to 15, as said below
- router_probs: float32 [1024, 16], P('expert'), may hold values from 0 to 1, as said below
- router_weight: bfloat16 [5120, 16], P('tensor'), may hold values from -0.29882812 to 0.29882812
- gate_weight: bfloat16 [16, 5120, 768], P('expert', 'tensor'), may hold values from -0.078125 to 0.078125
- up_weight: bfloat16 [16, 5120, 768], P('expert', 'tensor'), may hold values from -0.078125 to 0.078125
- down_weight: bfloat16 [16, 768, 5120], P('expert', None, 'tensor'), may hold values from -0.21875 to 0.21875
- gate_saved: bfloat16 [16, 512, 768], P('expert'), may hold values from -6 to 6
- up_saved: bfloat16 [16, 512, 768], P('expert'), may hold values from -6 to 6
- shared_gate: bfloat16 [5120, 2048], P(None, 'tensor'), may hold values from -0.078125 to 0.078125
- shared_up: bfloat16 [5120, 2048], P(None, 'tensor'), may hold values from -0.078125 to 0.078125
- shared_down: bfloat16 [2048, 5120], P('tensor'), may hold values from -0.125 to 0.125
Outputs:
- input_grad: bfloat16 [1024, 5120], P('expert', 'tensor')
The draws below stay inside these ranges and needn't reach their ends.
Inputs may be any that keep to these rules, and one draw needn't show every extreme that they name: `expert_ids`: each row names 6 different experts. `router_probs`: each row is positive and sums to one.
All inputs are finite; a program needn't handle non-finite values.
Results may differ from the reference program's by a relative error of at most 0.014.
Values may be sent and summed in bfloat16 or wider, within the bound.
No kernel may reach another device: no remote copies, remote signals or barrier semaphores. Data moves between devices by JAX's collectives and lax.ppermute only.
A program may use at most 128 MiB of HBM per device.

```python
import jax
import jax.numpy as jnp
from jax import lax

D = 5120
ROUTED_FF = 768
SHARED_FF = 2048
TOP = 6
TOK_DEV = 128
EXPERTS = 16
CAP = 64
SLOTS = 512
TOKENS = 1024
N_TENSOR = 4


def route_scores(key):
    base_score = jax.random.randint(key, (TOKENS, EXPERTS), 0, 65536, dtype=jnp.int32)
    popular = jax.random.randint(jax.random.fold_in(key, 11), (EXPERTS,), 0, 16384, dtype=jnp.int32)
    return base_score + popular[None, :]


def draw_expert_ids(key, part):
    scores = route_scores(key)
    ranked = scores * EXPERTS + jnp.arange(EXPERTS, dtype=jnp.int32)[None, :]
    values, chosen = lax.top_k(ranked, TOP)
    return chosen.astype(jnp.int32)


def draw_router_probs(key, part):
    scores = route_scores(key).astype(jnp.float32) / 65536.0
    key = jax.random.fold_in(key, 7)
    jitter = jax.random.normal(key, scores.shape, jnp.float32)
    logits = 6.0 * scores + 0.3 * jitter
    return jax.nn.softmax(logits, axis=1)


def steps_of(own_key, extent, shards, low, largest):
    def one(axis_at, parts):
        steps = jax.random.uniform(jax.random.fold_in(jax.random.fold_in(own_key, 6), axis_at), (parts,), jnp.float32, low / len(shards), largest / len(shards))
        return jnp.repeat(jnp.exp(steps), extent[axis_at] // parts).reshape((-1,) + (1,) * (len(extent) - axis_at - 1))

    factor_of = one(*shards[0])
    for cut in shards[1:]:
        factor_of = factor_of * one(*cut)
    return factor_of


def normal_values(key, shape, width, reach, shards=(), kind=jnp.bfloat16):
    array = width * jax.random.normal(key, shape, jnp.float32)
    if shards:
        array = array * steps_of(key, shape, shards, -0.22, 0.18)
    return jnp.clip(array, -reach, reach).astype(kind)


def setup_inputs(seed: int = 0) -> dict:
    splits = jax.random.split(jax.random.key(seed), 14)
    return {
        "tokens": normal_values(splits[0], (TOKENS, D), 1.0, 6.0, ((0, 8), (1, 4))),
        "out_grad": normal_values(splits[1], (TOKENS, D), 1.0, 6.0, ((0, 8), (1, 4))),
        "expert_ids": draw_expert_ids(jax.random.fold_in(splits[13], 71), 0),
        "router_probs": draw_router_probs(jax.random.fold_in(splits[13], 71), 0),
        "router_weight": normal_values(splits[4], (D, EXPERTS), 0.05, 0.29882812, ((0, 4),)),
        "gate_weight": normal_values(splits[5], (EXPERTS, D, ROUTED_FF), D ** -0.5, 0.078125, ((0, 8), (1, 4))),
        "up_weight": normal_values(splits[6], (EXPERTS, D, ROUTED_FF), D ** -0.5, 0.078125, ((0, 8), (1, 4))),
        "down_weight": normal_values(splits[7], (EXPERTS, ROUTED_FF, D), ROUTED_FF ** -0.5, 0.21875, ((0, 8), (2, 4))),
        "gate_saved": normal_values(splits[8], (EXPERTS, SLOTS, ROUTED_FF), 1.0, 6.0, ((0, 8),)),
        "up_saved": normal_values(splits[9], (EXPERTS, SLOTS, ROUTED_FF), 1.0, 6.0, ((0, 8),)),
        "shared_gate": normal_values(splits[10], (D, SHARED_FF), D ** -0.5, 0.078125, ((1, 4),)),
        "shared_up": normal_values(splits[11], (D, SHARED_FF), D ** -0.5, 0.078125, ((1, 4),)),
        "shared_down": normal_values(splits[12], (SHARED_FF, D), SHARED_FF ** -0.5, 0.125, ((0, 4),)),
    }


def silu_parts(preact):
    sigmoid_value = jax.nn.sigmoid(preact)
    return preact * sigmoid_value, sigmoid_value * (1.0 + preact * (1.0 - sigmoid_value))


def route_slots(expert_ids):
    blocks = expert_ids.reshape(-1, TOK_DEV * TOP)
    onehot = (blocks[:, :, None] == jnp.arange(EXPERTS, dtype=jnp.int32)[None, None, :]).astype(jnp.int32)
    before = jnp.cumsum(onehot, axis=1) - onehot
    return jnp.sum(before * onehot, axis=2).astype(jnp.int32).reshape(-1)


def reference(tokens, out_grad, expert_ids, router_probs, router_weight, gate_weight, up_weight, down_weight, gate_saved, up_saved, shared_gate, shared_up, shared_down):
    route_count = TOKENS * TOP
    slot_index = route_slots(expert_ids)
    flat_ids = expert_ids.reshape(-1)
    route_ids = jnp.arange(route_count, dtype=jnp.int32)
    block_of = (route_ids // TOP) // TOK_DEV
    slot_place = jnp.where(slot_index < CAP, block_of * CAP + slot_index, SLOTS).astype(jnp.int32)
    slot_table = jnp.full((EXPERTS, SLOTS), -1, dtype=jnp.int32).at[flat_ids, slot_place].set(route_ids, mode="drop")
    gate_value = jnp.take_along_axis(router_probs, expert_ids, axis=1).reshape(-1)
    group_cols = D // N_TENSOR

    def per_expert(state_pair, inputs):
        routed, scores = state_pair
        slot_entry, w_gate, w_up, w_down, saved_gate, saved_up = inputs
        valid_mask = slot_entry >= 0
        safe_route = jnp.where(valid_mask, slot_entry, 0).astype(jnp.int32)
        route_rows = jnp.where(valid_mask[:, None], out_grad[safe_route // TOP], jnp.zeros((), out_grad.dtype))
        pieces = jnp.einsum("sqd,fqd->qsf", route_rows.reshape(SLOTS, N_TENSOR, group_cols).astype(jnp.float32), w_down.reshape(ROUTED_FF, N_TENSOR, group_cols).astype(jnp.float32))
        rounded = lax.optimization_barrier(pieces.astype(jnp.bfloat16))
        hidden_grad = jnp.sum(rounded.astype(jnp.float32), axis=0)
        active, slope_term = silu_parts(saved_gate.astype(jnp.float32))
        up_full = saved_up.astype(jnp.float32)
        d_gate = (hidden_grad * up_full * slope_term).astype(jnp.bfloat16)
        d_up = (hidden_grad * active).astype(jnp.bfloat16)
        score_rows = jnp.sum(up_full * d_up.astype(jnp.float32), axis=1).astype(jnp.bfloat16)
        grad_rows = jnp.einsum("sf,df->sd", d_gate.astype(jnp.float32), w_gate.astype(jnp.float32)) + jnp.einsum("sf,df->sd", d_up.astype(jnp.float32), w_up.astype(jnp.float32))
        grad_rows = grad_rows.astype(jnp.bfloat16)
        weight = jnp.where(valid_mask, gate_value[safe_route], 0.0)
        routed = routed.at[safe_route // TOP].add(weight[:, None] * grad_rows.astype(jnp.float32))
        scores = scores.at[jnp.where(valid_mask, slot_entry, route_count)].set(score_rows.astype(jnp.float32), mode="drop")
        return (routed, scores), None

    initial = (jnp.zeros((TOKENS, D), jnp.float32), jnp.zeros((route_count,), jnp.float32))
    (routed, scores), ignored = lax.scan(per_expert, initial, (slot_table, gate_weight, up_weight, down_weight, gate_saved, up_saved))
    route_score = scores.reshape(TOKENS, TOP)
    route_gates = gate_value.reshape(TOKENS, TOP)
    onehot = (expert_ids[:, :, None] == jnp.arange(EXPERTS, dtype=jnp.int32)[None, None, :]).astype(jnp.float32)
    prob_grad = jnp.sum(onehot * route_score[:, :, None], axis=1)
    gate_total = jnp.sum(route_gates * route_score, axis=1)
    logit_grad = (router_probs * (prob_grad - gate_total[:, None])).astype(jnp.bfloat16)
    router_part = jnp.dot(logit_grad, router_weight.T, preferred_element_type=jnp.float32)
    gate_pre = jnp.dot(tokens, shared_gate, preferred_element_type=jnp.float32)
    up_pre = jnp.dot(tokens, shared_up, preferred_element_type=jnp.float32)
    hidden_pre = jnp.dot(out_grad, shared_down.T, preferred_element_type=jnp.float32)
    active, slope_term = silu_parts(gate_pre)
    shared_dgate = (hidden_pre * up_pre * slope_term).astype(jnp.bfloat16)
    shared_dup = (hidden_pre * active).astype(jnp.bfloat16)
    group_units = SHARED_FF // N_TENSOR
    dgate_groups = jnp.transpose(shared_dgate.reshape(TOKENS, N_TENSOR, group_units), (1, 0, 2))
    dup_groups = jnp.transpose(shared_dup.reshape(TOKENS, N_TENSOR, group_units), (1, 0, 2))
    wgate_groups = jnp.transpose(shared_gate.reshape(D, N_TENSOR, group_units), (1, 0, 2))
    wup_groups = jnp.transpose(shared_up.reshape(D, N_TENSOR, group_units), (1, 0, 2))

    def per_group(total, inputs):
        dgate_piece, dup_piece, wgate_piece, wup_piece = inputs
        term = jnp.dot(dgate_piece, wgate_piece.T, preferred_element_type=jnp.float32) + jnp.dot(dup_piece, wup_piece.T, preferred_element_type=jnp.float32)
        rounded = lax.optimization_barrier(term.astype(jnp.bfloat16))
        return total + rounded.astype(jnp.float32), None

    shared_part, ignored_two = lax.scan(per_group, jnp.zeros((TOKENS, D), jnp.float32), (dgate_groups, dup_groups, wgate_groups, wup_groups))
    return (shared_part + routed + router_part).astype(jnp.bfloat16)
```

```python
import jax
import jax.numpy as jnp
from jax import lax
from jax.sharding import PartitionSpec as P


def silu_parts(preact):
    sigmoid_value = jax.nn.sigmoid(preact)
    return (preact * sigmoid_value, sigmoid_value * (1.0 + preact * (1.0 - sigmoid_value)))


def per_device_wide(
    tokens,
    out_grad,
    expert_ids,
    router_probs,
    router_weight,
    gate_weight,
    up_weight,
    down_weight,
    gate_saved,
    up_saved,
    shared_gate,
    shared_up,
    shared_down,
):
    groups = lax.axis_size("expert")
    local_count, slot_count, hidden_units = gate_saved.shape
    capacity = slot_count // groups
    token_rows, route_width = expert_ids.shape
    expert_total = router_probs.shape[1]
    feature_cols = tokens.shape[1]
    column_total = local_count * groups * capacity
    flat_ids = expert_ids.reshape(-1)
    onehot = (flat_ids[:, None] == jnp.arange(expert_total, dtype=jnp.int32)[None, :]).astype(
        jnp.int32
    )
    slot_index = jnp.sum((jnp.cumsum(onehot, axis=0) - onehot) * onehot, axis=1)
    kept_mask = slot_index < capacity
    owner_group = flat_ids // local_count
    local_expert = flat_ids % local_count
    column_id = jnp.where(
        kept_mask, local_expert * (groups * capacity) + owner_group * capacity + slot_index, -1
    )
    column_grid = column_id.reshape(token_rows, route_width)
    column_match = (
        column_grid[:, :, None] == jnp.arange(column_total, dtype=jnp.int32)[None, None, :]
    )
    placement = jnp.sum(column_match.astype(jnp.float32), axis=1).astype(jnp.bfloat16)
    sectioning = jnp.einsum(
        "tc,td->cd", placement, out_grad, preferred_element_type=jnp.float32
    ).astype(jnp.bfloat16)
    outgoing = sectioning.reshape(local_count, groups, capacity * feature_cols)
    token_piece = lax.all_gather(tokens, "tensor", axis=1, tiled=True)
    grad_piece = lax.all_gather(out_grad, "tensor", axis=1, tiled=True)
    gate_pre = jnp.dot(token_piece, shared_gate, preferred_element_type=jnp.float32)
    up_pre = jnp.dot(token_piece, shared_up, preferred_element_type=jnp.float32)
    hidden_pre = jnp.einsum(
        "tc,fc->tf", grad_piece, shared_down, preferred_element_type=jnp.float32
    )
    active, slope_term = silu_parts(gate_pre)
    shared_dgate = (hidden_pre * up_pre * slope_term).astype(jnp.bfloat16)
    shared_dup = (hidden_pre * active).astype(jnp.bfloat16)
    shared_term = jnp.einsum(
        "tf,df->td", shared_dgate, shared_gate, preferred_element_type=jnp.float32
    ) + jnp.einsum("tf,df->td", shared_dup, shared_up, preferred_element_type=jnp.float32)
    shared_part = lax.psum_scatter(
        shared_term.astype(jnp.bfloat16), "tensor", scatter_dimension=1, tiled=True
    ).astype(jnp.float32)
    arrived = lax.all_to_all(outgoing, "expert", split_axis=1, concat_axis=1, tiled=True)
    arrived = arrived.reshape(local_count, slot_count, feature_cols)
    partial_hidden = jnp.einsum(
        "esd,efd->esf", arrived, down_weight, preferred_element_type=jnp.float32
    )
    up_full = up_saved.astype(jnp.float32)
    hidden_grad = lax.psum(partial_hidden.astype(jnp.bfloat16), "tensor").astype(jnp.float32)
    active, slope_term = silu_parts(gate_saved.astype(jnp.float32))
    d_gate = (hidden_grad * up_full * slope_term).astype(jnp.bfloat16)
    d_up = (hidden_grad * active).astype(jnp.bfloat16)
    score_rows = jnp.sum(up_full * d_up.astype(jnp.float32), axis=2).astype(jnp.bfloat16)
    expert_grad = jnp.einsum(
        "esf,edf->esd", d_gate, gate_weight, preferred_element_type=jnp.float32
    ) + jnp.einsum("esf,edf->esd", d_up, up_weight, preferred_element_type=jnp.float32)
    expert_grad = expert_grad.astype(jnp.bfloat16)
    back_grad, back_score = (
        lax.all_to_all(
            expert_grad.reshape(local_count, groups, capacity * feature_cols),
            "expert",
            split_axis=1,
            concat_axis=1,
            tiled=True,
        ),
        lax.all_to_all(
            score_rows.reshape(local_count, groups, capacity),
            "expert",
            split_axis=1,
            concat_axis=1,
            tiled=True,
        ),
    )
    returned_rows = back_grad.reshape(column_total, feature_cols)
    returned_scores = back_score.reshape(column_total).astype(jnp.float32)
    kept_value = kept_mask.astype(jnp.float32)
    probs_rows = jnp.repeat(router_probs, route_width, axis=0)
    onehot_float = onehot.astype(jnp.float32)
    gate_value = jnp.sum(onehot_float * probs_rows, axis=1)
    route_weight = (gate_value * kept_value).reshape(token_rows, route_width)
    combine_weight = jnp.sum(jnp.where(column_match, route_weight[:, :, None], 0.0), axis=1)
    routed_part = jnp.dot(
        combine_weight,
        returned_rows.astype(jnp.float32),
        precision=lax.Precision.HIGHEST,
        preferred_element_type=jnp.float32,
    )
    safe_column = jnp.maximum(column_id, 0)
    route_score = returned_scores[safe_column] * kept_value
    prob_grad = jnp.sum(
        (onehot_float * route_score[:, None]).reshape(token_rows, route_width, expert_total), axis=1
    )
    gate_total = jnp.sum((gate_value * route_score).reshape(token_rows, route_width), axis=1)
    logit_grad = (router_probs * (prob_grad - gate_total[:, None])).astype(jnp.bfloat16)
    router_part = jnp.einsum(
        "te,de->td", logit_grad, router_weight, preferred_element_type=jnp.float32
    )
    return (shared_part + routed_part + router_part).astype(jnp.bfloat16)


def ring_place(position):
    position = position % 8
    return jnp.where(position < 4, 2 * position, 15 - 2 * position)


def per_device_ring(
    tokens,
    out_grad,
    expert_ids,
    router_probs,
    router_weight,
    gate_weight,
    up_weight,
    down_weight,
    gate_saved,
    up_saved,
    shared_gate,
    shared_up,
    shared_down,
):
    f32, bf16 = jnp.float32, jnp.bfloat16
    local_count, slot_count, hidden_units = gate_saved.shape
    groups = lax.axis_size("expert")
    capacity = slot_count // groups
    rows, cols = tokens.shape
    expert_total = router_probs.shape[1]
    tiles = expert_total // 8
    order = [0, 2, 4, 6, 7, 5, 3, 1]
    ahead = [(order[i], order[(i + 1) % 8]) for i in range(8)]
    behind = [(order[i], order[(i - 1) % 8]) for i in range(8)]
    x_pairs = [(i, i ^ 2) for i in range(4)]
    core_pairs = [(i, i ^ 1) for i in range(4)]
    me = lax.axis_index("expert")
    place = jnp.where(me % 2 == 0, me // 2, 7 - me // 2)
    t_index = lax.axis_index("tensor")
    core = t_index % 2

    def swap_x(a):
        return lax.ppermute(a, "tensor", x_pairs)

    def swap_core(a):
        return lax.ppermute(a, "tensor", core_pairs)

    tok_core, grad_core = swap_core(tokens), swap_core(out_grad)
    tok_x, grad_x = swap_x(tokens), swap_x(out_grad)

    ids_t = expert_ids.T
    member = jnp.any(
        ids_t[None, :, :] == jnp.arange(expert_total, dtype=jnp.int32)[:, None, None], axis=1
    )
    lower = (jnp.arange(rows)[:, None] < jnp.arange(rows)[None, :]).astype(bf16)
    before = jnp.dot(member.astype(bf16), lower, preferred_element_type=f32)
    slot_t = jnp.where(member & (before < capacity), before, -1.0).astype(bf16)
    probs_t = router_probs.T
    high = probs_t.astype(bf16)
    low = (probs_t - high.astype(f32)).astype(bf16)
    meta = jnp.concatenate(
        [a[8 * i : 8 * i + 8] for a in (slot_t, high, low) for i in range(tiles)]
        + [jnp.zeros((8, cols - 3 * tiles * rows), bf16)],
        axis=1,
    )
    payload = jnp.concatenate([out_grad, meta], axis=0)
    half = (rows + 8) // 2

    fore, back = payload, payload
    blocks = {0: payload}
    for r in range(1, 4):
        fore = lax.ppermute(fore, "expert", ahead)
        back = lax.ppermute(back, "expert", behind)
        blocks[-r], blocks[r] = fore, back
    top = lax.ppermute(fore[:half], "expert", ahead)
    bottom = lax.ppermute(back[half:], "expert", behind)
    blocks[4] = jnp.concatenate([top, bottom], axis=0)

    first = me * local_count
    slot_iota = jnp.arange(capacity, dtype=jnp.int32).astype(bf16)
    contribution = {}
    for chunk in ((0, -1, 1), (-2, 2), (-3, 3), (4,)):
        data = jnp.stack([blocks[d] for d in chunk])
        count = len(chunk)
        info = data[:, rows:].reshape(count, 8, cols // rows, rows).transpose(0, 2, 1, 3)
        info = info[:, : 3 * tiles].reshape(count, 3, expert_total, rows)
        info = lax.dynamic_slice_in_dim(info, first, local_count, 2)
        match = info[:, 0, :, None, :] == slot_iota[None, None, :, None]
        gates = info[:, 1].astype(f32) + info[:, 2].astype(f32)
        placed = jnp.einsum(
            "best,btd->ebsd", match.astype(bf16), data[:, :rows], preferred_element_type=f32
        ).astype(bf16)
        placed = placed.reshape(local_count, count * capacity, cols)
        partial = jnp.einsum("esd,efd->esf", placed, down_weight, preferred_element_type=f32)
        partial = partial.astype(bf16)
        mine = lax.dynamic_index_in_dim(partial, core, 0, keepdims=False)
        other = lax.dynamic_index_in_dim(partial, 1 - core, 0, keepdims=False)
        chip = (mine.astype(f32) + swap_core(other).astype(f32)).astype(bf16)
        full = (chip.astype(f32) + swap_x(chip).astype(f32)).astype(bf16)
        pair = swap_core(full)
        hidden = jnp.stack([jnp.where(core == 0, full, pair), jnp.where(core == 0, pair, full)])
        hidden = hidden.astype(f32)
        starts = [ring_place(place + d) * capacity for d in chunk]
        gate_rows = jnp.concatenate(
            [lax.dynamic_slice_in_dim(gate_saved, s, capacity, 1) for s in starts], axis=1
        ).astype(f32)
        up_rows = jnp.concatenate(
            [lax.dynamic_slice_in_dim(up_saved, s, capacity, 1) for s in starts], axis=1
        ).astype(f32)
        active, slope_term = silu_parts(gate_rows)
        d_gate = (hidden * up_rows * slope_term).astype(bf16)
        d_up = (hidden * active).astype(bf16)
        score = jnp.sum(up_rows * d_up.astype(f32), axis=2).astype(bf16)
        grad = jnp.einsum("esf,edf->esd", d_gate, gate_weight, preferred_element_type=f32)
        grad = grad + jnp.einsum("esf,edf->esd", d_up, up_weight, preferred_element_type=f32)
        grad = grad.astype(bf16).reshape(local_count, count, capacity, cols)
        weights = jnp.where(match, gates[:, :, None, :], 0.0)
        w_high = weights.astype(bf16)
        w_low = (weights - w_high.astype(f32)).astype(bf16)
        grad_b = grad.transpose(1, 0, 2, 3).reshape(count, local_count * capacity, cols)
        w_high = w_high.reshape(count, local_count * capacity, rows)
        w_low = w_low.reshape(count, local_count * capacity, rows)
        token_rows = jnp.einsum("bct,bcd->btd", w_high, grad_b, preferred_element_type=f32)
        token_rows = token_rows + jnp.einsum(
            "bct,bcd->btd", w_low, grad_b, preferred_element_type=f32
        )
        score = score.reshape(local_count, count, capacity).astype(f32)
        token_score = jnp.sum(
            jnp.where(match, score.transpose(1, 0, 2)[:, :, :, None], 0.0), axis=2
        )
        wide = jnp.zeros((count, expert_total, rows), f32)
        wide = lax.dynamic_update_slice_in_dim(wide, token_score, first, 1)
        wide = jnp.concatenate(
            [wide[:, 8 * i : 8 * i + 8] for i in range(tiles)]
            + [jnp.zeros((count, 8, cols - tiles * rows), f32)],
            axis=2,
        )
        both = jnp.concatenate([token_rows, wide], axis=1)
        for i, d in enumerate(chunk):
            contribution[d] = both[i]

    top = lax.ppermute(contribution[4][:half].astype(bf16), "expert", ahead).astype(f32)
    bottom = lax.ppermute(contribution[4][half:].astype(bf16), "expert", behind).astype(f32)
    fore = jnp.concatenate([contribution[3][:half] + top, contribution[3][half:]], axis=0)
    back = jnp.concatenate([contribution[-3][:half], contribution[-3][half:] + bottom], axis=0)
    for d in (2, 1, 0):
        fore = lax.ppermute(fore.astype(bf16), "expert", ahead).astype(f32)
        back = lax.ppermute(back.astype(bf16), "expert", behind).astype(f32)
        if d:
            fore = fore + contribution[d]
            back = back + contribution[-d]
    total = contribution[0] + fore + back
    routed_part = total[:rows]

    def assemble(own, by_core, by_x):
        by_both = swap_core(by_x)
        wide = jnp.zeros((rows, 4 * cols), bf16)
        for piece, flip in ((own, 0), (by_core, 1), (by_x, 2), (by_both, 3)):
            at = jnp.bitwise_xor(t_index, flip) * cols
            wide = lax.dynamic_update_slice_in_dim(wide, piece, at, 1)
        return wide

    token_piece = assemble(tokens, tok_core, tok_x)
    grad_piece = assemble(out_grad, grad_core, grad_x)
    gate_pre = jnp.dot(token_piece, shared_gate, preferred_element_type=f32)
    up_pre = jnp.dot(token_piece, shared_up, preferred_element_type=f32)
    hidden_pre = jnp.einsum("tc,fc->tf", grad_piece, shared_down, preferred_element_type=f32)
    active, slope_term = silu_parts(gate_pre)
    shared_dgate = (hidden_pre * up_pre * slope_term).astype(bf16)
    shared_dup = (hidden_pre * active).astype(bf16)
    term = jnp.einsum("tf,df->td", shared_dgate, shared_gate, preferred_element_type=f32)
    term = term + jnp.einsum("tf,df->td", shared_dup, shared_up, preferred_element_type=f32)
    term = term.astype(bf16)

    def part(flip):
        at = jnp.bitwise_xor(t_index, flip) * cols
        return lax.dynamic_slice_in_dim(term, at, cols, 1)

    near = swap_core(part(1)).astype(f32) + part(0).astype(f32)
    far = swap_core(part(3)).astype(f32) + part(2).astype(f32)
    shared_part = near + swap_x(far.astype(bf16)).astype(f32)

    prob_grad = jnp.concatenate(
        [total[rows:, i * rows : (i + 1) * rows] for i in range(tiles)], axis=0
    ).T
    gate_total = jnp.sum(router_probs * prob_grad, axis=1, keepdims=True)
    logit_grad = (router_probs * (prob_grad - gate_total)).astype(bf16)
    router_part = jnp.einsum("te,de->td", logit_grad, router_weight, preferred_element_type=f32)
    return (shared_part + routed_part + router_part).astype(bf16)


def per_device(*args):
    tokens, router_probs, gate_weight = args[0], args[3], args[5]
    rows, cols = tokens.shape
    expert_total = router_probs.shape[1]
    ring = (
        lax.axis_size("expert") == 8
        and lax.axis_size("tensor") == 4
        and gate_weight.shape[0] == 2
        and expert_total % 8 == 0
        and cols % rows == 0
        and 3 * (expert_total // 8) * rows <= cols
    )
    return (per_device_ring if ring else per_device_wide)(*args)


def solution(mesh):
    return jax.shard_map(
        per_device,
        mesh=mesh,
        in_specs=(
            P("expert", "tensor"),
            P("expert", "tensor"),
            P("expert", None),
            P("expert", None),
            P("tensor", None),
            P("expert", "tensor", None),
            P("expert", "tensor", None),
            P("expert", None, "tensor"),
            P("expert", None, None),
            P("expert", None, None),
            P(None, "tensor"),
            P(None, "tensor"),
            P("tensor", None),
        ),
        out_specs=P("expert", "tensor"),
        check_vma=False,
    )
```

```python
import functools

import jax
import jax.numpy as jnp
from jax import lax
from jax.experimental import pallas as pl
from jax.experimental.pallas import tpu as pltpu
from jax.sharding import PartitionSpec as P


def silu_parts(preact):
    sigmoid_value = jax.nn.sigmoid(preact)
    return (preact * sigmoid_value, sigmoid_value * (1.0 + preact * (1.0 - sigmoid_value)))


def per_device_wide(
    tokens,
    out_grad,
    expert_ids,
    router_probs,
    router_weight,
    gate_weight,
    up_weight,
    down_weight,
    gate_saved,
    up_saved,
    shared_gate,
    shared_up,
    shared_down,
):
    groups = lax.axis_size("expert")
    local_count, slot_count, hidden_units = gate_saved.shape
    capacity = slot_count // groups
    token_rows, route_width = expert_ids.shape
    expert_total = router_probs.shape[1]
    feature_cols = tokens.shape[1]
    column_total = local_count * groups * capacity
    flat_ids = expert_ids.reshape(-1)
    onehot = (flat_ids[:, None] == jnp.arange(expert_total, dtype=jnp.int32)[None, :]).astype(
        jnp.int32
    )
    slot_index = jnp.sum((jnp.cumsum(onehot, axis=0) - onehot) * onehot, axis=1)
    kept_mask = slot_index < capacity
    owner_group = flat_ids // local_count
    local_expert = flat_ids % local_count
    column_id = jnp.where(
        kept_mask, local_expert * (groups * capacity) + owner_group * capacity + slot_index, -1
    )
    column_grid = column_id.reshape(token_rows, route_width)
    column_match = (
        column_grid[:, :, None] == jnp.arange(column_total, dtype=jnp.int32)[None, None, :]
    )
    placement = jnp.sum(column_match.astype(jnp.float32), axis=1).astype(jnp.bfloat16)
    sectioning = jnp.einsum(
        "tc,td->cd", placement, out_grad, preferred_element_type=jnp.float32
    ).astype(jnp.bfloat16)
    outgoing = sectioning.reshape(local_count, groups, capacity * feature_cols)
    token_piece = lax.all_gather(tokens, "tensor", axis=1, tiled=True)
    grad_piece = lax.all_gather(out_grad, "tensor", axis=1, tiled=True)
    gate_pre = jnp.dot(token_piece, shared_gate, preferred_element_type=jnp.float32)
    up_pre = jnp.dot(token_piece, shared_up, preferred_element_type=jnp.float32)
    hidden_pre = jnp.einsum(
        "tc,fc->tf", grad_piece, shared_down, preferred_element_type=jnp.float32
    )
    active, slope_term = silu_parts(gate_pre)
    shared_dgate = (hidden_pre * up_pre * slope_term).astype(jnp.bfloat16)
    shared_dup = (hidden_pre * active).astype(jnp.bfloat16)
    shared_term = jnp.einsum(
        "tf,df->td", shared_dgate, shared_gate, preferred_element_type=jnp.float32
    ) + jnp.einsum("tf,df->td", shared_dup, shared_up, preferred_element_type=jnp.float32)
    shared_part = lax.psum_scatter(
        shared_term.astype(jnp.bfloat16), "tensor", scatter_dimension=1, tiled=True
    ).astype(jnp.float32)
    arrived = lax.all_to_all(outgoing, "expert", split_axis=1, concat_axis=1, tiled=True)
    arrived = arrived.reshape(local_count, slot_count, feature_cols)
    partial_hidden = jnp.einsum(
        "esd,efd->esf", arrived, down_weight, preferred_element_type=jnp.float32
    )
    up_full = up_saved.astype(jnp.float32)
    hidden_grad = lax.psum(partial_hidden.astype(jnp.bfloat16), "tensor").astype(jnp.float32)
    active, slope_term = silu_parts(gate_saved.astype(jnp.float32))
    d_gate = (hidden_grad * up_full * slope_term).astype(jnp.bfloat16)
    d_up = (hidden_grad * active).astype(jnp.bfloat16)
    score_rows = jnp.sum(up_full * d_up.astype(jnp.float32), axis=2).astype(jnp.bfloat16)
    expert_grad = jnp.einsum(
        "esf,edf->esd", d_gate, gate_weight, preferred_element_type=jnp.float32
    ) + jnp.einsum("esf,edf->esd", d_up, up_weight, preferred_element_type=jnp.float32)
    expert_grad = expert_grad.astype(jnp.bfloat16)
    back_grad, back_score = (
        lax.all_to_all(
            expert_grad.reshape(local_count, groups, capacity * feature_cols),
            "expert",
            split_axis=1,
            concat_axis=1,
            tiled=True,
        ),
        lax.all_to_all(
            score_rows.reshape(local_count, groups, capacity),
            "expert",
            split_axis=1,
            concat_axis=1,
            tiled=True,
        ),
    )
    returned_rows = back_grad.reshape(column_total, feature_cols)
    returned_scores = back_score.reshape(column_total).astype(jnp.float32)
    kept_value = kept_mask.astype(jnp.float32)
    probs_rows = jnp.repeat(router_probs, route_width, axis=0)
    onehot_float = onehot.astype(jnp.float32)
    gate_value = jnp.sum(onehot_float * probs_rows, axis=1)
    route_weight = (gate_value * kept_value).reshape(token_rows, route_width)
    combine_weight = jnp.sum(jnp.where(column_match, route_weight[:, :, None], 0.0), axis=1)
    routed_part = jnp.dot(
        combine_weight,
        returned_rows.astype(jnp.float32),
        precision=lax.Precision.HIGHEST,
        preferred_element_type=jnp.float32,
    )
    safe_column = jnp.maximum(column_id, 0)
    route_score = returned_scores[safe_column] * kept_value
    prob_grad = jnp.sum(
        (onehot_float * route_score[:, None]).reshape(token_rows, route_width, expert_total), axis=1
    )
    gate_total = jnp.sum((gate_value * route_score).reshape(token_rows, route_width), axis=1)
    logit_grad = (router_probs * (prob_grad - gate_total[:, None])).astype(jnp.bfloat16)
    router_part = jnp.einsum(
        "te,de->td", logit_grad, router_weight, preferred_element_type=jnp.float32
    )
    return (shared_part + routed_part + router_part).astype(jnp.bfloat16)


F32, BF16 = jnp.float32, jnp.bfloat16
LAST = (((1,), (1,)), ((), ()))
FIRST = (((0,), (0,)), ((), ()))
VMEM_BYTES = 48 * 1024 * 1024
TOP_ROWS = 64


def call(kernel, **settings):
    return pl.pallas_call(
        kernel,
        compiler_params=pltpu.CompilerParams(vmem_limit_bytes=VMEM_BYTES),
        cost_estimate=pl.CostEstimate(flops=1000, bytes_accessed=1000, transcendentals=0),
        **settings,
    )


def whole(shape):
    return pl.BlockSpec(shape, lambda *_: (0,) * len(shape))


def payload_kernel(capacity, ids_ref, probs_ref, grad_ref, out_ref):
    rows, expert_total = probs_ref.shape
    cols = grad_ref.shape[1]
    experts = lax.broadcasted_iota(jnp.int32, (rows, expert_total), 1)
    ids = ids_ref[...]
    member = jnp.zeros((rows, expert_total), F32)
    for k in range(ids.shape[1]):
        member = member + jnp.where(ids[:, k : k + 1] == experts, 1.0, 0.0)
    member = member.astype(BF16)
    row_at = lax.broadcasted_iota(jnp.int32, (rows, rows), 0)
    col_at = lax.broadcasted_iota(jnp.int32, (rows, rows), 1)
    lower = jnp.where(row_at < col_at, 1.0, 0.0).astype(BF16)
    same = jnp.where(row_at == col_at, 1.0, 0.0).astype(BF16)
    probs = probs_ref[...]
    high = probs.astype(BF16)
    low = (probs - high.astype(F32)).astype(BF16)

    def turned(a, by):
        return lax.dot_general(a, by, FIRST, preferred_element_type=F32)

    before = turned(member, lower)
    slot = jnp.where((turned(member, same) > 0.5) & (before < capacity), before, -1.0)
    parts = [slot, turned(high, same), turned(low, same)]
    pieces = [a[8 * i : 8 * i + 8] for a in parts for i in range(expert_total // 8)]
    pieces.append(jnp.zeros((8, cols - len(pieces) * rows), F32))
    out_ref[0:rows, :] = grad_ref[...]
    out_ref[rows : rows + 8, :] = jnp.concatenate(pieces, axis=1).astype(BF16)


def hidden_kernel(halves, tiles, capacity, info_ref, *refs):
    block_refs = refs[: len(halves)]
    weight_ref, other_ref, mine_ref, meta_ref, placed_ref = refs[len(halves) :]
    step, part = pl.program_id(0), pl.program_id(1)
    core, tile, row = info_ref[0], info_ref[1], info_ref[2]
    blocks, at = [], 0
    while at < len(halves):
        if halves[at]:
            blocks.append((block_refs[at], block_refs[at + 1]))
            at += 2
        else:
            blocks.append((block_refs[at],))
            at += 1
    rows = 128

    def meta_of(block):
        last = block[-1]
        return last[last.shape[0] - 8 :, :].astype(F32)

    def pick(meta, kind, which):
        value = meta[:, kind * tiles * rows : (kind * tiles + 1) * rows]
        for i in range(1, tiles):
            at_lane = (kind * tiles + i) * rows
            value = jnp.where(tile == i, meta[:, at_lane : at_lane + rows], value)
        line = lax.broadcasted_iota(jnp.int32, (8, rows), 0)
        return jnp.sum(jnp.where(line == which, value, 0.0), axis=0, keepdims=True)

    @pl.when(part == 0)
    def _():
        expert = jnp.where(step == 0, 1 - core, core)
        for b, block in enumerate(blocks):
            slot = pick(meta_of(block), 0, row + expert)
            slot_at = lax.broadcasted_iota(jnp.int32, (capacity, rows), 0).astype(F32)
            match = jnp.where(slot_at == slot, 1.0, 0.0).astype(BF16)
            if len(block) == 1:
                data = block[0][0:rows, :]
            else:
                data = jnp.concatenate([block[0][...], block[1][0 : rows - TOP_ROWS, :]], axis=0)
            placed = jnp.dot(match, data, preferred_element_type=F32)
            placed_ref[b * capacity : (b + 1) * capacity, :] = placed.astype(BF16)

    @pl.when((part == 0) & (step == 0))
    def _():
        for b, block in enumerate(blocks):
            meta = meta_of(block)
            lines = [pick(meta, 0, row), pick(meta, 0, row + 1)]
            lines += [pick(meta, 1, row) + pick(meta, 2, row)]
            lines += [pick(meta, 1, row + 1) + pick(meta, 2, row + 1)]
            lines += [jnp.zeros((4, rows), F32)]
            meta_ref[8 * b : 8 * b + 8, :] = jnp.concatenate(lines, axis=0)

    value = lax.dot_general(placed_ref[...], weight_ref[0], LAST, preferred_element_type=F32)
    value = value.astype(BF16)
    width = value.shape[1]
    lanes = pl.ds(pl.multiple_of(part * width, width), width)

    @pl.when(step == 0)
    def _():
        other_ref[:, lanes] = value

    @pl.when(step == 1)
    def _():
        mine_ref[:, lanes] = value


def hidden_part(info, blocks, down_weight, tiles, capacity):
    local_count, hidden_units, cols = down_weight.shape
    flat, halves = [], []
    for block in blocks:
        pair = isinstance(block, tuple)
        flat += list(block) if pair else [block]
        halves += [pair, pair] if pair else [False]
    count = len(blocks)
    width = hidden_units // 2
    shape = (count * capacity, hidden_units)
    spec = pltpu.PrefetchScalarGridSpec(
        num_scalar_prefetch=1,
        grid=(2, 2),
        in_specs=[whole(a.shape) for a in flat]
        + [
            pl.BlockSpec(
                (1, width, cols),
                lambda s, p, info: (jnp.where(s == 0, 1 - info[0], info[0]), p, 0),
            )
        ],
        out_specs=[whole(shape), whole(shape), whole((8 * count, 128))],
        scratch_shapes=[pltpu.VMEM((count * capacity, cols), BF16)],
    )
    return call(
        functools.partial(hidden_kernel, halves, tiles, capacity),
        grid_spec=spec,
        out_shape=[
            jax.ShapeDtypeStruct(shape, BF16),
            jax.ShapeDtypeStruct(shape, BF16),
            jax.ShapeDtypeStruct((8 * count, 128), F32),
        ],
    )(info, *flat, down_weight)


def grad_kernel(count, split, tiles, capacity, info_ref, *refs):
    gate_refs, up_refs = refs[:count], refs[count : 2 * count]
    full_ref, pair_ref, meta_ref, gate_w_ref, up_w_ref = refs[2 * count : 2 * count + 5]
    out_refs = refs[2 * count + 5 : -4]
    dgate_ref, dup_ref, combine_ref, score_ref = refs[-4:]
    step = pl.program_id(0)
    core, tile, row = info_ref[0], info_ref[1], info_ref[2]
    rows = 128

    @pl.when(step == 0)
    def _():
        line = lax.broadcasted_iota(jnp.int32, (8, rows), 0)
        slot_at = lax.broadcasted_iota(jnp.int32, (capacity, rows), 0).astype(F32)
        for b in range(count):
            span = slice(b * capacity, (b + 1) * capacity)
            lines = meta_ref[8 * b : 8 * b + 8, :]
            score_rows = jnp.zeros((8, rows), F32)
            stacked = []
            for e in range(2):
                hidden = jnp.where(core == e, full_ref[span, :], pair_ref[span, :]).astype(F32)
                gate = gate_refs[b][e].astype(F32)
                up = up_refs[b][e].astype(F32)
                active, slope_term = silu_parts(gate)
                dup = (hidden * active).astype(BF16)
                dgate_ref[e, span, :] = (hidden * up * slope_term).astype(BF16)
                dup_ref[e, span, :] = dup
                score = jnp.sum(up * dup.astype(F32), axis=1, keepdims=True)
                score = score.astype(BF16).astype(F32)
                match = slot_at == lines[e : e + 1, :]
                token_score = jnp.sum(jnp.where(match, score, 0.0), axis=0, keepdims=True)
                score_rows = score_rows + jnp.where(line == row + e, token_score, 0.0)
                weight = jnp.where(match, lines[2 + e : 3 + e, :], 0.0)
                high = weight.astype(BF16)
                stacked += [high, (weight - high.astype(F32)).astype(BF16)]
            combine_ref[b] = jnp.concatenate(stacked, axis=0)
            score_ref[b] = score_rows

    grads = []
    for e in range(2):
        value = lax.dot_general(dgate_ref[e], gate_w_ref[e], LAST, preferred_element_type=F32)
        value = value + lax.dot_general(dup_ref[e], up_w_ref[e], LAST, preferred_element_type=F32)
        grads.append(value.astype(BF16))
    width = grads[0].shape[1]
    for b in range(count):
        span = slice(b * capacity, (b + 1) * capacity)
        pile = jnp.concatenate([g[span] for g in grads for _ in range(2)], axis=0)
        value = lax.dot_general(combine_ref[b], pile, FIRST, preferred_element_type=F32)
        lanes = [jnp.where((step == 0) & (tile == i), score_ref[b], 0.0) for i in range(tiles)]
        if tiles * rows < width:
            lanes.append(jnp.zeros((8, width - tiles * rows), F32))
        lanes = jnp.concatenate(lanes, axis=1)
        if split:
            out_refs[2 * b][...] = value[:TOP_ROWS].astype(BF16)
            out_refs[2 * b + 1][...] = jnp.concatenate([value[TOP_ROWS:], lanes], 0).astype(BF16)
        else:
            out_refs[b][...] = jnp.concatenate([value, lanes], axis=0).astype(BF16)


def grad_part(info, full, pair, meta, saved, weights, count, split, tiles, capacity):
    gate_saved, up_saved = saved
    gate_weight, up_weight = weights
    local_count, cols, hidden_units = gate_weight.shape
    width = 256
    heights = [TOP_ROWS, 136 - TOP_ROWS] * count if split else [136] * count

    def saved_spec(b):
        return pl.BlockSpec((2, capacity, hidden_units), lambda n, info: (0, info[3 + b], 0))

    weight_spec = pl.BlockSpec((2, width, hidden_units), lambda n, info: (0, n, 0))
    spec = pltpu.PrefetchScalarGridSpec(
        num_scalar_prefetch=1,
        grid=(cols // width,),
        in_specs=[saved_spec(b) for b in range(count)] * 2
        + [whole(full.shape), whole(pair.shape), whole(meta.shape)]
        + [weight_spec, weight_spec],
        out_specs=[pl.BlockSpec((h, width), lambda n, info: (0, n)) for h in heights],
        scratch_shapes=[
            pltpu.VMEM((2, count * capacity, hidden_units), BF16),
            pltpu.VMEM((2, count * capacity, hidden_units), BF16),
            pltpu.VMEM((count, 4 * capacity, 128), BF16),
            pltpu.VMEM((count, 8, 128), F32),
        ],
    )
    return call(
        functools.partial(grad_kernel, count, split, tiles, capacity),
        grid_spec=spec,
        out_shape=[jax.ShapeDtypeStruct((h, cols), BF16) for h in heights],
    )(
        info,
        *([gate_saved] * count),
        *([up_saved] * count),
        full,
        pair,
        meta,
        gate_weight,
        up_weight,
    )


def shared_kernel(info_ref, *refs):
    token_refs, grad_refs = refs[0:4], refs[4:8]
    gate_hbm, up_hbm, down_hbm = refs[8:11]
    out_refs = refs[11:15]
    gate_ref, up_ref, down_ref, sems = refs[15:]
    here = info_ref[0]
    rows, cols = token_refs[0].shape
    units = gate_ref.shape[2]

    def copies(q):
        at = pl.multiple_of(jnp.bitwise_xor(here, q) * cols, cols)
        return (
            pltpu.make_async_copy(gate_hbm.at[pl.ds(at, cols), :], gate_ref.at[q], sems.at[q, 0]),
            pltpu.make_async_copy(up_hbm.at[pl.ds(at, cols), :], up_ref.at[q], sems.at[q, 1]),
            pltpu.make_async_copy(down_hbm.at[:, pl.ds(at, cols)], down_ref.at[q], sems.at[q, 2]),
        )

    for q in range(4):
        for copy in copies(q):
            copy.start()
    gate_pre = jnp.zeros((rows, units), F32)
    up_pre = jnp.zeros((rows, units), F32)
    hidden_pre = jnp.zeros((rows, units), F32)
    for q in range(4):
        for copy in copies(q):
            copy.wait()
        token, grad = token_refs[q][...], grad_refs[q][...]
        gate_pre = gate_pre + jnp.dot(token, gate_ref[q], preferred_element_type=F32)
        up_pre = up_pre + jnp.dot(token, up_ref[q], preferred_element_type=F32)
        hidden_pre = hidden_pre + lax.dot_general(
            grad, down_ref[q], LAST, preferred_element_type=F32
        )
    active, slope_term = silu_parts(gate_pre)
    dgate = (hidden_pre * up_pre * slope_term).astype(BF16)
    dup = (hidden_pre * active).astype(BF16)
    for q in range(4):
        term = lax.dot_general(dgate, gate_ref[q], LAST, preferred_element_type=F32)
        term = term + lax.dot_general(dup, up_ref[q], LAST, preferred_element_type=F32)
        out_refs[q][...] = term.astype(BF16)


def shared_part_terms(here, token_blocks, grad_blocks, shared_gate, shared_up, shared_down):
    rows, cols = token_blocks[0].shape
    units = shared_gate.shape[1]
    spec = pltpu.PrefetchScalarGridSpec(
        num_scalar_prefetch=1,
        grid=(1,),
        in_specs=[whole((rows, cols))] * 8 + [pl.BlockSpec(memory_space=pl.ANY)] * 3,
        out_specs=[whole((rows, cols))] * 4,
        scratch_shapes=[
            pltpu.VMEM((4, cols, units), BF16),
            pltpu.VMEM((4, cols, units), BF16),
            pltpu.VMEM((4, units, cols), BF16),
            pltpu.SemaphoreType.DMA((4, 3)),
        ],
    )
    return call(
        shared_kernel,
        grid_spec=spec,
        out_shape=[jax.ShapeDtypeStruct((rows, cols), BF16)] * 4,
    )(here, *token_blocks, *grad_blocks, shared_gate, shared_up, shared_down)


def ring_place(position):
    position = position % 8
    return jnp.where(position < 4, 2 * position, 15 - 2 * position)


def per_device_ring(
    tokens,
    out_grad,
    expert_ids,
    router_probs,
    router_weight,
    gate_weight,
    up_weight,
    down_weight,
    gate_saved,
    up_saved,
    shared_gate,
    shared_up,
    shared_down,
):
    slot_count = gate_saved.shape[1]
    capacity = slot_count // 8
    rows, cols = tokens.shape
    expert_total = router_probs.shape[1]
    tiles = expert_total // 8
    order = [0, 2, 4, 6, 7, 5, 3, 1]
    ahead = [(order[i], order[(i + 1) % 8]) for i in range(8)]
    behind = [(order[i], order[(i - 1) % 8]) for i in range(8)]
    x_pairs = [(i, i ^ 2) for i in range(4)]
    core_pairs = [(i, i ^ 1) for i in range(4)]
    me = lax.axis_index("expert")
    place = jnp.where(me % 2 == 0, me // 2, 7 - me // 2)
    here = lax.axis_index("tensor")
    first = me * 2
    base = [here % 2, first // 8, first % 8]
    tie = lax.optimization_barrier

    def swap_x(a):
        return lax.ppermute(a, "tensor", x_pairs)

    def swap_core(a):
        return lax.ppermute(a, "tensor", core_pairs)

    def ring(fore, back):
        return lax.ppermute(fore, "expert", ahead), lax.ppermute(back, "expert", behind)

    def info(chunk):
        numbers = base + [ring_place(place + d) for d in chunk]
        return jnp.stack([jnp.asarray(n, jnp.int32) for n in numbers])

    def hidden(blocks):
        return hidden_part(info(()), blocks, down_weight, tiles, capacity)

    def grads(chunk, full, pair, meta):
        split = chunk == (4,)
        return grad_part(
            info(chunk),
            full,
            pair,
            meta,
            (gate_saved, up_saved),
            (gate_weight, up_weight),
            len(chunk),
            split,
            tiles,
            capacity,
        )

    def add(a, *others):
        total = a.astype(F32)
        for other in others:
            total = total + other.astype(F32)
        return total.astype(BF16)

    tok_core, grad_core = swap_core(tokens), swap_core(out_grad)
    tok_x, grad_x = swap_x(tokens), swap_x(out_grad)
    payload = call(
        functools.partial(payload_kernel, capacity),
        out_shape=jax.ShapeDtypeStruct((rows + 8, cols), BF16),
    )(expert_ids, router_probs, out_grad)

    fore1, back1 = ring(payload, payload)
    fore2, back2 = ring(fore1, back1)
    other1, mine1, meta1 = hidden([payload, fore1, back1])
    fore2, back2, other1, mine1 = tie((fore2, back2, other1, mine1))

    fore3, back3 = ring(fore2, back2)
    chip1 = add(mine1, swap_core(other1))
    far1 = swap_x(chip1)
    other2, mine2, meta2 = hidden([fore2, back2])
    fore3, back3, chip1, other2, mine2 = tie((fore3, back3, chip1, other2, mine2))

    top, bottom = ring(fore3[:TOP_ROWS], back3[TOP_ROWS:])
    chip2 = add(mine2, swap_core(other2))
    far2 = swap_x(chip2)
    other3, mine3, meta3 = hidden([fore3, back3])
    top, bottom, chip2, other3, mine3 = tie((top, bottom, chip2, other3, mine3))

    other4, mine4, meta4 = hidden([(top, bottom)])
    chip3 = add(mine3, swap_core(other3))
    chip4 = add(mine4, swap_core(other4))
    far4 = swap_x(chip4)
    full1 = add(chip1, far1)
    pair1 = swap_core(full1)
    full2 = add(chip2, far2)
    pair2 = swap_core(full2)
    near0, near_b1, near_f1 = grads((0, -1, 1), full1, pair1, meta1)
    far4, near0 = tie((far4, near0))
    full4 = add(chip4, far4)
    pair4 = swap_core(full4)
    far3 = swap_x(chip3)
    top, bottom = grads((4,), full4, pair4, meta4)

    top, bottom, full2, pair2 = tie((top, bottom, full2, pair2))
    fore, back = ring(top, bottom)
    full3 = add(chip3, far3)
    pair3 = swap_core(full3)
    near_b3, near_f3 = grads((-3, 3), full3, pair3, meta3)
    near_b2, near_f2 = grads((-2, 2), full2, pair2, meta2)
    fore, back, near_f3, near_b3, near_f2, near_b2 = tie(
        (fore, back, near_f3, near_b3, near_f2, near_b2)
    )

    fore = jnp.concatenate([add(near_f3[:TOP_ROWS], fore), near_f3[TOP_ROWS:]], axis=0)
    back = jnp.concatenate([near_b3[:TOP_ROWS], add(near_b3[TOP_ROWS:], back)], axis=0)
    tok_both, grad_both = swap_core(tok_x), swap_core(grad_x)
    fore, back, tok_both, grad_both = tie((fore, back, tok_both, grad_both))
    fore, back = ring(fore, back)
    terms = shared_part_terms(
        here.reshape(1).astype(jnp.int32),
        [tokens, tok_core, tok_x, tok_both],
        [out_grad, grad_core, grad_x, grad_both],
        shared_gate,
        shared_up,
        shared_down,
    )
    fore, back, *terms = tie((fore, back, *terms))

    fore, back = add(near_f2, fore), add(near_b2, back)
    fore, back = ring(fore, back)
    far = add(terms[2], swap_core(terms[3]))
    near = swap_core(terms[1])
    shared_far = swap_x(far)
    fore, back, near = tie((fore, back, near))

    fore, back = add(near_f1, fore), add(near_b1, back)
    fore, back = ring(fore, back)
    total = near0.astype(F32) + fore.astype(F32) + back.astype(F32)
    shared_part = terms[0].astype(F32) + near.astype(F32) + shared_far.astype(F32)
    prob_grad = jnp.concatenate(
        [total[rows:, i * rows : (i + 1) * rows] for i in range(tiles)], axis=0
    ).T
    gate_total = jnp.sum(router_probs * prob_grad, axis=1, keepdims=True)
    logit_grad = (router_probs * (prob_grad - gate_total)).astype(BF16)
    router_part = jnp.einsum("te,de->td", logit_grad, router_weight, preferred_element_type=F32)
    return (shared_part + total[:rows] + router_part).astype(BF16)


def per_device(*args):
    tokens, router_probs, gate_weight, gate_saved = args[0], args[3], args[5], args[8]
    rows, cols = tokens.shape
    expert_total = router_probs.shape[1]
    ring = (
        lax.axis_size("expert") == 8
        and lax.axis_size("tensor") == 4
        and gate_weight.shape[0] == 2
        and gate_saved.shape[1] == 8 * 64
        and gate_saved.shape[2] % 256 == 0
        and rows == 128
        and expert_total == 16
        and cols % 256 == 0
        and cols >= 6 * rows
    )
    return (per_device_ring if ring else per_device_wide)(*args)


def solution(mesh):

    return jax.shard_map(
        per_device,
        mesh=mesh,
        in_specs=(
            P("expert", "tensor"),
            P("expert", "tensor"),
            P("expert", None),
            P("expert", None),
            P("tensor", None),
            P("expert", "tensor", None),
            P("expert", "tensor", None),
            P("expert", None, "tensor"),
            P("expert", None, None),
            P("expert", None, None),
            P(None, "tensor"),
            P(None, "tensor"),
            P("tensor", None),
        ),
        out_specs=P("expert", "tensor"),
        check_vma=False,
    )
```

```python
import functools

import jax
import jax.numpy as jnp
from jax import lax
from jax.experimental import pallas as pl
from jax.experimental.pallas import tpu as pltpu
from jax.sharding import PartitionSpec as P


def silu_parts(preact):
    sigmoid_value = jax.nn.sigmoid(preact)
    return (preact * sigmoid_value, sigmoid_value * (1.0 + preact * (1.0 - sigmoid_value)))


def per_device_wide(
    tokens,
    out_grad,
    expert_ids,
    router_probs,
    router_weight,
    gate_weight,
    up_weight,
    down_weight,
    gate_saved,
    up_saved,
    shared_gate,
    shared_up,
    shared_down,
):
    groups = lax.axis_size("expert")
    local_count, slot_count, hidden_units = gate_saved.shape
    capacity = slot_count // groups
    token_rows, route_width = expert_ids.shape
    expert_total = router_probs.shape[1]
    feature_cols = tokens.shape[1]
    column_total = local_count * groups * capacity
    flat_ids = expert_ids.reshape(-1)
    onehot = (flat_ids[:, None] == jnp.arange(expert_total, dtype=jnp.int32)[None, :]).astype(
        jnp.int32
    )
    slot_index = jnp.sum((jnp.cumsum(onehot, axis=0) - onehot) * onehot, axis=1)
    kept_mask = slot_index < capacity
    owner_group = flat_ids // local_count
    local_expert = flat_ids % local_count
    column_id = jnp.where(
        kept_mask, local_expert * (groups * capacity) + owner_group * capacity + slot_index, -1
    )
    column_grid = column_id.reshape(token_rows, route_width)
    column_match = (
        column_grid[:, :, None] == jnp.arange(column_total, dtype=jnp.int32)[None, None, :]
    )
    placement = jnp.sum(column_match.astype(jnp.float32), axis=1).astype(jnp.bfloat16)
    sectioning = jnp.einsum(
        "tc,td->cd", placement, out_grad, preferred_element_type=jnp.float32
    ).astype(jnp.bfloat16)
    outgoing = sectioning.reshape(local_count, groups, capacity * feature_cols)
    token_piece = lax.all_gather(tokens, "tensor", axis=1, tiled=True)
    grad_piece = lax.all_gather(out_grad, "tensor", axis=1, tiled=True)
    gate_pre = jnp.dot(token_piece, shared_gate, preferred_element_type=jnp.float32)
    up_pre = jnp.dot(token_piece, shared_up, preferred_element_type=jnp.float32)
    hidden_pre = jnp.einsum(
        "tc,fc->tf", grad_piece, shared_down, preferred_element_type=jnp.float32
    )
    active, slope_term = silu_parts(gate_pre)
    shared_dgate = (hidden_pre * up_pre * slope_term).astype(jnp.bfloat16)
    shared_dup = (hidden_pre * active).astype(jnp.bfloat16)
    shared_term = jnp.einsum(
        "tf,df->td", shared_dgate, shared_gate, preferred_element_type=jnp.float32
    ) + jnp.einsum("tf,df->td", shared_dup, shared_up, preferred_element_type=jnp.float32)
    shared_part = lax.psum_scatter(
        shared_term.astype(jnp.bfloat16), "tensor", scatter_dimension=1, tiled=True
    ).astype(jnp.float32)
    arrived = lax.all_to_all(outgoing, "expert", split_axis=1, concat_axis=1, tiled=True)
    arrived = arrived.reshape(local_count, slot_count, feature_cols)
    partial_hidden = jnp.einsum(
        "esd,efd->esf", arrived, down_weight, preferred_element_type=jnp.float32
    )
    up_full = up_saved.astype(jnp.float32)
    hidden_grad = lax.psum(partial_hidden.astype(jnp.bfloat16), "tensor").astype(jnp.float32)
    active, slope_term = silu_parts(gate_saved.astype(jnp.float32))
    d_gate = (hidden_grad * up_full * slope_term).astype(jnp.bfloat16)
    d_up = (hidden_grad * active).astype(jnp.bfloat16)
    score_rows = jnp.sum(up_full * d_up.astype(jnp.float32), axis=2).astype(jnp.bfloat16)
    expert_grad = jnp.einsum(
        "esf,edf->esd", d_gate, gate_weight, preferred_element_type=jnp.float32
    ) + jnp.einsum("esf,edf->esd", d_up, up_weight, preferred_element_type=jnp.float32)
    expert_grad = expert_grad.astype(jnp.bfloat16)
    back_grad, back_score = (
        lax.all_to_all(
            expert_grad.reshape(local_count, groups, capacity * feature_cols),
            "expert",
            split_axis=1,
            concat_axis=1,
            tiled=True,
        ),
        lax.all_to_all(
            score_rows.reshape(local_count, groups, capacity),
            "expert",
            split_axis=1,
            concat_axis=1,
            tiled=True,
        ),
    )
    returned_rows = back_grad.reshape(column_total, feature_cols)
    returned_scores = back_score.reshape(column_total).astype(jnp.float32)
    kept_value = kept_mask.astype(jnp.float32)
    probs_rows = jnp.repeat(router_probs, route_width, axis=0)
    onehot_float = onehot.astype(jnp.float32)
    gate_value = jnp.sum(onehot_float * probs_rows, axis=1)
    route_weight = (gate_value * kept_value).reshape(token_rows, route_width)
    combine_weight = jnp.sum(jnp.where(column_match, route_weight[:, :, None], 0.0), axis=1)
    routed_part = jnp.dot(
        combine_weight,
        returned_rows.astype(jnp.float32),
        precision=lax.Precision.HIGHEST,
        preferred_element_type=jnp.float32,
    )
    safe_column = jnp.maximum(column_id, 0)
    route_score = returned_scores[safe_column] * kept_value
    prob_grad = jnp.sum(
        (onehot_float * route_score[:, None]).reshape(token_rows, route_width, expert_total), axis=1
    )
    gate_total = jnp.sum((gate_value * route_score).reshape(token_rows, route_width), axis=1)
    logit_grad = (router_probs * (prob_grad - gate_total[:, None])).astype(jnp.bfloat16)
    router_part = jnp.einsum(
        "te,de->td", logit_grad, router_weight, preferred_element_type=jnp.float32
    )
    return (shared_part + routed_part + router_part).astype(jnp.bfloat16)


F32, BF16 = jnp.float32, jnp.bfloat16
LAST = (((1,), (1,)), ((), ()))
FIRST = (((0,), (0,)), ((), ()))
TOP_ROWS = 64
INFO_BLOCKS = 7


def call(kernel, megabytes, out_shape, scratch_shapes=(), scalars=0, far=0):
    def run(*operands):
        near = len(operands) - scalars - far
        memory = [pltpu.SMEM] * scalars + [pltpu.VMEM] * near + [pl.ANY] * far
        return pl.pallas_call(
            kernel,
            in_specs=[pl.BlockSpec(memory_space=m) for m in memory],
            out_specs=jax.tree.map(lambda _: pl.BlockSpec(memory_space=pltpu.VMEM), out_shape),
            out_shape=out_shape,
            scratch_shapes=scratch_shapes,
            compiler_params=pltpu.CompilerParams(vmem_limit_bytes=megabytes * 1024 * 1024),
            cost_estimate=pl.CostEstimate(flops=1000, bytes_accessed=1000, transcendentals=0),
        )(*operands)

    return run


def sum_kernel(groups, *refs):
    count = sum(groups)
    at = 0
    for out_ref, size in zip(refs[count:], groups):
        total = refs[at][...].astype(F32)
        for ref in refs[at + 1 : at + size]:
            total = total + ref[...].astype(F32)
        out_ref[...] = total.astype(BF16)
        at += size


def sums(*groups):
    return call(
        functools.partial(sum_kernel, [len(g) for g in groups]),
        2,
        [jax.ShapeDtypeStruct(g[0].shape, BF16) for g in groups],
    )(*[a for g in groups for a in g])


def halves_kernel(fore_ref, back_ref, top_ref, bottom_ref):
    top_ref[...] = fore_ref[0:TOP_ROWS, :]
    bottom_ref[...] = back_ref[TOP_ROWS:, :]


def halves_of(fore, back):
    rows, cols = fore.shape
    return call(
        halves_kernel,
        2,
        [
            jax.ShapeDtypeStruct((TOP_ROWS, cols), BF16),
            jax.ShapeDtypeStruct((rows - TOP_ROWS, cols), BF16),
        ],
    )(fore, back)


def join_kernel(near_f_ref, top_ref, near_b_ref, bottom_ref, fore_ref, back_ref):
    top = near_f_ref[0:TOP_ROWS, :].astype(F32) + top_ref[...].astype(F32)
    fore_ref[0:TOP_ROWS, :] = top.astype(BF16)
    fore_ref[TOP_ROWS:, :] = near_f_ref[TOP_ROWS:, :]
    back_ref[0:TOP_ROWS, :] = near_b_ref[0:TOP_ROWS, :]
    bottom = near_b_ref[TOP_ROWS:, :].astype(F32) + bottom_ref[...].astype(F32)
    back_ref[TOP_ROWS:, :] = bottom.astype(BF16)


def join(near_f, top, near_b, bottom):
    shape = jax.ShapeDtypeStruct(near_f.shape, BF16)
    return call(join_kernel, 2, [shape, shape])(near_f, top, near_b, bottom)


def payload_kernel(capacity, ids_hbm, probs_hbm, grad_hbm, out_ref, ids_ref, probs_ref, sems):
    expert_total, rows = probs_ref.shape
    cols = grad_hbm.shape[1]
    copies = [
        pltpu.make_async_copy(ids_hbm, ids_ref, sems.at[0]),
        pltpu.make_async_copy(probs_hbm, probs_ref, sems.at[1]),
        pltpu.make_async_copy(grad_hbm, out_ref.at[0:rows, :], sems.at[2]),
    ]
    for copy in copies:
        copy.start()
    experts = lax.broadcasted_iota(jnp.int32, (expert_total, rows), 0)
    row_at = lax.broadcasted_iota(jnp.int32, (rows, rows), 0)
    col_at = lax.broadcasted_iota(jnp.int32, (rows, rows), 1)
    lower = jnp.where(row_at < col_at, 1.0, 0.0).astype(BF16)
    copies[0].wait()
    ids = ids_ref[...]
    member = jnp.zeros((expert_total, rows), F32)
    for k in range(ids.shape[0]):
        member = member + jnp.where(ids[k : k + 1, :] == experts, 1.0, 0.0)
    before = jnp.dot(member.astype(BF16), lower, preferred_element_type=F32)
    slot = jnp.where((member > 0.5) & (before < capacity), before, -1.0)
    copies[1].wait()
    probs = probs_ref[...]
    high = probs.astype(BF16).astype(F32)
    parts = [slot, high, probs - high]
    pieces = [a[8 * i : 8 * i + 8] for a in parts for i in range(expert_total // 8)]
    pieces.append(jnp.zeros((8, cols - len(pieces) * rows), F32))
    out_ref[rows : rows + 8, :] = jnp.concatenate(pieces, axis=1).astype(BF16)
    copies[2].wait()


def payload_of(ids_t, probs_t, grad, capacity):
    rows, cols = grad.shape
    return call(
        functools.partial(payload_kernel, capacity),
        60,
        jax.ShapeDtypeStruct((rows + 8, cols), BF16),
        [
            pltpu.VMEM(ids_t.shape, jnp.int32),
            pltpu.VMEM(probs_t.shape, F32),
            pltpu.SemaphoreType.DMA((3,)),
        ],
        0,
        3,
    )(ids_t, probs_t, grad)


def hidden_kernel(halves, tiles, capacity, info_ref, *refs):
    block_refs = refs[: len(halves)]
    weight_ref, other_ref, mine_ref, meta_ref, placed_ref = refs[len(halves) :]
    core, tile, row = info_ref[0], info_ref[1], info_ref[2]
    blocks, at = [], 0
    while at < len(halves):
        size = 2 if halves[at] else 1
        blocks.append(block_refs[at : at + size])
        at += size
    rows = 128
    units = weight_ref.shape[1]

    def pick(meta, kind, which):
        value = meta[:, kind * tiles * rows : (kind * tiles + 1) * rows]
        for i in range(1, tiles):
            at_lane = (kind * tiles + i) * rows
            value = jnp.where(tile == i, meta[:, at_lane : at_lane + rows], value)
        line = lax.broadcasted_iota(jnp.int32, (8, rows), 0)
        return jnp.sum(jnp.where(line == which, value, 0.0), axis=0, keepdims=True)

    slot_at = lax.broadcasted_iota(jnp.int32, (capacity, rows), 0).astype(F32)
    for step in range(2):
        expert = 1 - core if step == 0 else core
        for b, block in enumerate(blocks):
            last = block[-1]
            meta = last[last.shape[0] - 8 :, :].astype(F32)
            match = jnp.where(slot_at == pick(meta, 0, row + expert), 1.0, 0.0).astype(BF16)
            if len(block) == 1:
                data = block[0][0:rows, :]
            else:
                data = jnp.concatenate([block[0][...], block[1][0 : rows - TOP_ROWS, :]], axis=0)
            placed = jnp.dot(match, data, preferred_element_type=F32)
            placed_ref[step, b * capacity : (b + 1) * capacity, :] = placed.astype(BF16)
            if step == 1:
                lines = [pick(meta, 0, row), pick(meta, 0, row + 1)]
                lines += [pick(meta, 1, row) + pick(meta, 2, row)]
                lines += [pick(meta, 1, row + 1) + pick(meta, 2, row + 1)]
                lines += [jnp.zeros((4, rows), F32)]
                meta_ref[8 * b : 8 * b + 8, :] = jnp.concatenate(lines, axis=0)
        out_ref = other_ref if step == 0 else mine_ref
        for n in range(0, units, 256):
            value = lax.dot_general(
                placed_ref[step],
                weight_ref[expert, n : n + 256, :],
                LAST,
                preferred_element_type=F32,
            )
            out_ref[:, n : n + 256] = value.astype(BF16)


def hidden_part(info, blocks, down_weight, tiles, capacity):
    local_count, hidden_units, cols = down_weight.shape
    flat, halves = [], []
    for block in blocks:
        pair = isinstance(block, tuple)
        flat += list(block) if pair else [block]
        halves += [pair, pair] if pair else [False]
    count = len(blocks)
    shape = (count * capacity, hidden_units)
    return call(
        functools.partial(hidden_kernel, halves, tiles, capacity),
        10,
        [
            jax.ShapeDtypeStruct(shape, BF16),
            jax.ShapeDtypeStruct(shape, BF16),
            jax.ShapeDtypeStruct((8 * count, 128), F32),
        ],
        [pltpu.VMEM((2, count * capacity, cols), BF16)],
        1,
    )(info, *flat, down_weight)


def grad_kernel(counts, chunk, split, tiles, capacity, info_ref, *refs):
    groups = len(counts)
    total = sum(counts)
    hidden_refs = refs[: 3 * groups]
    gate_ref, up_ref, gate_w_ref, up_w_ref = refs[3 * groups : 3 * groups + 4]
    out_refs = refs[3 * groups + 4 : -2]
    dgate_ref, dup_ref = refs[-2:]
    core, tile, row = info_ref[0], info_ref[1], info_ref[2]
    rows = 128
    cols = gate_w_ref.shape[1]
    line = lax.broadcasted_iota(jnp.int32, (8, rows), 0)
    slot_at = lax.broadcasted_iota(jnp.int32, (capacity, rows), 0).astype(F32)
    combine, scores = [], []
    b = 0
    for g in range(groups):
        full_ref, pair_ref, meta_ref = hidden_refs[3 * g : 3 * g + 3]
        for i in range(counts[g]):
            span = slice(i * capacity, (i + 1) * capacity)
            store = slice(b * capacity, (b + 1) * capacity)
            saved = pl.ds(pl.multiple_of(info_ref[INFO_BLOCKS + chunk[b]] * capacity, capacity), capacity)
            lines = meta_ref[8 * i : 8 * i + 8, :]
            score_rows = jnp.zeros((8, rows), F32)
            stacked = []
            for e in range(2):
                hidden = jnp.where(core == e, full_ref[span, :], pair_ref[span, :]).astype(F32)
                gate = gate_ref[e, saved, :].astype(F32)
                up = up_ref[e, saved, :].astype(F32)
                active, slope_term = silu_parts(gate)
                dup = hidden * active
                match = slot_at == lines[e : e + 1, :]
                weight = jnp.sum(
                    jnp.where(match, lines[2 + e : 3 + e, :], 0.0), axis=1, keepdims=True
                )
                dgate_ref[e, store, :] = (hidden * up * slope_term * weight).astype(BF16)
                dup_ref[e, store, :] = (dup * weight).astype(BF16)
                score = jnp.sum(up * dup.astype(BF16).astype(F32), axis=1, keepdims=True)
                score = score.astype(BF16).astype(F32)
                token_score = jnp.sum(jnp.where(match, score, 0.0), axis=0, keepdims=True)
                score_rows = score_rows + jnp.where(line == row + e, token_score, 0.0)
                stacked.append(jnp.where(match, 1.0, 0.0).astype(BF16))
            combine.append(jnp.concatenate(stacked, axis=0))
            scores.append(score_rows)
            b += 1
    for n in range(0, cols, 256):
        grads = []
        for e in range(2):
            value = lax.dot_general(
                dgate_ref[e], gate_w_ref[e, n : n + 256, :], LAST, preferred_element_type=F32
            )
            value = value + lax.dot_general(
                dup_ref[e], up_w_ref[e, n : n + 256, :], LAST, preferred_element_type=F32
            )
            grads.append(value.astype(BF16))
        for b in range(total):
            span = slice(b * capacity, (b + 1) * capacity)
            pile = jnp.concatenate([g[span] for g in grads], axis=0)
            value = lax.dot_general(combine[b], pile, FIRST, preferred_element_type=F32)
            if n == 0:
                lanes = [jnp.where(tile == i, scores[b], 0.0) for i in range(tiles)]
                lanes = jnp.concatenate(lanes, axis=1)
            else:
                lanes = jnp.zeros((8, 256), F32)
            if split:
                out_refs[2 * b][:, n : n + 256] = value[:TOP_ROWS].astype(BF16)
                low = jnp.concatenate([value[TOP_ROWS:], lanes], axis=0)
                out_refs[2 * b + 1][:, n : n + 256] = low.astype(BF16)
            else:
                out_refs[b][:, n : n + 256] = jnp.concatenate([value, lanes], axis=0).astype(BF16)


def grad_part(info, parts, saved, weights, counts, chunk, split, tiles, capacity):
    local_count, cols, hidden_units = weights[0].shape
    total = sum(counts)
    heights = [TOP_ROWS, 136 - TOP_ROWS] * total if split else [136] * total
    return call(
        functools.partial(grad_kernel, counts, chunk, split, tiles, capacity),
        14,
        [jax.ShapeDtypeStruct((h, cols), BF16) for h in heights],
        [
            pltpu.VMEM((2, total * capacity, hidden_units), BF16),
            pltpu.VMEM((2, total * capacity, hidden_units), BF16),
        ],
        1,
    )(info, *parts, *saved, *weights)


def shared_kernel(info_ref, *refs):
    token_refs, grad_refs = refs[0:4], refs[4:8]
    gate_ref, up_ref, down_ref = refs[8:11]
    out_refs = refs[11:15]
    here = info_ref[3]
    rows, cols = token_refs[0].shape
    units = gate_ref.shape[1]
    spans = []
    for q in range(4):
        at = pl.multiple_of(jnp.bitwise_xor(here, q) * cols, cols)
        spans.append(pl.ds(at, cols))
    gate_pre = jnp.zeros((rows, units), F32)
    up_pre = jnp.zeros((rows, units), F32)
    hidden_pre = jnp.zeros((rows, units), F32)
    for q in range(4):
        token, grad = token_refs[q][...], grad_refs[q][...]
        gate_pre = gate_pre + jnp.dot(token, gate_ref[spans[q], :], preferred_element_type=F32)
        up_pre = up_pre + jnp.dot(token, up_ref[spans[q], :], preferred_element_type=F32)
        hidden_pre = hidden_pre + lax.dot_general(
            grad, down_ref[:, spans[q]], LAST, preferred_element_type=F32
        )
    active, slope_term = silu_parts(gate_pre)
    dgate = (hidden_pre * up_pre * slope_term).astype(BF16)
    dup = (hidden_pre * active).astype(BF16)
    for q in range(4):
        term = lax.dot_general(dgate, gate_ref[spans[q], :], LAST, preferred_element_type=F32)
        term = term + lax.dot_general(dup, up_ref[spans[q], :], LAST, preferred_element_type=F32)
        out_refs[q][...] = term.astype(BF16)


def shared_part_terms(here, token_blocks, grad_blocks, shared_gate, shared_up, shared_down):
    rows, cols = token_blocks[0].shape
    return call(
        shared_kernel,
        10,
        [jax.ShapeDtypeStruct((rows, cols), BF16)] * 4,
        (),
        1,
    )(here, *token_blocks, *grad_blocks, shared_gate, shared_up, shared_down)


def ring_place(position):
    position = position % 8
    return jnp.where(position < 4, 2 * position, 15 - 2 * position)


def per_device_ring(
    tokens,
    out_grad,
    expert_ids,
    router_probs,
    router_weight,
    gate_weight,
    up_weight,
    down_weight,
    gate_saved,
    up_saved,
    shared_gate,
    shared_up,
    shared_down,
):
    slot_count = gate_saved.shape[1]
    capacity = slot_count // 8
    rows, cols = tokens.shape
    expert_total = router_probs.shape[1]
    tiles = expert_total // 8
    order = [0, 2, 4, 6, 7, 5, 3, 1]
    ahead = [(order[i], order[(i + 1) % 8]) for i in range(8)]
    behind = [(order[i], order[(i - 1) % 8]) for i in range(8)]
    x_pairs = [(i, i ^ 2) for i in range(4)]
    core_pairs = [(i, i ^ 1) for i in range(4)]
    me = lax.axis_index("expert")
    place = jnp.where(me % 2 == 0, me // 2, 7 - me // 2)
    here = lax.axis_index("tensor")
    first = me * 2
    base = [here % 2, first // 8, first % 8]
    tie = lax.optimization_barrier

    def swap_x(a):
        return lax.ppermute(a, "tensor", x_pairs)

    def swap_core(a):
        return lax.ppermute(a, "tensor", core_pairs)

    def ring(fore, back):
        return lax.ppermute(fore, "expert", ahead), lax.ppermute(back, "expert", behind)

    def hidden(blocks):
        return hidden_part(info, blocks, down_weight, tiles, capacity)

    def grads(saved, weights, *parts):
        chunk = sum((part[0] for part in parts), ())
        return grad_part(
            info,
            [a for part in parts for a in part[1:]],
            saved,
            weights,
            [len(part[0]) for part in parts],
            chunk,
            chunk == (4,),
            tiles,
            capacity,
        )

    numbers = base + [here] + [ring_place(place + d) for d in range(-3, 5)]
    info = jnp.stack([jnp.asarray(n, jnp.int32) for n in numbers])
    payload = payload_of(expert_ids.T, router_probs.T, out_grad, capacity)

    payload, tokens, out_grad, info = tie((payload, tokens, out_grad, info))
    fore, back = ring(payload, payload)
    fore1, back1 = tie((fore, back))

    fore, back = ring(fore1, back1)
    other1, mine1, meta1 = hidden([payload, fore1, back1])
    fore2, back2, other1, mine1 = tie((fore, back, other1, mine1))

    fore, back = ring(fore2, back2)
    (chip1,) = sums((mine1, swap_core(other1)))
    far1 = swap_x(chip1)
    other2, mine2, meta2 = hidden([fore2, back2])
    fore3, back3, chip1, other2, mine2 = tie((fore, back, chip1, other2, mine2))

    top, bottom = ring(*halves_of(fore3, back3))
    (chip2,) = sums((mine2, swap_core(other2)))
    far2 = swap_x(chip2)
    other3, mine3, meta3 = hidden([fore3, back3])
    top, bottom, chip2, other3, mine3, far1 = tie((top, bottom, chip2, other3, mine3, far1))

    other4, mine4, meta4 = hidden([(top, bottom)])
    swapped4, swapped3 = swap_core(other4), swap_core(other3)
    (full1,) = sums((chip1, far1))
    pair1 = swap_core(full1)
    (chip4,) = sums((mine4, swapped4))
    chip4, far2, swapped3, pair1 = tie((chip4, far2, swapped3, pair1))
    far4 = swap_x(chip4)
    chip3, full2 = sums((mine3, swapped3), (chip2, far2))
    pair2 = swap_core(full2)
    far4, chip3, full2, pair2 = tie((far4, chip3, full2, pair2))
    (full4,) = sums((chip4, far4))
    pair4 = swap_core(full4)
    far3 = swap_x(chip3)
    pair4, full4 = tie((pair4, full4))
    saved = (gate_saved, up_saved)
    weights = (gate_weight, up_weight)
    top, bottom = grads(saved, weights, ((4,), full4, pair4, meta4))

    top, bottom, far3, tokens, out_grad = tie((top, bottom, far3, tokens, out_grad))
    fore, back = ring(top, bottom)
    tok_x = swap_x(tokens)
    tok_core, grad_core = swap_core(tokens), swap_core(out_grad)
    (full3,) = sums((chip3, far3))
    pair3 = swap_core(full3)
    near_b3, near_f3, near_b2, near_f2 = grads(
        saved, weights, ((-3, 3), full3, pair3, meta3), ((-2, 2), full2, pair2, meta2)
    )
    fore, back, near_f3, near_b3, near_f2, near_b2, full1, pair1, out_grad = tie(
        (fore, back, near_f3, near_b3, near_f2, near_b2, full1, pair1, out_grad)
    )

    fore, back = join(near_f3, fore, near_b3, back)
    fore, back = ring(fore, back)
    grad_x = swap_x(out_grad)
    tok_both = swap_core(tok_x)
    near0, near_b1, near_f1 = grads(saved, weights, ((0, -1, 1), full1, pair1, meta1))
    fore, back, near0, near_b1, near_f1, tok_x, tok_both, grad_x = tie(
        (fore, back, near0, near_b1, near_f1, tok_x, tok_both, grad_x)
    )

    fore, back = sums((near_f2, fore), (near_b2, back))
    fore, back = ring(fore, back)
    grad_both = swap_core(grad_x)
    terms = shared_part_terms(
        info,
        [tokens, tok_core, tok_x, tok_both],
        [out_grad, grad_core, grad_x, grad_both],
        shared_gate,
        shared_up,
        shared_down,
    )
    fore, back, *terms = tie((fore, back, *terms))

    swapped = swap_core(terms[3])
    near = swap_core(terms[1])
    fore, back = sums((near_f1, fore), (near_b1, back))
    fore, back = ring(fore, back)
    (far,) = sums((terms[2], swapped))
    shared_far = swap_x(far)
    total = near0.astype(F32) + fore.astype(F32) + back.astype(F32)
    shared_part = terms[0].astype(F32) + near.astype(F32) + shared_far.astype(F32)
    prob_grad = jnp.concatenate(
        [total[rows:, i * rows : (i + 1) * rows] for i in range(tiles)], axis=0
    ).T
    gate_total = jnp.sum(router_probs * prob_grad, axis=1, keepdims=True)
    logit_grad = (router_probs * (prob_grad - gate_total)).astype(BF16)
    router_part = jnp.einsum("te,de->td", logit_grad, router_weight, preferred_element_type=F32)
    return (shared_part + total[:rows] + router_part).astype(BF16)


def per_device(*args):
    tokens, router_probs, gate_weight, gate_saved = args[0], args[3], args[5], args[8]
    rows, cols = tokens.shape
    expert_total = router_probs.shape[1]
    ring = (
        lax.axis_size("expert") == 8
        and lax.axis_size("tensor") == 4
        and gate_weight.shape[0] == 2
        and gate_saved.shape[1] == 8 * 64
        and gate_saved.shape[2] % 256 == 0
        and rows == 128
        and expert_total == 16
        and cols % 256 == 0
        and cols >= 6 * rows
    )
    return (per_device_ring if ring else per_device_wide)(*args)


def solution(mesh):

    return jax.shard_map(
        per_device,
        mesh=mesh,
        in_specs=(
            P("expert", "tensor"),
            P("expert", "tensor"),
            P("expert", None),
            P("expert", None),
            P("tensor", None),
            P("expert", "tensor", None),
            P("expert", "tensor", None),
            P("expert", None, "tensor"),
            P("expert", None, None),
            P("expert", None, None),
            P(None, "tensor"),
            P(None, "tensor"),
            P("tensor", None),
        ),
        out_specs=P("expert", "tensor"),
        check_vma=False,
    )
```

```python
import functools

import jax
import jax.numpy as jnp
from jax import lax
from jax.experimental import pallas as pl
from jax.experimental.pallas import tpu as pltpu
from jax.sharding import PartitionSpec as P


def silu_parts(preact):
    sigmoid_value = jax.nn.sigmoid(preact)
    return (preact * sigmoid_value, sigmoid_value * (1.0 + preact * (1.0 - sigmoid_value)))


def per_device_wide(
    tokens,
    out_grad,
    expert_ids,
    router_probs,
    router_weight,
    gate_weight,
    up_weight,
    down_weight,
    gate_saved,
    up_saved,
    shared_gate,
    shared_up,
    shared_down,
):
    groups = lax.axis_size("expert")
    local_count, slot_count, hidden_units = gate_saved.shape
    capacity = slot_count // groups
    token_rows, route_width = expert_ids.shape
    expert_total = router_probs.shape[1]
    feature_cols = tokens.shape[1]
    column_total = local_count * groups * capacity
    flat_ids = expert_ids.reshape(-1)
    onehot = (flat_ids[:, None] == jnp.arange(expert_total, dtype=jnp.int32)[None, :]).astype(
        jnp.int32
    )
    slot_index = jnp.sum((jnp.cumsum(onehot, axis=0) - onehot) * onehot, axis=1)
    kept_mask = slot_index < capacity
    owner_group = flat_ids // local_count
    local_expert = flat_ids % local_count
    column_id = jnp.where(
        kept_mask, local_expert * (groups * capacity) + owner_group * capacity + slot_index, -1
    )
    column_grid = column_id.reshape(token_rows, route_width)
    column_match = (
        column_grid[:, :, None] == jnp.arange(column_total, dtype=jnp.int32)[None, None, :]
    )
    placement = jnp.sum(column_match.astype(jnp.float32), axis=1).astype(jnp.bfloat16)
    sectioning = jnp.einsum(
        "tc,td->cd", placement, out_grad, preferred_element_type=jnp.float32
    ).astype(jnp.bfloat16)
    outgoing = sectioning.reshape(local_count, groups, capacity * feature_cols)
    token_piece = lax.all_gather(tokens, "tensor", axis=1, tiled=True)
    grad_piece = lax.all_gather(out_grad, "tensor", axis=1, tiled=True)
    gate_pre = jnp.dot(token_piece, shared_gate, preferred_element_type=jnp.float32)
    up_pre = jnp.dot(token_piece, shared_up, preferred_element_type=jnp.float32)
    hidden_pre = jnp.einsum(
        "tc,fc->tf", grad_piece, shared_down, preferred_element_type=jnp.float32
    )
    active, slope_term = silu_parts(gate_pre)
    shared_dgate = (hidden_pre * up_pre * slope_term).astype(jnp.bfloat16)
    shared_dup = (hidden_pre * active).astype(jnp.bfloat16)
    shared_term = jnp.einsum(
        "tf,df->td", shared_dgate, shared_gate, preferred_element_type=jnp.float32
    ) + jnp.einsum("tf,df->td", shared_dup, shared_up, preferred_element_type=jnp.float32)
    shared_part = lax.psum_scatter(
        shared_term.astype(jnp.bfloat16), "tensor", scatter_dimension=1, tiled=True
    ).astype(jnp.float32)
    arrived = lax.all_to_all(outgoing, "expert", split_axis=1, concat_axis=1, tiled=True)
    arrived = arrived.reshape(local_count, slot_count, feature_cols)
    partial_hidden = jnp.einsum(
        "esd,efd->esf", arrived, down_weight, preferred_element_type=jnp.float32
    )
    up_full = up_saved.astype(jnp.float32)
    hidden_grad = lax.psum(partial_hidden.astype(jnp.bfloat16), "tensor").astype(jnp.float32)
    active, slope_term = silu_parts(gate_saved.astype(jnp.float32))
    d_gate = (hidden_grad * up_full * slope_term).astype(jnp.bfloat16)
    d_up = (hidden_grad * active).astype(jnp.bfloat16)
    score_rows = jnp.sum(up_full * d_up.astype(jnp.float32), axis=2).astype(jnp.bfloat16)
    expert_grad = jnp.einsum(
        "esf,edf->esd", d_gate, gate_weight, preferred_element_type=jnp.float32
    ) + jnp.einsum("esf,edf->esd", d_up, up_weight, preferred_element_type=jnp.float32)
    expert_grad = expert_grad.astype(jnp.bfloat16)
    back_grad, back_score = (
        lax.all_to_all(
            expert_grad.reshape(local_count, groups, capacity * feature_cols),
            "expert",
            split_axis=1,
            concat_axis=1,
            tiled=True,
        ),
        lax.all_to_all(
            score_rows.reshape(local_count, groups, capacity),
            "expert",
            split_axis=1,
            concat_axis=1,
            tiled=True,
        ),
    )
    returned_rows = back_grad.reshape(column_total, feature_cols)
    returned_scores = back_score.reshape(column_total).astype(jnp.float32)
    kept_value = kept_mask.astype(jnp.float32)
    probs_rows = jnp.repeat(router_probs, route_width, axis=0)
    onehot_float = onehot.astype(jnp.float32)
    gate_value = jnp.sum(onehot_float * probs_rows, axis=1)
    route_weight = (gate_value * kept_value).reshape(token_rows, route_width)
    combine_weight = jnp.sum(jnp.where(column_match, route_weight[:, :, None], 0.0), axis=1)
    routed_part = jnp.dot(
        combine_weight,
        returned_rows.astype(jnp.float32),
        precision=lax.Precision.HIGHEST,
        preferred_element_type=jnp.float32,
    )
    safe_column = jnp.maximum(column_id, 0)
    route_score = returned_scores[safe_column] * kept_value
    prob_grad = jnp.sum(
        (onehot_float * route_score[:, None]).reshape(token_rows, route_width, expert_total), axis=1
    )
    gate_total = jnp.sum((gate_value * route_score).reshape(token_rows, route_width), axis=1)
    logit_grad = (router_probs * (prob_grad - gate_total[:, None])).astype(jnp.bfloat16)
    router_part = jnp.einsum(
        "te,de->td", logit_grad, router_weight, preferred_element_type=jnp.float32
    )
    return (shared_part + routed_part + router_part).astype(jnp.bfloat16)


F32, BF16 = jnp.float32, jnp.bfloat16
LAST = (((1,), (1,)), ((), ()))
FIRST = (((0,), (0,)), ((), ()))
TOP_ROWS = 64
INFO_BLOCKS = 7


def call(kernel, megabytes, out_shape, scratch_shapes=(), scalars=0, far=0):
    def run(*operands):
        near = len(operands) - scalars - far
        memory = [pltpu.SMEM] * scalars + [pltpu.VMEM] * near + [pl.ANY] * far
        return pl.pallas_call(
            kernel,
            in_specs=[pl.BlockSpec(memory_space=m) for m in memory],
            out_specs=jax.tree.map(lambda _: pl.BlockSpec(memory_space=pltpu.VMEM), out_shape),
            out_shape=out_shape,
            scratch_shapes=scratch_shapes,
            compiler_params=pltpu.CompilerParams(vmem_limit_bytes=megabytes * 1024 * 1024),
            cost_estimate=pl.CostEstimate(flops=1000, bytes_accessed=1000, transcendentals=0),
        )(*operands)

    return run


def sum_kernel(groups, *refs):
    count = sum(groups)
    at = 0
    for out_ref, size in zip(refs[count:], groups):
        total = refs[at][...].astype(F32)
        for ref in refs[at + 1 : at + size]:
            total = total + ref[...].astype(F32)
        out_ref[...] = total.astype(BF16)
        at += size


def sums(*groups):
    return call(
        functools.partial(sum_kernel, [len(g) for g in groups]),
        2,
        [jax.ShapeDtypeStruct(g[0].shape, BF16) for g in groups],
    )(*[a for g in groups for a in g])


def halves_kernel(fore_ref, back_ref, top_ref, bottom_ref):
    top_ref[...] = fore_ref[0:TOP_ROWS, :]
    bottom_ref[...] = back_ref[TOP_ROWS:, :]


def halves_of(fore, back):
    rows, cols = fore.shape
    return call(
        halves_kernel,
        2,
        [
            jax.ShapeDtypeStruct((TOP_ROWS, cols), BF16),
            jax.ShapeDtypeStruct((rows - TOP_ROWS, cols), BF16),
        ],
    )(fore, back)


def join_kernel(near_f_ref, top_ref, near_b_ref, bottom_ref, fore_ref, back_ref):
    top = near_f_ref[0:TOP_ROWS, :].astype(F32) + top_ref[...].astype(F32)
    fore_ref[0:TOP_ROWS, :] = top.astype(BF16)
    fore_ref[TOP_ROWS:, :] = near_f_ref[TOP_ROWS:, :]
    back_ref[0:TOP_ROWS, :] = near_b_ref[0:TOP_ROWS, :]
    bottom = near_b_ref[TOP_ROWS:, :].astype(F32) + bottom_ref[...].astype(F32)
    back_ref[TOP_ROWS:, :] = bottom.astype(BF16)


def join(near_f, top, near_b, bottom):
    shape = jax.ShapeDtypeStruct(near_f.shape, BF16)
    return call(join_kernel, 2, [shape, shape])(near_f, top, near_b, bottom)


def payload_kernel(capacity, ids_hbm, probs_hbm, grad_hbm, out_ref, ids_ref, probs_ref, sems):
    expert_total, rows = probs_ref.shape
    cols = grad_hbm.shape[1]
    copies = [
        pltpu.make_async_copy(ids_hbm, ids_ref, sems.at[0]),
        pltpu.make_async_copy(probs_hbm, probs_ref, sems.at[1]),
        pltpu.make_async_copy(grad_hbm, out_ref.at[0:rows, :], sems.at[2]),
    ]
    for copy in copies:
        copy.start()
    experts = lax.broadcasted_iota(jnp.int32, (expert_total, rows), 0)
    row_at = lax.broadcasted_iota(jnp.int32, (rows, rows), 0)
    col_at = lax.broadcasted_iota(jnp.int32, (rows, rows), 1)
    lower = jnp.where(row_at < col_at, 1.0, 0.0).astype(BF16)
    copies[0].wait()
    ids = ids_ref[...]
    member = jnp.zeros((expert_total, rows), F32)
    for k in range(ids.shape[0]):
        member = member + jnp.where(ids[k : k + 1, :] == experts, 1.0, 0.0)
    before = jnp.dot(member.astype(BF16), lower, preferred_element_type=F32)
    slot = jnp.where((member > 0.5) & (before < capacity), before, -1.0)
    copies[1].wait()
    probs = probs_ref[...]
    high = probs.astype(BF16).astype(F32)
    parts = [slot, high, probs - high]
    pieces = [a[8 * i : 8 * i + 8] for a in parts for i in range(expert_total // 8)]
    pieces.append(jnp.zeros((8, cols - len(pieces) * rows), F32))
    out_ref[rows : rows + 8, :] = jnp.concatenate(pieces, axis=1).astype(BF16)
    copies[2].wait()


def payload_of(ids_t, probs_t, grad, capacity):
    rows, cols = grad.shape
    return call(
        functools.partial(payload_kernel, capacity),
        60,
        jax.ShapeDtypeStruct((rows + 8, cols), BF16),
        [
            pltpu.VMEM(ids_t.shape, jnp.int32),
            pltpu.VMEM(probs_t.shape, F32),
            pltpu.SemaphoreType.DMA((3,)),
        ],
        0,
        3,
    )(ids_t, probs_t, grad)


def hidden_kernel(halves, tiles, capacity, steps, info_ref, *refs):
    block_refs = refs[: len(halves)]
    weight_ref, placed_ref = refs[len(halves)], refs[-1]
    out_refs = refs[len(halves) + 1 : -1]
    core, tile, row = info_ref[0], info_ref[1], info_ref[2]
    blocks, at = [], 0
    while at < len(halves):
        size = 2 if halves[at] else 1
        blocks.append(block_refs[at : at + size])
        at += size
    rows = 128
    units = weight_ref.shape[1]

    def pick(meta, kind, which):
        value = meta[:, kind * tiles * rows : (kind * tiles + 1) * rows]
        for i in range(1, tiles):
            at_lane = (kind * tiles + i) * rows
            value = jnp.where(tile == i, meta[:, at_lane : at_lane + rows], value)
        line = lax.broadcasted_iota(jnp.int32, (8, rows), 0)
        return jnp.sum(jnp.where(line == which, value, 0.0), axis=0, keepdims=True)

    slot_at = lax.broadcasted_iota(jnp.int32, (capacity, rows), 0).astype(F32)
    for step in steps:
        expert = 1 - core if step == 0 else core
        for b, block in enumerate(blocks):
            last = block[-1]
            meta = last[last.shape[0] - 8 :, :].astype(F32)
            match = jnp.where(slot_at == pick(meta, 0, row + expert), 1.0, 0.0).astype(BF16)
            if len(block) == 1:
                data = block[0][0:rows, :]
            else:
                data = jnp.concatenate([block[0][...], block[1][0 : rows - TOP_ROWS, :]], axis=0)
            placed = jnp.dot(match, data, preferred_element_type=F32)
            placed_ref[step, b * capacity : (b + 1) * capacity, :] = placed.astype(BF16)
            if step == 1:
                lines = [pick(meta, 0, row), pick(meta, 0, row + 1)]
                lines += [pick(meta, 1, row) + pick(meta, 2, row)]
                lines += [pick(meta, 1, row + 1) + pick(meta, 2, row + 1)]
                lines += [jnp.zeros((4, rows), F32)]
                out_refs[-1][8 * b : 8 * b + 8, :] = jnp.concatenate(lines, axis=0)
        out_ref = out_refs[steps.index(step)]
        for n in range(0, units, 256):
            value = lax.dot_general(
                placed_ref[step],
                weight_ref[expert, n : n + 256, :],
                LAST,
                preferred_element_type=F32,
            )
            out_ref[:, n : n + 256] = value.astype(BF16)


def hidden_part(info, blocks, down_weight, tiles, capacity, steps):
    local_count, hidden_units, cols = down_weight.shape
    flat, halves = [], []
    for block in blocks:
        pair = isinstance(block, tuple)
        flat += list(block) if pair else [block]
        halves += [pair, pair] if pair else [False]
    count = len(blocks)
    shape = (count * capacity, hidden_units)
    return call(
        functools.partial(hidden_kernel, halves, tiles, capacity, steps),
        10,
        [jax.ShapeDtypeStruct(shape, BF16)] * len(steps)
        + [jax.ShapeDtypeStruct((8 * count, 128), F32)] * (1 in steps),
        [pltpu.VMEM((2, count * capacity, cols), BF16)],
        1,
    )(info, *flat, down_weight)


def grad_kernel(counts, chunk, split, tiles, capacity, info_ref, *refs):
    groups = len(counts)
    total = sum(counts)
    hidden_refs = refs[: 3 * groups]
    gate_ref, up_ref, gate_w_ref, up_w_ref = refs[3 * groups : 3 * groups + 4]
    out_refs = refs[3 * groups + 4 : -2]
    dgate_ref, dup_ref = refs[-2:]
    core, tile, row = info_ref[0], info_ref[1], info_ref[2]
    rows = 128
    cols = gate_w_ref.shape[1]
    line = lax.broadcasted_iota(jnp.int32, (8, rows), 0)
    slot_at = lax.broadcasted_iota(jnp.int32, (capacity, rows), 0).astype(F32)
    combine, scores = [], []
    b = 0
    for g in range(groups):
        full_ref, pair_ref, meta_ref = hidden_refs[3 * g : 3 * g + 3]
        for i in range(counts[g]):
            span = slice(i * capacity, (i + 1) * capacity)
            store = slice(b * capacity, (b + 1) * capacity)
            saved = pl.ds(pl.multiple_of(info_ref[INFO_BLOCKS + chunk[b]] * capacity, capacity), capacity)
            lines = meta_ref[8 * i : 8 * i + 8, :]
            score_rows = jnp.zeros((8, rows), F32)
            stacked = []
            for e in range(2):
                hidden = jnp.where(core == e, full_ref[span, :], pair_ref[span, :]).astype(F32)
                gate = gate_ref[e, saved, :].astype(F32)
                up = up_ref[e, saved, :].astype(F32)
                active, slope_term = silu_parts(gate)
                dup = hidden * active
                match = slot_at == lines[e : e + 1, :]
                weight = jnp.sum(
                    jnp.where(match, lines[2 + e : 3 + e, :], 0.0), axis=1, keepdims=True
                )
                dgate_ref[e, store, :] = (hidden * up * slope_term * weight).astype(BF16)
                dup_ref[e, store, :] = (dup * weight).astype(BF16)
                score = jnp.sum(up * dup.astype(BF16).astype(F32), axis=1, keepdims=True)
                score = score.astype(BF16).astype(F32)
                token_score = jnp.sum(jnp.where(match, score, 0.0), axis=0, keepdims=True)
                score_rows = score_rows + jnp.where(line == row + e, token_score, 0.0)
                stacked.append(jnp.where(match, 1.0, 0.0).astype(BF16))
            combine.append(jnp.concatenate(stacked, axis=0))
            scores.append(score_rows)
            b += 1
    for n in range(0, cols, 256):
        grads = []
        for e in range(2):
            value = lax.dot_general(
                dgate_ref[e], gate_w_ref[e, n : n + 256, :], LAST, preferred_element_type=F32
            )
            value = value + lax.dot_general(
                dup_ref[e], up_w_ref[e, n : n + 256, :], LAST, preferred_element_type=F32
            )
            grads.append(value.astype(BF16))
        for b in range(total):
            span = slice(b * capacity, (b + 1) * capacity)
            pile = jnp.concatenate([g[span] for g in grads], axis=0)
            value = lax.dot_general(combine[b], pile, FIRST, preferred_element_type=F32)
            if n == 0:
                lanes = [jnp.where(tile == i, scores[b], 0.0) for i in range(tiles)]
                lanes = jnp.concatenate(lanes, axis=1)
            else:
                lanes = jnp.zeros((8, 256), F32)
            if split:
                out_refs[2 * b][:, n : n + 256] = value[:TOP_ROWS].astype(BF16)
                low = jnp.concatenate([value[TOP_ROWS:], lanes], axis=0)
                out_refs[2 * b + 1][:, n : n + 256] = low.astype(BF16)
            else:
                out_refs[b][:, n : n + 256] = jnp.concatenate([value, lanes], axis=0).astype(BF16)


def grad_part(info, parts, saved, weights, counts, chunk, split, tiles, capacity):
    local_count, cols, hidden_units = weights[0].shape
    total = sum(counts)
    heights = [TOP_ROWS, 136 - TOP_ROWS] * total if split else [136] * total
    return call(
        functools.partial(grad_kernel, counts, chunk, split, tiles, capacity),
        14,
        [jax.ShapeDtypeStruct((h, cols), BF16) for h in heights],
        [
            pltpu.VMEM((2, total * capacity, hidden_units), BF16),
            pltpu.VMEM((2, total * capacity, hidden_units), BF16),
        ],
        1,
    )(info, *parts, *saved, *weights)


def shared_spans(info_ref, cols):
    here = info_ref[3]
    return [
        pl.ds(pl.multiple_of(jnp.bitwise_xor(here, q) * cols, cols), cols) for q in range(4)
    ]


def shared_slopes_kernel(info_ref, *refs):
    token_refs, grad_refs = refs[0:4], refs[4:8]
    gate_ref, up_ref, down_ref, dgate_ref, dup_ref = refs[8:]
    rows, cols = token_refs[0].shape
    units = gate_ref.shape[1]
    spans = shared_spans(info_ref, cols)
    gate_pre = jnp.zeros((rows, units), F32)
    up_pre = jnp.zeros((rows, units), F32)
    hidden_pre = jnp.zeros((rows, units), F32)
    for q in range(4):
        token, grad = token_refs[q][...], grad_refs[q][...]
        gate_pre = gate_pre + jnp.dot(token, gate_ref[spans[q], :], preferred_element_type=F32)
        up_pre = up_pre + jnp.dot(token, up_ref[spans[q], :], preferred_element_type=F32)
        hidden_pre = hidden_pre + lax.dot_general(
            grad, down_ref[:, spans[q]], LAST, preferred_element_type=F32
        )
    active, slope_term = silu_parts(gate_pre)
    dgate_ref[...] = (hidden_pre * up_pre * slope_term).astype(BF16)
    dup_ref[...] = (hidden_pre * active).astype(BF16)


def shared_slopes(info, token_blocks, grad_blocks, shared_gate, shared_up, shared_down):
    shape = jax.ShapeDtypeStruct((token_blocks[0].shape[0], shared_gate.shape[1]), BF16)
    return call(shared_slopes_kernel, 8, [shape, shape], (), 1)(
        info, *token_blocks, *grad_blocks, shared_gate, shared_up, shared_down
    )


def shared_terms_kernel(info_ref, dgate_ref, dup_ref, gate_ref, up_ref, *out_refs):
    cols = out_refs[0].shape[1]
    spans = shared_spans(info_ref, cols)
    dgate, dup = dgate_ref[...], dup_ref[...]
    for q in range(4):
        term = lax.dot_general(dgate, gate_ref[spans[q], :], LAST, preferred_element_type=F32)
        term = term + lax.dot_general(dup, up_ref[spans[q], :], LAST, preferred_element_type=F32)
        out_refs[q][...] = term.astype(BF16)


def shared_terms(info, dgate, dup, shared_gate, shared_up, cols):
    shape = jax.ShapeDtypeStruct((dgate.shape[0], cols), BF16)
    return call(shared_terms_kernel, 8, [shape] * 4, (), 1)(
        info, dgate, dup, shared_gate, shared_up
    )


def ring_place(position):
    position = position % 8
    return jnp.where(position < 4, 2 * position, 15 - 2 * position)


def per_device_ring(
    tokens,
    out_grad,
    expert_ids,
    router_probs,
    router_weight,
    gate_weight,
    up_weight,
    down_weight,
    gate_saved,
    up_saved,
    shared_gate,
    shared_up,
    shared_down,
):
    slot_count = gate_saved.shape[1]
    capacity = slot_count // 8
    rows, cols = tokens.shape
    expert_total = router_probs.shape[1]
    tiles = expert_total // 8
    order = [0, 2, 4, 6, 7, 5, 3, 1]
    ahead = [(order[i], order[(i + 1) % 8]) for i in range(8)]
    behind = [(order[i], order[(i - 1) % 8]) for i in range(8)]
    x_pairs = [(i, i ^ 2) for i in range(4)]
    core_pairs = [(i, i ^ 1) for i in range(4)]
    me = lax.axis_index("expert")
    place = jnp.where(me % 2 == 0, me // 2, 7 - me // 2)
    here = lax.axis_index("tensor")
    first = me * 2
    base = [here % 2, first // 8, first % 8]
    tie = lax.optimization_barrier

    def swap_x(a):
        return lax.ppermute(a, "tensor", x_pairs)

    def swap_core(a):
        return lax.ppermute(a, "tensor", core_pairs)

    def ring(fore, back):
        return lax.ppermute(fore, "expert", ahead), lax.ppermute(back, "expert", behind)

    def hidden(blocks, steps=(0, 1)):
        return hidden_part(info, blocks, down_weight, tiles, capacity, steps)

    def grads(saved, weights, *parts):
        chunk = sum((part[0] for part in parts), ())
        return grad_part(
            info,
            [a for part in parts for a in part[1:]],
            saved,
            weights,
            [len(part[0]) for part in parts],
            chunk,
            chunk == (4,),
            tiles,
            capacity,
        )

    numbers = base + [here] + [ring_place(place + d) for d in range(-3, 5)]
    info = jnp.stack([jnp.asarray(n, jnp.int32) for n in numbers])
    payload = payload_of(expert_ids.T, router_probs.T, out_grad, capacity)

    payload, tokens, out_grad, info = tie((payload, tokens, out_grad, info))
    fore, back = ring(payload, payload)
    grad_x = swap_x(out_grad)
    fore1, back1, grad_x = tie((fore, back, grad_x))

    fore, back = ring(fore1, back1)
    tok_x = swap_x(tokens)
    other1, mine1, meta1 = hidden([payload, fore1, back1])
    fore2, back2, other1, mine1, tok_x = tie((fore, back, other1, mine1, tok_x))

    fore, back = ring(fore2, back2)
    (chip1,) = sums((mine1, swap_core(other1)))
    far1 = swap_x(chip1)
    other2, mine2, meta2 = hidden([fore2, back2])
    (chip2,) = sums((mine2, swap_core(other2)))
    tok_core, grad_core = swap_core(tokens), swap_core(out_grad)
    fore3, back3, chip1, chip2, tok_core, grad_core = tie(
        (fore, back, chip1, chip2, tok_core, grad_core)
    )

    top, bottom = ring(*halves_of(fore3, back3))
    far2 = swap_x(chip2)
    other3, mine3, meta3 = hidden([fore3, back3])
    tok_both, grad_both = swap_core(tok_x), swap_core(grad_x)
    top, bottom, chip2, other3, mine3, far1, far2, tok_both, grad_both = tie(
        (top, bottom, chip2, other3, mine3, far1, far2, tok_both, grad_both)
    )

    (other4,) = hidden([(top, bottom)], (0,))
    swapped4 = swap_core(other4)
    top, bottom, other4 = tie((top, bottom, other4))
    mine4, meta4 = hidden([(top, bottom)], (1,))
    (chip4,) = sums((mine4, swapped4))
    chip4, other3, dgate_in = tie((chip4, other3, tokens))
    far4 = swap_x(chip4)
    (chip3,) = sums((mine3, swap_core(other3)))
    far3 = swap_x(chip3)
    chip3, chip2 = tie((chip3, chip2))
    (full2,) = sums((chip2, far2))
    pair2 = swap_core(full2)
    dgate, dup = shared_slopes(
        info,
        [dgate_in, tok_core, tok_x, tok_both],
        [out_grad, grad_core, grad_x, grad_both],
        shared_gate,
        shared_up,
        shared_down,
    )
    far4, full2, pair2, dgate, dup = tie((far4, full2, pair2, dgate, dup))
    (full4,) = sums((chip4, far4))
    pair4 = swap_core(full4)
    saved = (gate_saved, up_saved)
    weights = (gate_weight, up_weight)
    top, bottom = grads(saved, weights, ((4,), full4, pair4, meta4))

    top, bottom, pair2, full2, far3, chip1 = tie((top, bottom, pair2, full2, far3, chip1))
    fore, back = ring(top, bottom)
    (full3,) = sums((chip3, far3))
    pair3 = swap_core(full3)
    (full1,) = sums((chip1, far1))
    pair1 = swap_core(full1)
    near_b3, near_f3, near_b2, near_f2 = grads(
        saved, weights, ((-3, 3), full3, pair3, meta3), ((-2, 2), full2, pair2, meta2)
    )
    fore, back, near_f3, near_b3, near_f2, near_b2, full1, pair1 = tie(
        (fore, back, near_f3, near_b3, near_f2, near_b2, full1, pair1)
    )

    fore, back = join(near_f3, fore, near_b3, back)
    fore, back = ring(fore, back)
    near0, near_b1, near_f1 = grads(saved, weights, ((0, -1, 1), full1, pair1, meta1))
    fore, back, near0, near_b1, near_f1, dgate = tie(
        (fore, back, near0, near_b1, near_f1, dgate)
    )

    fore, back = sums((near_f2, fore), (near_b2, back))
    fore, back = ring(fore, back)
    terms = shared_terms(info, dgate, dup, shared_gate, shared_up, cols)
    swapped, near = swap_core(terms[3]), swap_core(terms[1])
    fore, back, swapped, near = tie((fore, back, swapped, near))

    fore, back, far = sums((near_f1, fore), (near_b1, back), (terms[2], swapped))
    fore, back = ring(fore, back)
    shared_far = swap_x(far)
    total = near0.astype(F32) + fore.astype(F32) + back.astype(F32)
    shared_part = terms[0].astype(F32) + near.astype(F32) + shared_far.astype(F32)
    prob_grad = jnp.concatenate(
        [total[rows:, i * rows : (i + 1) * rows] for i in range(tiles)], axis=0
    ).T
    gate_total = jnp.sum(router_probs * prob_grad, axis=1, keepdims=True)
    logit_grad = (router_probs * (prob_grad - gate_total)).astype(BF16)
    router_part = jnp.einsum("te,de->td", logit_grad, router_weight, preferred_element_type=F32)
    return (shared_part + total[:rows] + router_part).astype(BF16)


def per_device(*args):
    tokens, router_probs, gate_weight, gate_saved = args[0], args[3], args[5], args[8]
    rows, cols = tokens.shape
    expert_total = router_probs.shape[1]
    ring = (
        lax.axis_size("expert") == 8
        and lax.axis_size("tensor") == 4
        and gate_weight.shape[0] == 2
        and gate_saved.shape[1] == 8 * 64
        and gate_saved.shape[2] % 256 == 0
        and rows == 128
        and expert_total == 16
        and cols % 256 == 0
        and cols >= 6 * rows
    )
    return (per_device_ring if ring else per_device_wide)(*args)


def solution(mesh):

    return jax.shard_map(
        per_device,
        mesh=mesh,
        in_specs=(
            P("expert", "tensor"),
            P("expert", "tensor"),
            P("expert", None),
            P("expert", None),
            P("tensor", None),
            P("expert", "tensor", None),
            P("expert", "tensor", None),
            P("expert", None, "tensor"),
            P("expert", None, None),
            P("expert", None, None),
            P(None, "tensor"),
            P(None, "tensor"),
            P("tensor", None),
        ),
        out_specs=P("expert", "tensor"),
        check_vma=False,
    )
```

```python
import functools

import jax
import jax.numpy as jnp
from jax import lax
from jax.experimental import pallas as pl
from jax.experimental.pallas import tpu as pltpu
from jax.sharding import PartitionSpec as P


def silu_parts(preact):
    sigmoid_value = jax.nn.sigmoid(preact)
    return (preact * sigmoid_value, sigmoid_value * (1.0 + preact * (1.0 - sigmoid_value)))


def per_device_wide(
    tokens,
    out_grad,
    expert_ids,
    router_probs,
    router_weight,
    gate_weight,
    up_weight,
    down_weight,
    gate_saved,
    up_saved,
    shared_gate,
    shared_up,
    shared_down,
):
    groups = lax.axis_size("expert")
    local_count, slot_count, hidden_units = gate_saved.shape
    capacity = slot_count // groups
    token_rows, route_width = expert_ids.shape
    expert_total = router_probs.shape[1]
    feature_cols = tokens.shape[1]
    column_total = local_count * groups * capacity
    flat_ids = expert_ids.reshape(-1)
    onehot = (flat_ids[:, None] == jnp.arange(expert_total, dtype=jnp.int32)[None, :]).astype(
        jnp.int32
    )
    slot_index = jnp.sum((jnp.cumsum(onehot, axis=0) - onehot) * onehot, axis=1)
    kept_mask = slot_index < capacity
    owner_group = flat_ids // local_count
    local_expert = flat_ids % local_count
    column_id = jnp.where(
        kept_mask, local_expert * (groups * capacity) + owner_group * capacity + slot_index, -1
    )
    column_grid = column_id.reshape(token_rows, route_width)
    column_match = (
        column_grid[:, :, None] == jnp.arange(column_total, dtype=jnp.int32)[None, None, :]
    )
    placement = jnp.sum(column_match.astype(jnp.float32), axis=1).astype(jnp.bfloat16)
    sectioning = jnp.einsum(
        "tc,td->cd", placement, out_grad, preferred_element_type=jnp.float32
    ).astype(jnp.bfloat16)
    outgoing = sectioning.reshape(local_count, groups, capacity * feature_cols)
    token_piece = lax.all_gather(tokens, "tensor", axis=1, tiled=True)
    grad_piece = lax.all_gather(out_grad, "tensor", axis=1, tiled=True)
    gate_pre = jnp.dot(token_piece, shared_gate, preferred_element_type=jnp.float32)
    up_pre = jnp.dot(token_piece, shared_up, preferred_element_type=jnp.float32)
    hidden_pre = jnp.einsum(
        "tc,fc->tf", grad_piece, shared_down, preferred_element_type=jnp.float32
    )
    active, slope_term = silu_parts(gate_pre)
    shared_dgate = (hidden_pre * up_pre * slope_term).astype(jnp.bfloat16)
    shared_dup = (hidden_pre * active).astype(jnp.bfloat16)
    shared_term = jnp.einsum(
        "tf,df->td", shared_dgate, shared_gate, preferred_element_type=jnp.float32
    ) + jnp.einsum("tf,df->td", shared_dup, shared_up, preferred_element_type=jnp.float32)
    shared_part = lax.psum_scatter(
        shared_term.astype(jnp.bfloat16), "tensor", scatter_dimension=1, tiled=True
    ).astype(jnp.float32)
    arrived = lax.all_to_all(outgoing, "expert", split_axis=1, concat_axis=1, tiled=True)
    arrived = arrived.reshape(local_count, slot_count, feature_cols)
    partial_hidden = jnp.einsum(
        "esd,efd->esf", arrived, down_weight, preferred_element_type=jnp.float32
    )
    up_full = up_saved.astype(jnp.float32)
    hidden_grad = lax.psum(partial_hidden.astype(jnp.bfloat16), "tensor").astype(jnp.float32)
    active, slope_term = silu_parts(gate_saved.astype(jnp.float32))
    d_gate = (hidden_grad * up_full * slope_term).astype(jnp.bfloat16)
    d_up = (hidden_grad * active).astype(jnp.bfloat16)
    score_rows = jnp.sum(up_full * d_up.astype(jnp.float32), axis=2).astype(jnp.bfloat16)
    expert_grad = jnp.einsum(
        "esf,edf->esd", d_gate, gate_weight, preferred_element_type=jnp.float32
    ) + jnp.einsum("esf,edf->esd", d_up, up_weight, preferred_element_type=jnp.float32)
    expert_grad = expert_grad.astype(jnp.bfloat16)
    back_grad, back_score = (
        lax.all_to_all(
            expert_grad.reshape(local_count, groups, capacity * feature_cols),
            "expert",
            split_axis=1,
            concat_axis=1,
            tiled=True,
        ),
        lax.all_to_all(
            score_rows.reshape(local_count, groups, capacity),
            "expert",
            split_axis=1,
            concat_axis=1,
            tiled=True,
        ),
    )
    returned_rows = back_grad.reshape(column_total, feature_cols)
    returned_scores = back_score.reshape(column_total).astype(jnp.float32)
    kept_value = kept_mask.astype(jnp.float32)
    probs_rows = jnp.repeat(router_probs, route_width, axis=0)
    onehot_float = onehot.astype(jnp.float32)
    gate_value = jnp.sum(onehot_float * probs_rows, axis=1)
    route_weight = (gate_value * kept_value).reshape(token_rows, route_width)
    combine_weight = jnp.sum(jnp.where(column_match, route_weight[:, :, None], 0.0), axis=1)
    routed_part = jnp.dot(
        combine_weight,
        returned_rows.astype(jnp.float32),
        precision=lax.Precision.HIGHEST,
        preferred_element_type=jnp.float32,
    )
    safe_column = jnp.maximum(column_id, 0)
    route_score = returned_scores[safe_column] * kept_value
    prob_grad = jnp.sum(
        (onehot_float * route_score[:, None]).reshape(token_rows, route_width, expert_total), axis=1
    )
    gate_total = jnp.sum((gate_value * route_score).reshape(token_rows, route_width), axis=1)
    logit_grad = (router_probs * (prob_grad - gate_total[:, None])).astype(jnp.bfloat16)
    router_part = jnp.einsum(
        "te,de->td", logit_grad, router_weight, preferred_element_type=jnp.float32
    )
    return (shared_part + routed_part + router_part).astype(jnp.bfloat16)


F32, BF16 = jnp.float32, jnp.bfloat16
LAST = (((1,), (1,)), ((), ()))
FIRST = (((0,), (0,)), ((), ()))
TOP_ROWS = 64
INFO_BLOCKS = 7


def call(kernel, megabytes, out_shape, scratch_shapes=(), scalars=0, far=0):
    def run(*operands):
        near = len(operands) - scalars - far
        memory = [pltpu.SMEM] * scalars + [pltpu.VMEM] * near + [pl.ANY] * far
        return pl.pallas_call(
            kernel,
            in_specs=[pl.BlockSpec(memory_space=m) for m in memory],
            out_specs=jax.tree.map(lambda _: pl.BlockSpec(memory_space=pltpu.VMEM), out_shape),
            out_shape=out_shape,
            scratch_shapes=scratch_shapes,
            compiler_params=pltpu.CompilerParams(vmem_limit_bytes=megabytes * 1024 * 1024),
            cost_estimate=pl.CostEstimate(flops=1000, bytes_accessed=1000, transcendentals=0),
        )(*operands)

    return run


def sum_kernel(groups, *refs):
    count = sum(groups)
    at = 0
    for out_ref, size in zip(refs[count:], groups):
        total = refs[at][...].astype(F32)
        for ref in refs[at + 1 : at + size]:
            total = total + ref[...].astype(F32)
        out_ref[...] = total.astype(BF16)
        at += size


def sums(*groups):
    return call(
        functools.partial(sum_kernel, [len(g) for g in groups]),
        2,
        [jax.ShapeDtypeStruct(g[0].shape, BF16) for g in groups],
    )(*[a for g in groups for a in g])


def halves_kernel(fore_ref, back_ref, top_ref, bottom_ref):
    top_ref[...] = fore_ref[0:TOP_ROWS, :]
    bottom_ref[...] = back_ref[TOP_ROWS:, :]


def halves_of(fore, back):
    rows, cols = fore.shape
    return call(
        halves_kernel,
        2,
        [
            jax.ShapeDtypeStruct((TOP_ROWS, cols), BF16),
            jax.ShapeDtypeStruct((rows - TOP_ROWS, cols), BF16),
        ],
    )(fore, back)


def join_kernel(near_f_ref, top_ref, near_b_ref, bottom_ref, fore_ref, back_ref):
    top = near_f_ref[0:TOP_ROWS, :].astype(F32) + top_ref[...].astype(F32)
    fore_ref[0:TOP_ROWS, :] = top.astype(BF16)
    fore_ref[TOP_ROWS:, :] = near_f_ref[TOP_ROWS:, :]
    back_ref[0:TOP_ROWS, :] = near_b_ref[0:TOP_ROWS, :]
    bottom = near_b_ref[TOP_ROWS:, :].astype(F32) + bottom_ref[...].astype(F32)
    back_ref[TOP_ROWS:, :] = bottom.astype(BF16)


def join(near_f, top, near_b, bottom):
    shape = jax.ShapeDtypeStruct(near_f.shape, BF16)
    return call(join_kernel, 2, [shape, shape])(near_f, top, near_b, bottom)


def attach_kernel(fore_ref, meta_f_ref, back_ref, meta_b_ref, fore_out, back_out):
    rows = fore_ref.shape[0]
    for ref, meta_ref, out_ref in (
        (fore_ref, meta_f_ref, fore_out),
        (back_ref, meta_b_ref, back_out),
    ):
        out_ref[0:rows, :] = ref[...]
        out_ref[rows:, :] = meta_ref[...]


def attach(fore, meta_f, back, meta_b):
    rows, cols = fore.shape
    shape = jax.ShapeDtypeStruct((rows + 8, cols), BF16)
    return call(attach_kernel, 2, [shape, shape])(fore, meta_f, back, meta_b)


def payload_kernel(
    capacity, ids_hbm, probs_hbm, grad_hbm, out_ref, meta_ref, ids_ref, probs_ref, sems
):
    expert_total, rows = probs_ref.shape
    cols = grad_hbm.shape[1]
    copies = [
        pltpu.make_async_copy(ids_hbm, ids_ref, sems.at[0]),
        pltpu.make_async_copy(probs_hbm, probs_ref, sems.at[1]),
        pltpu.make_async_copy(grad_hbm, out_ref.at[0:rows, :], sems.at[2]),
    ]
    for copy in copies:
        copy.start()
    experts = lax.broadcasted_iota(jnp.int32, (expert_total, rows), 0)
    row_at = lax.broadcasted_iota(jnp.int32, (rows, rows), 0)
    col_at = lax.broadcasted_iota(jnp.int32, (rows, rows), 1)
    lower = jnp.where(row_at < col_at, 1.0, 0.0).astype(BF16)
    copies[0].wait()
    ids = ids_ref[...]
    member = jnp.zeros((expert_total, rows), F32)
    for k in range(ids.shape[0]):
        member = member + jnp.where(ids[k : k + 1, :] == experts, 1.0, 0.0)
    before = jnp.dot(member.astype(BF16), lower, preferred_element_type=F32)
    slot = jnp.where((member > 0.5) & (before < capacity), before, -1.0)
    copies[1].wait()
    probs = probs_ref[...]
    high = probs.astype(BF16).astype(F32)
    parts = [slot, high, probs - high]
    pieces = [a[8 * i : 8 * i + 8] for a in parts for i in range(expert_total // 8)]
    pieces.append(jnp.zeros((8, cols - len(pieces) * rows), F32))
    meta = jnp.concatenate(pieces, axis=1).astype(BF16)
    out_ref[rows : rows + 8, :] = meta
    meta_ref[...] = meta
    copies[2].wait()


def payload_of(ids_t, probs_t, grad, capacity):
    rows, cols = grad.shape
    return call(
        functools.partial(payload_kernel, capacity),
        60,
        [
            jax.ShapeDtypeStruct((rows + 8, cols), BF16),
            jax.ShapeDtypeStruct((8, cols), BF16),
        ],
        [
            pltpu.VMEM(ids_t.shape, jnp.int32),
            pltpu.VMEM(probs_t.shape, F32),
            pltpu.SemaphoreType.DMA((3,)),
        ],
        0,
        3,
    )(ids_t, probs_t, grad)


def hidden_kernel(halves, tiles, capacity, steps, info_ref, *refs):
    block_refs = refs[: len(halves)]
    weight_ref, placed_ref = refs[len(halves)], refs[-1]
    out_refs = refs[len(halves) + 1 : -1]
    core, tile, row = info_ref[0], info_ref[1], info_ref[2]
    blocks, at = [], 0
    while at < len(halves):
        size = 2 if halves[at] else 1
        blocks.append(block_refs[at : at + size])
        at += size
    rows = 128
    units = weight_ref.shape[1]

    def pick(meta, kind, which):
        value = meta[:, kind * tiles * rows : (kind * tiles + 1) * rows]
        for i in range(1, tiles):
            at_lane = (kind * tiles + i) * rows
            value = jnp.where(tile == i, meta[:, at_lane : at_lane + rows], value)
        line = lax.broadcasted_iota(jnp.int32, (8, rows), 0)
        return jnp.sum(jnp.where(line == which, value, 0.0), axis=0, keepdims=True)

    slot_at = lax.broadcasted_iota(jnp.int32, (capacity, rows), 0).astype(F32)
    for step in steps:
        expert = 1 - core if step == 0 else core
        for b, block in enumerate(blocks):
            last = block[-1]
            meta = last[last.shape[0] - 8 :, :].astype(F32)
            match = jnp.where(slot_at == pick(meta, 0, row + expert), 1.0, 0.0).astype(BF16)
            if len(block) == 1:
                data = block[0][0:rows, :]
            else:
                data = jnp.concatenate([block[0][...], block[1][0 : rows - TOP_ROWS, :]], axis=0)
            placed = jnp.dot(match, data, preferred_element_type=F32)
            placed_ref[step, b * capacity : (b + 1) * capacity, :] = placed.astype(BF16)
            if step == 1:
                lines = [pick(meta, 0, row), pick(meta, 0, row + 1)]
                lines += [pick(meta, 1, row) + pick(meta, 2, row)]
                lines += [pick(meta, 1, row + 1) + pick(meta, 2, row + 1)]
                lines += [jnp.zeros((4, rows), F32)]
                out_refs[-1][8 * b : 8 * b + 8, :] = jnp.concatenate(lines, axis=0)
        out_ref = out_refs[steps.index(step)]
        for n in range(0, units, 256):
            value = lax.dot_general(
                placed_ref[step],
                weight_ref[expert, n : n + 256, :],
                LAST,
                preferred_element_type=F32,
            )
            out_ref[:, n : n + 256] = value.astype(BF16)


def hidden_part(info, blocks, down_weight, tiles, capacity, steps):
    local_count, hidden_units, cols = down_weight.shape
    flat, halves = [], []
    for block in blocks:
        pair = isinstance(block, tuple)
        flat += list(block) if pair else [block]
        halves += [pair, pair] if pair else [False]
    count = len(blocks)
    shape = (count * capacity, hidden_units)
    return call(
        functools.partial(hidden_kernel, halves, tiles, capacity, steps),
        10,
        [jax.ShapeDtypeStruct(shape, BF16)] * len(steps)
        + [jax.ShapeDtypeStruct((8 * count, 128), F32)] * (1 in steps),
        [pltpu.VMEM((2, count * capacity, cols), BF16)],
        1,
    )(info, *flat, down_weight)


def grad_kernel(counts, chunk, split, tiles, capacity, info_ref, *refs):
    groups = len(counts)
    total = sum(counts)
    hidden_refs = refs[: 3 * groups]
    gate_ref, up_ref, gate_w_ref, up_w_ref = refs[3 * groups : 3 * groups + 4]
    out_refs = refs[3 * groups + 4 : -2]
    dgate_ref, dup_ref = refs[-2:]
    core, tile, row = info_ref[0], info_ref[1], info_ref[2]
    rows = 128
    cols = gate_w_ref.shape[1]
    line = lax.broadcasted_iota(jnp.int32, (8, rows), 0)
    slot_at = lax.broadcasted_iota(jnp.int32, (capacity, rows), 0).astype(F32)
    combine, scores = [], []
    b = 0
    for g in range(groups):
        full_ref, pair_ref, meta_ref = hidden_refs[3 * g : 3 * g + 3]
        for i in range(counts[g]):
            span = slice(i * capacity, (i + 1) * capacity)
            store = slice(b * capacity, (b + 1) * capacity)
            saved = pl.ds(pl.multiple_of(info_ref[INFO_BLOCKS + chunk[b]] * capacity, capacity), capacity)
            lines = meta_ref[8 * i : 8 * i + 8, :]
            score_rows = jnp.zeros((8, rows), F32)
            stacked = []
            for e in range(2):
                hidden = jnp.where(core == e, full_ref[span, :], pair_ref[span, :]).astype(F32)
                gate = gate_ref[e, saved, :].astype(F32)
                up = up_ref[e, saved, :].astype(F32)
                active, slope_term = silu_parts(gate)
                dup = hidden * active
                match = slot_at == lines[e : e + 1, :]
                weight = jnp.sum(
                    jnp.where(match, lines[2 + e : 3 + e, :], 0.0), axis=1, keepdims=True
                )
                dgate_ref[e, store, :] = (hidden * up * slope_term * weight).astype(BF16)
                dup_ref[e, store, :] = (dup * weight).astype(BF16)
                score = jnp.sum(up * dup.astype(BF16).astype(F32), axis=1, keepdims=True)
                score = score.astype(BF16).astype(F32)
                token_score = jnp.sum(jnp.where(match, score, 0.0), axis=0, keepdims=True)
                score_rows = score_rows + jnp.where(line == row + e, token_score, 0.0)
                stacked.append(jnp.where(match, 1.0, 0.0).astype(BF16))
            combine.append(jnp.concatenate(stacked, axis=0))
            scores.append(score_rows)
            b += 1
    for n in range(0, cols, 1280):
        grads = []
        for e in range(2):
            value = lax.dot_general(
                dgate_ref[e], gate_w_ref[e, n : n + 1280, :], LAST, preferred_element_type=F32
            )
            value = value + lax.dot_general(
                dup_ref[e], up_w_ref[e, n : n + 1280, :], LAST, preferred_element_type=F32
            )
            grads.append(value.astype(BF16))
        for b in range(total):
            span = slice(b * capacity, (b + 1) * capacity)
            pile = jnp.concatenate([g[span] for g in grads], axis=0)
            value = lax.dot_general(combine[b], pile, FIRST, preferred_element_type=F32)
            if n == 0:
                lanes = [jnp.where(tile == i, scores[b], 0.0) for i in range(tiles)]
                lanes = jnp.concatenate(lanes + [jnp.zeros((8, 1280 - tiles * rows), F32)], axis=1)
            else:
                lanes = jnp.zeros((8, 1280), F32)
            if split:
                out_refs[2 * b][:, n : n + 1280] = value[:TOP_ROWS].astype(BF16)
                low = jnp.concatenate([value[TOP_ROWS:], lanes], axis=0)
                out_refs[2 * b + 1][:, n : n + 1280] = low.astype(BF16)
            else:
                out_refs[b][:, n : n + 1280] = jnp.concatenate([value, lanes], axis=0).astype(BF16)


def grad_part(info, parts, saved, weights, counts, chunk, split, tiles, capacity):
    local_count, cols, hidden_units = weights[0].shape
    total = sum(counts)
    heights = [TOP_ROWS, 136 - TOP_ROWS] * total if split else [136] * total
    return call(
        functools.partial(grad_kernel, counts, chunk, split, tiles, capacity),
        14,
        [jax.ShapeDtypeStruct((h, cols), BF16) for h in heights],
        [
            pltpu.VMEM((2, total * capacity, hidden_units), BF16),
            pltpu.VMEM((2, total * capacity, hidden_units), BF16),
        ],
        1,
    )(info, *parts, *saved, *weights)


def shared_spans(info_ref, cols):
    here = info_ref[3]
    return [
        pl.ds(pl.multiple_of(jnp.bitwise_xor(here, q) * cols, cols), cols) for q in range(4)
    ]


def shared_inner_kernel(info_ref, *refs):
    token_refs, (gate_ref, up_ref, active_ref, slope_ref) = refs[0:4], refs[4:]
    rows, cols = token_refs[0].shape
    units = gate_ref.shape[1]
    spans = shared_spans(info_ref, cols)
    gate_pre = jnp.zeros((rows, units), F32)
    up_pre = jnp.zeros((rows, units), F32)
    for q in range(4):
        token = token_refs[q][...]
        gate_pre = gate_pre + jnp.dot(token, gate_ref[spans[q], :], preferred_element_type=F32)
        up_pre = up_pre + jnp.dot(token, up_ref[spans[q], :], preferred_element_type=F32)
    active, slope_term = silu_parts(gate_pre)
    active_ref[...] = active
    slope_ref[...] = up_pre * slope_term


def shared_inner(info, token_blocks, shared_gate, shared_up):
    shape = jax.ShapeDtypeStruct((token_blocks[0].shape[0], shared_gate.shape[1]), F32)
    return call(shared_inner_kernel, 8, [shape, shape], (), 1)(
        info, *token_blocks, shared_gate, shared_up
    )


def shared_slopes_kernel(info_ref, *refs):
    grad_refs, (down_ref, active_ref, slope_ref, dgate_ref, dup_ref) = refs[0:4], refs[4:]
    rows, cols = grad_refs[0].shape
    spans = shared_spans(info_ref, cols)
    hidden_pre = jnp.zeros((rows, down_ref.shape[0]), F32)
    for q in range(4):
        hidden_pre = hidden_pre + lax.dot_general(
            grad_refs[q][...], down_ref[:, spans[q]], LAST, preferred_element_type=F32
        )
    dgate_ref[...] = (hidden_pre * slope_ref[...]).astype(BF16)
    dup_ref[...] = (hidden_pre * active_ref[...]).astype(BF16)


def shared_slopes(info, grad_blocks, shared_down, active, slope):
    shape = jax.ShapeDtypeStruct(active.shape, BF16)
    return call(shared_slopes_kernel, 8, [shape, shape], (), 1)(
        info, *grad_blocks, shared_down, active, slope
    )


def shared_terms_kernel(info_ref, dgate_ref, dup_ref, gate_ref, up_ref, *out_refs):
    cols = out_refs[0].shape[1]
    spans = shared_spans(info_ref, cols)
    dgate, dup = dgate_ref[...], dup_ref[...]
    for q in range(4):
        term = lax.dot_general(dgate, gate_ref[spans[q], :], LAST, preferred_element_type=F32)
        term = term + lax.dot_general(dup, up_ref[spans[q], :], LAST, preferred_element_type=F32)
        out_refs[q][...] = term.astype(BF16)


def shared_terms(info, dgate, dup, shared_gate, shared_up, cols):
    shape = jax.ShapeDtypeStruct((dgate.shape[0], cols), BF16)
    return call(shared_terms_kernel, 8, [shape] * 4, (), 1)(
        info, dgate, dup, shared_gate, shared_up
    )


def ring_place(position):
    position = position % 8
    return jnp.where(position < 4, 2 * position, 15 - 2 * position)


def per_device_ring(
    tokens,
    out_grad,
    expert_ids,
    router_probs,
    router_weight,
    gate_weight,
    up_weight,
    down_weight,
    gate_saved,
    up_saved,
    shared_gate,
    shared_up,
    shared_down,
):
    slot_count = gate_saved.shape[1]
    capacity = slot_count // 8
    rows, cols = tokens.shape
    expert_total = router_probs.shape[1]
    tiles = expert_total // 8
    order = [0, 2, 4, 6, 7, 5, 3, 1]
    ahead = [(order[i], order[(i + 1) % 8]) for i in range(8)]
    behind = [(order[i], order[(i - 1) % 8]) for i in range(8)]
    x_pairs = [(i, i ^ 2) for i in range(4)]
    core_pairs = [(i, i ^ 1) for i in range(4)]
    me = lax.axis_index("expert")
    place = jnp.where(me % 2 == 0, me // 2, 7 - me // 2)
    here = lax.axis_index("tensor")
    first = me * 2
    base = [here % 2, first // 8, first % 8]
    tie = lax.optimization_barrier

    def swap_x(a):
        return lax.ppermute(a, "tensor", x_pairs)

    def swap_core(a):
        return lax.ppermute(a, "tensor", core_pairs)

    def ring(fore, back):
        return lax.ppermute(fore, "expert", ahead), lax.ppermute(back, "expert", behind)

    def hidden(blocks, steps=(0, 1)):
        return hidden_part(info, blocks, down_weight, tiles, capacity, steps)

    def grads(saved, weights, *parts):
        chunk = sum((part[0] for part in parts), ())
        return grad_part(
            info,
            [a for part in parts for a in part[1:]],
            saved,
            weights,
            [len(part[0]) for part in parts],
            chunk,
            chunk == (4,),
            tiles,
            capacity,
        )

    numbers = base + [here] + [ring_place(place + d) for d in range(-3, 5)]
    info = jnp.stack([jnp.asarray(n, jnp.int32) for n in numbers])
    payload, meta = payload_of(expert_ids.T, router_probs.T, out_grad, capacity)

    fore, back = ring(out_grad, out_grad)
    meta_f, meta_b = ring(meta, meta)
    grad_x = swap_x(out_grad)
    fore, back, grad_x, meta_f, meta_b, info = tie((fore, back, grad_x, meta_f, meta_b, info))
    fore1, back1 = attach(fore, meta_f, back, meta_b)

    fore, back = ring(fore1, back1)
    tok_x = swap_x(tokens)
    other1, mine1, meta1 = hidden([payload, fore1, back1])
    fore2, back2, other1, mine1, tok_x = tie((fore, back, other1, mine1, tok_x))

    fore, back = ring(fore2, back2)
    (chip1,) = sums((mine1, swap_core(other1)))
    far1 = swap_x(chip1)
    other2, mine2, meta2 = hidden([fore2, back2])
    (chip2,) = sums((mine2, swap_core(other2)))
    tok_core, grad_core = swap_core(tokens), swap_core(out_grad)
    fore3, back3, chip1, chip2, tok_core, grad_core = tie(
        (fore, back, chip1, chip2, tok_core, grad_core)
    )

    top, bottom = ring(*halves_of(fore3, back3))
    far2 = swap_x(chip2)
    other3, mine3, meta3 = hidden([fore3, back3])
    tok_both = swap_core(tok_x)
    top, bottom, chip2, other3, mine3, far1, far2, tok_both = tie(
        (top, bottom, chip2, other3, mine3, far1, far2, tok_both)
    )

    (other4,) = hidden([(top, bottom)], (0,))
    top, bottom, other4, other3 = tie((top, bottom, other4, other3))
    swapped4 = swap_core(other4)
    mine4, meta4 = hidden([(top, bottom)], (1,))
    swapped3 = swap_core(other3)
    (chip4,) = sums((mine4, swapped4))
    chip4, chip1, far1 = tie((chip4, chip1, far1))
    far4 = swap_x(chip4)
    (full1,) = sums((chip1, far1))
    full1, swapped3, mine3 = tie((full1, swapped3, mine3))
    (chip3,) = sums((mine3, swapped3))
    far3 = swap_x(chip3)
    chip3, tok_in, full1 = tie((chip3, tokens, full1))
    pair1 = swap_core(full1)
    active, slope = shared_inner(
        info, [tok_in, tok_core, tok_x, tok_both], shared_gate, shared_up
    )
    active, slope, chip2, far2 = tie((active, slope, chip2, far2))
    (full2,) = sums((chip2, far2))
    pair2 = swap_core(full2)
    far4, full2, active, pair1 = tie((far4, full2, active, pair1))
    (full4,) = sums((chip4, far4))
    pair4 = swap_core(full4)
    saved = (gate_saved, up_saved)
    weights = (gate_weight, up_weight)
    top, bottom = grads(saved, weights, ((4,), full4, pair4, meta4))

    top, bottom, pair2, full2, far3 = tie((top, bottom, pair2, full2, far3))
    fore, back = ring(top, bottom)
    (full3,) = sums((chip3, far3))
    pair3 = swap_core(full3)
    near_b3, near_f3, near_b2, near_f2 = grads(
        saved, weights, ((-3, 3), full3, pair3, meta3), ((-2, 2), full2, pair2, meta2)
    )
    fore, back, near_f3, near_b3, near_f2, near_b2, full1, pair1, grad_in = tie(
        (fore, back, near_f3, near_b3, near_f2, near_b2, full1, pair1, out_grad)
    )

    fore, back = join(near_f3, fore, near_b3, back)
    fore, back = ring(fore, back)
    near0, near_b1, near_f1 = grads(saved, weights, ((0, -1, 1), full1, pair1, meta1))
    grad_both = swap_core(grad_x)
    dgate, dup = shared_slopes(
        info, [grad_in, grad_core, grad_x, grad_both], shared_down, active, slope
    )
    fore, back, near0, near_b1, near_f1, dgate, dup = tie(
        (fore, back, near0, near_b1, near_f1, dgate, dup)
    )

    fore, back = sums((near_f2, fore), (near_b2, back))
    fore, back = ring(fore, back)
    terms = shared_terms(info, dgate, dup, shared_gate, shared_up, cols)
    swapped, near = swap_core(terms[3]), swap_core(terms[1])
    fore, back, swapped, near = tie((fore, back, swapped, near))

    fore, back, far = sums((near_f1, fore), (near_b1, back), (terms[2], swapped))
    fore, back = ring(fore, back)
    shared_far = swap_x(far)
    total = near0.astype(F32) + fore.astype(F32) + back.astype(F32)
    shared_part = terms[0].astype(F32) + near.astype(F32) + shared_far.astype(F32)
    prob_grad = jnp.concatenate(
        [total[rows:, i * rows : (i + 1) * rows] for i in range(tiles)], axis=0
    ).T
    gate_total = jnp.sum(router_probs * prob_grad, axis=1, keepdims=True)
    logit_grad = (router_probs * (prob_grad - gate_total)).astype(BF16)
    router_part = jnp.einsum("te,de->td", logit_grad, router_weight, preferred_element_type=F32)
    return (shared_part + total[:rows] + router_part).astype(BF16)


def per_device(*args):
    tokens, router_probs, gate_weight, gate_saved = args[0], args[3], args[5], args[8]
    rows, cols = tokens.shape
    expert_total = router_probs.shape[1]
    ring = (
        lax.axis_size("expert") == 8
        and lax.axis_size("tensor") == 4
        and gate_weight.shape[0] == 2
        and gate_saved.shape[1] == 8 * 64
        and gate_saved.shape[2] % 256 == 0
        and rows == 128
        and expert_total == 16
        and cols % 256 == 0
        and cols >= 6 * rows
    )
    return (per_device_ring if ring else per_device_wide)(*args)


def solution(mesh):

    return jax.shard_map(
        per_device,
        mesh=mesh,
        in_specs=(
            P("expert", "tensor"),
            P("expert", "tensor"),
            P("expert", None),
            P("expert", None),
            P("tensor", None),
            P("expert", "tensor", None),
            P("expert", "tensor", None),
            P("expert", None, "tensor"),
            P("expert", None, None),
            P("expert", None, None),
            P(None, "tensor"),
            P(None, "tensor"),
            P("tensor", None),
        ),
        out_specs=P("expert", "tensor"),
        check_vma=False,
    )
```

```python
import functools

import jax
import jax.numpy as jnp
from jax import lax
from jax.experimental import pallas as pl
from jax.experimental.pallas import tpu as pltpu
from jax.sharding import PartitionSpec as P


def silu_parts(preact):
    sigmoid_value = jax.nn.sigmoid(preact)
    return (preact * sigmoid_value, sigmoid_value * (1.0 + preact * (1.0 - sigmoid_value)))


def per_device_wide(
    tokens,
    out_grad,
    expert_ids,
    router_probs,
    router_weight,
    gate_weight,
    up_weight,
    down_weight,
    gate_saved,
    up_saved,
    shared_gate,
    shared_up,
    shared_down,
):
    groups = lax.axis_size("expert")
    local_count, slot_count, hidden_units = gate_saved.shape
    capacity = slot_count // groups
    token_rows, route_width = expert_ids.shape
    expert_total = router_probs.shape[1]
    feature_cols = tokens.shape[1]
    column_total = local_count * groups * capacity
    flat_ids = expert_ids.reshape(-1)
    onehot = (flat_ids[:, None] == jnp.arange(expert_total, dtype=jnp.int32)[None, :]).astype(
        jnp.int32
    )
    slot_index = jnp.sum((jnp.cumsum(onehot, axis=0) - onehot) * onehot, axis=1)
    kept_mask = slot_index < capacity
    owner_group = flat_ids // local_count
    local_expert = flat_ids % local_count
    column_id = jnp.where(
        kept_mask, local_expert * (groups * capacity) + owner_group * capacity + slot_index, -1
    )
    column_grid = column_id.reshape(token_rows, route_width)
    column_match = (
        column_grid[:, :, None] == jnp.arange(column_total, dtype=jnp.int32)[None, None, :]
    )
    placement = jnp.sum(column_match.astype(jnp.float32), axis=1).astype(jnp.bfloat16)
    sectioning = jnp.einsum(
        "tc,td->cd", placement, out_grad, preferred_element_type=jnp.float32
    ).astype(jnp.bfloat16)
    outgoing = sectioning.reshape(local_count, groups, capacity * feature_cols)
    token_piece = lax.all_gather(tokens, "tensor", axis=1, tiled=True)
    grad_piece = lax.all_gather(out_grad, "tensor", axis=1, tiled=True)
    gate_pre = jnp.dot(token_piece, shared_gate, preferred_element_type=jnp.float32)
    up_pre = jnp.dot(token_piece, shared_up, preferred_element_type=jnp.float32)
    hidden_pre = jnp.einsum(
        "tc,fc->tf", grad_piece, shared_down, preferred_element_type=jnp.float32
    )
    active, slope_term = silu_parts(gate_pre)
    shared_dgate = (hidden_pre * up_pre * slope_term).astype(jnp.bfloat16)
    shared_dup = (hidden_pre * active).astype(jnp.bfloat16)
    shared_term = jnp.einsum(
        "tf,df->td", shared_dgate, shared_gate, preferred_element_type=jnp.float32
    ) + jnp.einsum("tf,df->td", shared_dup, shared_up, preferred_element_type=jnp.float32)
    shared_part = lax.psum_scatter(
        shared_term.astype(jnp.bfloat16), "tensor", scatter_dimension=1, tiled=True
    ).astype(jnp.float32)
    arrived = lax.all_to_all(outgoing, "expert", split_axis=1, concat_axis=1, tiled=True)
    arrived = arrived.reshape(local_count, slot_count, feature_cols)
    partial_hidden = jnp.einsum(
        "esd,efd->esf", arrived, down_weight, preferred_element_type=jnp.float32
    )
    up_full = up_saved.astype(jnp.float32)
    hidden_grad = lax.psum(partial_hidden.astype(jnp.bfloat16), "tensor").astype(jnp.float32)
    active, slope_term = silu_parts(gate_saved.astype(jnp.float32))
    d_gate = (hidden_grad * up_full * slope_term).astype(jnp.bfloat16)
    d_up = (hidden_grad * active).astype(jnp.bfloat16)
    score_rows = jnp.sum(up_full * d_up.astype(jnp.float32), axis=2).astype(jnp.bfloat16)
    expert_grad = jnp.einsum(
        "esf,edf->esd", d_gate, gate_weight, preferred_element_type=jnp.float32
    ) + jnp.einsum("esf,edf->esd", d_up, up_weight, preferred_element_type=jnp.float32)
    expert_grad = expert_grad.astype(jnp.bfloat16)
    back_grad, back_score = (
        lax.all_to_all(
            expert_grad.reshape(local_count, groups, capacity * feature_cols),
            "expert",
            split_axis=1,
            concat_axis=1,
            tiled=True,
        ),
        lax.all_to_all(
            score_rows.reshape(local_count, groups, capacity),
            "expert",
            split_axis=1,
            concat_axis=1,
            tiled=True,
        ),
    )
    returned_rows = back_grad.reshape(column_total, feature_cols)
    returned_scores = back_score.reshape(column_total).astype(jnp.float32)
    kept_value = kept_mask.astype(jnp.float32)
    probs_rows = jnp.repeat(router_probs, route_width, axis=0)
    onehot_float = onehot.astype(jnp.float32)
    gate_value = jnp.sum(onehot_float * probs_rows, axis=1)
    route_weight = (gate_value * kept_value).reshape(token_rows, route_width)
    combine_weight = jnp.sum(jnp.where(column_match, route_weight[:, :, None], 0.0), axis=1)
    routed_part = jnp.dot(
        combine_weight,
        returned_rows.astype(jnp.float32),
        precision=lax.Precision.HIGHEST,
        preferred_element_type=jnp.float32,
    )
    safe_column = jnp.maximum(column_id, 0)
    route_score = returned_scores[safe_column] * kept_value
    prob_grad = jnp.sum(
        (onehot_float * route_score[:, None]).reshape(token_rows, route_width, expert_total), axis=1
    )
    gate_total = jnp.sum((gate_value * route_score).reshape(token_rows, route_width), axis=1)
    logit_grad = (router_probs * (prob_grad - gate_total[:, None])).astype(jnp.bfloat16)
    router_part = jnp.einsum(
        "te,de->td", logit_grad, router_weight, preferred_element_type=jnp.float32
    )
    return (shared_part + routed_part + router_part).astype(jnp.bfloat16)


F32, BF16 = jnp.float32, jnp.bfloat16
LAST = (((1,), (1,)), ((), ()))
FIRST = (((0,), (0,)), ((), ()))
TOP_ROWS = 64
INFO_BLOCKS = 7


def call(kernel, megabytes, out_shape, scratch_shapes=(), scalars=0, far=0):
    def run(*operands):
        near = len(operands) - scalars - far
        memory = [pltpu.SMEM] * scalars + [pltpu.VMEM] * near + [pl.ANY] * far
        return pl.pallas_call(
            kernel,
            in_specs=[pl.BlockSpec(memory_space=m) for m in memory],
            out_specs=jax.tree.map(lambda _: pl.BlockSpec(memory_space=pltpu.VMEM), out_shape),
            out_shape=out_shape,
            scratch_shapes=scratch_shapes,
            compiler_params=pltpu.CompilerParams(vmem_limit_bytes=megabytes * 1024 * 1024),
            cost_estimate=pl.CostEstimate(flops=1000, bytes_accessed=1000, transcendentals=0),
        )(*operands)

    return run


def sum_kernel(groups, *refs):
    count = sum(groups)
    at = 0
    for out_ref, size in zip(refs[count:], groups):
        total = refs[at][...].astype(F32)
        for ref in refs[at + 1 : at + size]:
            total = total + ref[...].astype(F32)
        out_ref[...] = total.astype(BF16)
        at += size


def sums(*groups):
    return call(
        functools.partial(sum_kernel, [len(g) for g in groups]),
        2,
        [jax.ShapeDtypeStruct(g[0].shape, BF16) for g in groups],
    )(*[a for g in groups for a in g])


def halves_kernel(fore_ref, back_ref, top_ref, bottom_ref):
    top_ref[...] = fore_ref[0:TOP_ROWS, :]
    bottom_ref[...] = back_ref[TOP_ROWS:, :]


def halves_of(fore, back):
    rows, cols = fore.shape
    return call(
        halves_kernel,
        2,
        [
            jax.ShapeDtypeStruct((TOP_ROWS, cols), BF16),
            jax.ShapeDtypeStruct((rows - TOP_ROWS, cols), BF16),
        ],
    )(fore, back)


def join_kernel(near_f_ref, top_ref, near_b_ref, bottom_ref, fore_ref, back_ref):
    top = near_f_ref[0:TOP_ROWS, :].astype(F32) + top_ref[...].astype(F32)
    fore_ref[0:TOP_ROWS, :] = top.astype(BF16)
    fore_ref[TOP_ROWS:, :] = near_f_ref[TOP_ROWS:, :]
    back_ref[0:TOP_ROWS, :] = near_b_ref[0:TOP_ROWS, :]
    bottom = near_b_ref[TOP_ROWS:, :].astype(F32) + bottom_ref[...].astype(F32)
    back_ref[TOP_ROWS:, :] = bottom.astype(BF16)


def join(near_f, top, near_b, bottom):
    shape = jax.ShapeDtypeStruct(near_f.shape, BF16)
    return call(join_kernel, 2, [shape, shape])(near_f, top, near_b, bottom)


def attach_kernel(fore_ref, meta_f_ref, back_ref, meta_b_ref, fore_out, back_out):
    rows = fore_ref.shape[0]
    for ref, meta_ref, out_ref in (
        (fore_ref, meta_f_ref, fore_out),
        (back_ref, meta_b_ref, back_out),
    ):
        out_ref[0:rows, :] = ref[...]
        out_ref[rows:, :] = meta_ref[...]


def attach(fore, meta_f, back, meta_b):
    rows, cols = fore.shape
    shape = jax.ShapeDtypeStruct((rows + 8, cols), BF16)
    return call(attach_kernel, 2, [shape, shape])(fore, meta_f, back, meta_b)


def payload_kernel(
    capacity, ids_hbm, probs_hbm, grad_hbm, out_ref, meta_ref, ids_ref, probs_ref, sems
):
    expert_total, rows = probs_ref.shape
    cols = grad_hbm.shape[1]
    copies = [
        pltpu.make_async_copy(ids_hbm, ids_ref, sems.at[0]),
        pltpu.make_async_copy(probs_hbm, probs_ref, sems.at[1]),
        pltpu.make_async_copy(grad_hbm, out_ref.at[0:rows, :], sems.at[2]),
    ]
    for copy in copies:
        copy.start()
    experts = lax.broadcasted_iota(jnp.int32, (expert_total, rows), 0)
    row_at = lax.broadcasted_iota(jnp.int32, (rows, rows), 0)
    col_at = lax.broadcasted_iota(jnp.int32, (rows, rows), 1)
    lower = jnp.where(row_at < col_at, 1.0, 0.0).astype(BF16)
    copies[0].wait()
    ids = ids_ref[...]
    member = jnp.zeros((expert_total, rows), F32)
    for k in range(ids.shape[0]):
        member = member + jnp.where(ids[k : k + 1, :] == experts, 1.0, 0.0)
    before = jnp.dot(member.astype(BF16), lower, preferred_element_type=F32)
    slot = jnp.where((member > 0.5) & (before < capacity), before, -1.0)
    copies[1].wait()
    probs = probs_ref[...]
    high = probs.astype(BF16).astype(F32)
    parts = [slot, high, probs - high]
    pieces = [a[8 * i : 8 * i + 8] for a in parts for i in range(expert_total // 8)]
    pieces.append(jnp.zeros((8, cols - len(pieces) * rows), F32))
    meta = jnp.concatenate(pieces, axis=1).astype(BF16)
    out_ref[rows : rows + 8, :] = meta
    meta_ref[...] = meta
    copies[2].wait()


def payload_of(ids_t, probs_t, grad, capacity):
    rows, cols = grad.shape
    return call(
        functools.partial(payload_kernel, capacity),
        60,
        [
            jax.ShapeDtypeStruct((rows + 8, cols), BF16),
            jax.ShapeDtypeStruct((8, cols), BF16),
        ],
        [
            pltpu.VMEM(ids_t.shape, jnp.int32),
            pltpu.VMEM(probs_t.shape, F32),
            pltpu.SemaphoreType.DMA((3,)),
        ],
        0,
        3,
    )(ids_t, probs_t, grad)


def hidden_kernel(halves, tiles, capacity, steps, info_ref, *refs):
    block_refs = refs[: len(halves)]
    weight_ref, placed_ref = refs[len(halves)], refs[-1]
    out_refs = refs[len(halves) + 1 : -1]
    core, tile, row = info_ref[0], info_ref[1], info_ref[2]
    blocks, at = [], 0
    while at < len(halves):
        size = 2 if halves[at] else 1
        blocks.append(block_refs[at : at + size])
        at += size
    rows = 128
    units = weight_ref.shape[1]

    def pick(meta, kind, which):
        value = meta[:, kind * tiles * rows : (kind * tiles + 1) * rows]
        for i in range(1, tiles):
            at_lane = (kind * tiles + i) * rows
            value = jnp.where(tile == i, meta[:, at_lane : at_lane + rows], value)
        line = lax.broadcasted_iota(jnp.int32, (8, rows), 0)
        return jnp.sum(jnp.where(line == which, value, 0.0), axis=0, keepdims=True)

    slot_at = lax.broadcasted_iota(jnp.int32, (capacity, rows), 0).astype(F32)
    for step in steps:
        expert = 1 - core if step == 0 else core
        for b, block in enumerate(blocks):
            last = block[-1]
            meta = last[last.shape[0] - 8 :, :].astype(F32)
            match = jnp.where(slot_at == pick(meta, 0, row + expert), 1.0, 0.0).astype(BF16)
            if len(block) == 1:
                data = block[0][0:rows, :]
            else:
                data = jnp.concatenate([block[0][...], block[1][0 : rows - TOP_ROWS, :]], axis=0)
            placed = jnp.dot(match, data, preferred_element_type=F32)
            placed_ref[step, b * capacity : (b + 1) * capacity, :] = placed.astype(BF16)
            if step == 1:
                lines = [pick(meta, 0, row), pick(meta, 0, row + 1)]
                lines += [pick(meta, 1, row) + pick(meta, 2, row)]
                lines += [pick(meta, 1, row + 1) + pick(meta, 2, row + 1)]
                lines += [jnp.zeros((4, rows), F32)]
                out_refs[-1][8 * b : 8 * b + 8, :] = jnp.concatenate(lines, axis=0)
        out_ref = out_refs[steps.index(step)]
        for n in range(0, units, 256):
            value = lax.dot_general(
                placed_ref[step],
                weight_ref[expert, n : n + 256, :],
                LAST,
                preferred_element_type=F32,
            )
            out_ref[:, n : n + 256] = value.astype(BF16)


def hidden_part(info, blocks, down_weight, tiles, capacity, steps):
    local_count, hidden_units, cols = down_weight.shape
    flat, halves = [], []
    for block in blocks:
        pair = isinstance(block, tuple)
        flat += list(block) if pair else [block]
        halves += [pair, pair] if pair else [False]
    count = len(blocks)
    shape = (count * capacity, hidden_units)
    return call(
        functools.partial(hidden_kernel, halves, tiles, capacity, steps),
        10,
        [jax.ShapeDtypeStruct(shape, BF16)] * len(steps)
        + [jax.ShapeDtypeStruct((8 * count, 128), F32)] * (1 in steps),
        [pltpu.VMEM((2, count * capacity, cols), BF16)],
        1,
    )(info, *flat, down_weight)


def grad_kernel(counts, chunk, split, tiles, capacity, info_ref, *refs):
    groups = len(counts)
    total = sum(counts)
    hidden_refs = refs[: 3 * groups]
    gate_ref, up_ref, gate_w_ref, up_w_ref = refs[3 * groups : 3 * groups + 4]
    out_refs = refs[3 * groups + 4 : -2]
    dgate_ref, dup_ref = refs[-2:]
    core, tile, row = info_ref[0], info_ref[1], info_ref[2]
    rows = 128
    cols = gate_w_ref.shape[1]
    line = lax.broadcasted_iota(jnp.int32, (8, rows), 0)
    slot_at = lax.broadcasted_iota(jnp.int32, (capacity, rows), 0).astype(F32)
    combine, scores = [], []
    b = 0
    for g in range(groups):
        full_ref, pair_ref, meta_ref = hidden_refs[3 * g : 3 * g + 3]
        for i in range(counts[g]):
            span = slice(i * capacity, (i + 1) * capacity)
            store = slice(b * capacity, (b + 1) * capacity)
            saved = pl.ds(pl.multiple_of(info_ref[INFO_BLOCKS + chunk[b]] * capacity, capacity), capacity)
            lines = meta_ref[8 * i : 8 * i + 8, :]
            score_rows = jnp.zeros((8, rows), F32)
            stacked = []
            for e in range(2):
                hidden = jnp.where(core == e, full_ref[span, :], pair_ref[span, :]).astype(F32)
                gate = gate_ref[e, saved, :].astype(F32)
                up = up_ref[e, saved, :].astype(F32)
                active, slope_term = silu_parts(gate)
                dup = hidden * active
                match = slot_at == lines[e : e + 1, :]
                weight = jnp.sum(
                    jnp.where(match, lines[2 + e : 3 + e, :], 0.0), axis=1, keepdims=True
                )
                dgate_ref[e, store, :] = (hidden * up * slope_term * weight).astype(BF16)
                dup_ref[e, store, :] = (dup * weight).astype(BF16)
                score = jnp.sum(up * dup.astype(BF16).astype(F32), axis=1, keepdims=True)
                score = score.astype(BF16).astype(F32)
                token_score = jnp.sum(jnp.where(match, score, 0.0), axis=0, keepdims=True)
                score_rows = score_rows + jnp.where(line == row + e, token_score, 0.0)
                stacked.append(jnp.where(match, 1.0, 0.0).astype(BF16))
            combine.append(jnp.concatenate(stacked, axis=0))
            scores.append(score_rows)
            b += 1
    for n in range(0, cols, 1280):
        grads = []
        for e in range(2):
            value = lax.dot_general(
                dgate_ref[e], gate_w_ref[e, n : n + 1280, :], LAST, preferred_element_type=F32
            )
            value = value + lax.dot_general(
                dup_ref[e], up_w_ref[e, n : n + 1280, :], LAST, preferred_element_type=F32
            )
            grads.append(value.astype(BF16))
        for b in range(total):
            span = slice(b * capacity, (b + 1) * capacity)
            pile = jnp.concatenate([g[span] for g in grads], axis=0)
            value = lax.dot_general(combine[b], pile, FIRST, preferred_element_type=F32)
            if n == 0:
                lanes = [jnp.where(tile == i, scores[b], 0.0) for i in range(tiles)]
                lanes = jnp.concatenate(lanes + [jnp.zeros((8, 1280 - tiles * rows), F32)], axis=1)
            else:
                lanes = jnp.zeros((8, 1280), F32)
            if split:
                out_refs[2 * b][:, n : n + 1280] = value[:TOP_ROWS].astype(BF16)
                low = jnp.concatenate([value[TOP_ROWS:], lanes], axis=0)
                out_refs[2 * b + 1][:, n : n + 1280] = low.astype(BF16)
            else:
                out_refs[b][:, n : n + 1280] = jnp.concatenate([value, lanes], axis=0).astype(BF16)


def grad_part(info, parts, saved, weights, counts, chunk, split, tiles, capacity):
    local_count, cols, hidden_units = weights[0].shape
    total = sum(counts)
    heights = [TOP_ROWS, 136 - TOP_ROWS] * total if split else [136] * total
    return call(
        functools.partial(grad_kernel, counts, chunk, split, tiles, capacity),
        14,
        [jax.ShapeDtypeStruct((h, cols), BF16) for h in heights],
        [
            pltpu.VMEM((2, total * capacity, hidden_units), BF16),
            pltpu.VMEM((2, total * capacity, hidden_units), BF16),
        ],
        1,
    )(info, *parts, *saved, *weights)


def shared_spans(info_ref, cols):
    here = info_ref[3]
    return [
        pl.ds(pl.multiple_of(jnp.bitwise_xor(here, q) * cols, cols), cols) for q in range(4)
    ]


def shared_inner_kernel(info_ref, *refs):
    token_refs, (gate_ref, up_ref, active_ref, slope_ref) = refs[0:4], refs[4:]
    rows, cols = token_refs[0].shape
    units = gate_ref.shape[1]
    spans = shared_spans(info_ref, cols)
    gate_pre = jnp.zeros((rows, units), F32)
    up_pre = jnp.zeros((rows, units), F32)
    for q in range(4):
        token = token_refs[q][...]
        gate_pre = gate_pre + jnp.dot(token, gate_ref[spans[q], :], preferred_element_type=F32)
        up_pre = up_pre + jnp.dot(token, up_ref[spans[q], :], preferred_element_type=F32)
    active, slope_term = silu_parts(gate_pre)
    active_ref[...] = active
    slope_ref[...] = up_pre * slope_term


def shared_inner(info, token_blocks, shared_gate, shared_up):
    shape = jax.ShapeDtypeStruct((token_blocks[0].shape[0], shared_gate.shape[1]), F32)
    return call(shared_inner_kernel, 8, [shape, shape], (), 1)(
        info, *token_blocks, shared_gate, shared_up
    )


def shared_slopes_kernel(info_ref, *refs):
    grad_refs, (down_ref, active_ref, slope_ref, dgate_ref, dup_ref) = refs[0:4], refs[4:]
    rows, cols = grad_refs[0].shape
    spans = shared_spans(info_ref, cols)
    hidden_pre = jnp.zeros((rows, down_ref.shape[0]), F32)
    for q in range(4):
        hidden_pre = hidden_pre + lax.dot_general(
            grad_refs[q][...], down_ref[:, spans[q]], LAST, preferred_element_type=F32
        )
    dgate_ref[...] = (hidden_pre * slope_ref[...]).astype(BF16)
    dup_ref[...] = (hidden_pre * active_ref[...]).astype(BF16)


def shared_slopes(info, grad_blocks, shared_down, active, slope):
    shape = jax.ShapeDtypeStruct(active.shape, BF16)
    return call(shared_slopes_kernel, 8, [shape, shape], (), 1)(
        info, *grad_blocks, shared_down, active, slope
    )


def shared_terms_kernel(which, info_ref, dgate_ref, dup_ref, gate_ref, up_ref, *out_refs):
    cols = out_refs[0].shape[1]
    spans = shared_spans(info_ref, cols)
    dgate, dup = dgate_ref[...], dup_ref[...]
    for out_ref, q in zip(out_refs, which):
        term = lax.dot_general(dgate, gate_ref[spans[q], :], LAST, preferred_element_type=F32)
        term = term + lax.dot_general(dup, up_ref[spans[q], :], LAST, preferred_element_type=F32)
        out_ref[...] = term.astype(BF16)


def shared_terms(info, dgate, dup, shared_gate, shared_up, cols, which):
    shape = jax.ShapeDtypeStruct((dgate.shape[0], cols), BF16)
    kernel = functools.partial(shared_terms_kernel, which)
    return call(kernel, 8, [shape] * len(which), (), 1)(info, dgate, dup, shared_gate, shared_up)


def ring_place(position):
    position = position % 8
    return jnp.where(position < 4, 2 * position, 15 - 2 * position)


def per_device_ring(
    tokens,
    out_grad,
    expert_ids,
    router_probs,
    router_weight,
    gate_weight,
    up_weight,
    down_weight,
    gate_saved,
    up_saved,
    shared_gate,
    shared_up,
    shared_down,
):
    slot_count = gate_saved.shape[1]
    capacity = slot_count // 8
    rows, cols = tokens.shape
    expert_total = router_probs.shape[1]
    tiles = expert_total // 8
    order = [0, 2, 4, 6, 7, 5, 3, 1]
    ahead = [(order[i], order[(i + 1) % 8]) for i in range(8)]
    behind = [(order[i], order[(i - 1) % 8]) for i in range(8)]
    x_pairs = [(i, i ^ 2) for i in range(4)]
    core_pairs = [(i, i ^ 1) for i in range(4)]
    me = lax.axis_index("expert")
    place = jnp.where(me % 2 == 0, me // 2, 7 - me // 2)
    here = lax.axis_index("tensor")
    first = me * 2
    base = [here % 2, first // 8, first % 8]
    tie = lax.optimization_barrier

    def swap_x(a):
        return lax.ppermute(a, "tensor", x_pairs)

    def swap_core(a):
        return lax.ppermute(a, "tensor", core_pairs)

    def ring(fore, back):
        return lax.ppermute(fore, "expert", ahead), lax.ppermute(back, "expert", behind)

    def hidden(blocks, steps=(0, 1)):
        return hidden_part(info, blocks, down_weight, tiles, capacity, steps)

    def grads(saved, weights, *parts):
        chunk = sum((part[0] for part in parts), ())
        return grad_part(
            info,
            [a for part in parts for a in part[1:]],
            saved,
            weights,
            [len(part[0]) for part in parts],
            chunk,
            chunk == (4,),
            tiles,
            capacity,
        )

    numbers = base + [here] + [ring_place(place + d) for d in range(-3, 5)]
    info = jnp.stack([jnp.asarray(n, jnp.int32) for n in numbers])
    payload, meta = payload_of(expert_ids.T, router_probs.T, out_grad, capacity)

    fore, back = ring(out_grad, out_grad)
    meta_f, meta_b = ring(meta, meta)
    grad_x = swap_x(out_grad)
    fore, back, grad_x, meta_f, meta_b, info = tie((fore, back, grad_x, meta_f, meta_b, info))
    fore1, back1 = attach(fore, meta_f, back, meta_b)

    fore, back = ring(fore1, back1)
    tok_x = swap_x(tokens)
    other1, mine1, meta1 = hidden([payload, fore1, back1])
    fore2, back2, other1, mine1, tok_x = tie((fore, back, other1, mine1, tok_x))

    fore, back = ring(fore2, back2)
    (chip1,) = sums((mine1, swap_core(other1)))
    other2, mine2, meta2 = hidden([fore2, back2])
    (chip2,) = sums((mine2, swap_core(other2)))
    fore3, back3, chip1, chip2 = tie((fore, back, chip1, chip2))

    top, bottom = ring(*halves_of(fore3, back3))
    far2 = swap_x(chip2)
    other3, mine3, meta3 = hidden([fore3, back3])
    tok_both = swap_core(tok_x)
    tok_core = swap_core(tokens)
    top, bottom, chip2, other3, mine3, tok_core, tok_both, out_grad = tie(
        (top, bottom, chip2, other3, mine3, tok_core, tok_both, out_grad)
    )

    (other4,) = hidden([(top, bottom)], (0,))
    top, bottom, other4, other3, far2 = tie((top, bottom, other4, other3, far2))
    swapped4 = swap_core(other4)
    mine4, meta4 = hidden([(top, bottom)], (1,))
    swapped3 = swap_core(other3)
    (chip4,) = sums((mine4, swapped4))
    chip4, swapped3, mine3, tok_in = tie((chip4, swapped3, mine3, tokens))
    far4 = swap_x(chip4)
    (chip3,) = sums((mine3, swapped3))
    far3 = swap_x(chip3)
    chip3, tok_in = tie((chip3, tok_in))
    active, slope = shared_inner(
        info, [tok_in, tok_core, tok_x, tok_both], shared_gate, shared_up
    )
    active, slope, chip2, far2 = tie((active, slope, chip2, far2))
    (full2,) = sums((chip2, far2))
    pair2 = swap_core(full2)
    far4, full2, active = tie((far4, full2, active))
    (full4,) = sums((chip4, far4))
    pair4 = swap_core(full4)
    saved = (gate_saved, up_saved)
    weights = (gate_weight, up_weight)
    top, bottom = grads(saved, weights, ((4,), full4, pair4, meta4))

    top, bottom, pair2, full2, far3, out_grad, chip1 = tie(
        (top, bottom, pair2, full2, far3, out_grad, chip1)
    )
    fore, back = ring(top, bottom)
    grad_core = swap_core(out_grad)
    far1 = swap_x(chip1)
    (full3,) = sums((chip3, far3))
    pair3 = swap_core(full3)
    near_b3, near_f3, near_b2, near_f2 = grads(
        saved, weights, ((-3, 3), full3, pair3, meta3), ((-2, 2), full2, pair2, meta2)
    )
    fore, back, near_f3, near_b3, near_f2, near_b2, grad_core, grad_in = tie(
        (fore, back, near_f3, near_b3, near_f2, near_b2, grad_core, out_grad)
    )

    fore, back = join(near_f3, fore, near_b3, back)
    fore, back = ring(fore, back)
    grad_both = swap_core(grad_x)
    grad_in, far1 = tie((grad_in, far1))
    dgate, dup = shared_slopes(
        info, [grad_in, grad_core, grad_x, grad_both], shared_down, active, slope
    )
    term3, term2 = shared_terms(info, dgate, dup, shared_gate, shared_up, cols, (3, 2))
    swapped = swap_core(term3)
    term3, dgate, dup = tie((term3, dgate, dup))
    term1, term0 = shared_terms(info, dgate, dup, shared_gate, shared_up, cols, (1, 0))
    fore, back, term1, term0, swapped, chip1, far1 = tie(
        (fore, back, term1, term0, swapped, chip1, far1)
    )

    fore, back, far = sums((near_f2, fore), (near_b2, back), (term2, swapped))
    fore, back = ring(fore, back)
    shared_far = swap_x(far)
    near = swap_core(term1)
    (full1,) = sums((chip1, far1))
    pair1 = swap_core(full1)
    near0, near_b1, near_f1 = grads(saved, weights, ((0, -1, 1), full1, pair1, meta1))
    fore, back, near, near0, near_b1, near_f1 = tie(
        (fore, back, near, near0, near_b1, near_f1)
    )

    fore, back = sums((near_f1, fore), (near_b1, back))
    fore, back = ring(fore, back)
    total = near0.astype(F32) + fore.astype(F32) + back.astype(F32)
    shared_part = term0.astype(F32) + near.astype(F32) + shared_far.astype(F32)
    prob_grad = jnp.concatenate(
        [total[rows:, i * rows : (i + 1) * rows] for i in range(tiles)], axis=0
    ).T
    gate_total = jnp.sum(router_probs * prob_grad, axis=1, keepdims=True)
    logit_grad = (router_probs * (prob_grad - gate_total)).astype(BF16)
    router_part = jnp.einsum("te,de->td", logit_grad, router_weight, preferred_element_type=F32)
    return (shared_part + total[:rows] + router_part).astype(BF16)


def per_device(*args):
    tokens, router_probs, gate_weight, gate_saved = args[0], args[3], args[5], args[8]
    rows, cols = tokens.shape
    expert_total = router_probs.shape[1]
    ring = (
        lax.axis_size("expert") == 8
        and lax.axis_size("tensor") == 4
        and gate_weight.shape[0] == 2
        and gate_saved.shape[1] == 8 * 64
        and gate_saved.shape[2] % 256 == 0
        and rows == 128
        and expert_total == 16
        and cols % 256 == 0
        and cols >= 6 * rows
    )
    return (per_device_ring if ring else per_device_wide)(*args)


def solution(mesh):

    return jax.shard_map(
        per_device,
        mesh=mesh,
        in_specs=(
            P("expert", "tensor"),
            P("expert", "tensor"),
            P("expert", None),
            P("expert", None),
            P("tensor", None),
            P("expert", "tensor", None),
            P("expert", "tensor", None),
            P("expert", None, "tensor"),
            P("expert", None, None),
            P("expert", None, None),
            P(None, "tensor"),
            P(None, "tensor"),
            P("tensor", None),
        ),
        out_specs=P("expert", "tensor"),
        check_vma=False,
    )
```

```python
import functools

import jax
import jax.numpy as jnp
from jax import lax
from jax.experimental import pallas as pl
from jax.experimental.pallas import tpu as pltpu
from jax.sharding import PartitionSpec as P


def silu_parts(preact):
    sigmoid_value = jax.nn.sigmoid(preact)
    return (preact * sigmoid_value, sigmoid_value * (1.0 + preact * (1.0 - sigmoid_value)))


def per_device_wide(
    tokens,
    out_grad,
    expert_ids,
    router_probs,
    router_weight,
    gate_weight,
    up_weight,
    down_weight,
    gate_saved,
    up_saved,
    shared_gate,
    shared_up,
    shared_down,
):
    groups = lax.axis_size("expert")
    local_count, slot_count, hidden_units = gate_saved.shape
    capacity = slot_count // groups
    token_rows, route_width = expert_ids.shape
    expert_total = router_probs.shape[1]
    feature_cols = tokens.shape[1]
    column_total = local_count * groups * capacity
    flat_ids = expert_ids.reshape(-1)
    onehot = (flat_ids[:, None] == jnp.arange(expert_total, dtype=jnp.int32)[None, :]).astype(
        jnp.int32
    )
    slot_index = jnp.sum((jnp.cumsum(onehot, axis=0) - onehot) * onehot, axis=1)
    kept_mask = slot_index < capacity
    owner_group = flat_ids // local_count
    local_expert = flat_ids % local_count
    column_id = jnp.where(
        kept_mask, local_expert * (groups * capacity) + owner_group * capacity + slot_index, -1
    )
    column_grid = column_id.reshape(token_rows, route_width)
    column_match = (
        column_grid[:, :, None] == jnp.arange(column_total, dtype=jnp.int32)[None, None, :]
    )
    placement = jnp.sum(column_match.astype(jnp.float32), axis=1).astype(jnp.bfloat16)
    sectioning = jnp.einsum(
        "tc,td->cd", placement, out_grad, preferred_element_type=jnp.float32
    ).astype(jnp.bfloat16)
    outgoing = sectioning.reshape(local_count, groups, capacity * feature_cols)
    token_piece = lax.all_gather(tokens, "tensor", axis=1, tiled=True)
    grad_piece = lax.all_gather(out_grad, "tensor", axis=1, tiled=True)
    gate_pre = jnp.dot(token_piece, shared_gate, preferred_element_type=jnp.float32)
    up_pre = jnp.dot(token_piece, shared_up, preferred_element_type=jnp.float32)
    hidden_pre = jnp.einsum(
        "tc,fc->tf", grad_piece, shared_down, preferred_element_type=jnp.float32
    )
    active, slope_term = silu_parts(gate_pre)
    shared_dgate = (hidden_pre * up_pre * slope_term).astype(jnp.bfloat16)
    shared_dup = (hidden_pre * active).astype(jnp.bfloat16)
    shared_term = jnp.einsum(
        "tf,df->td", shared_dgate, shared_gate, preferred_element_type=jnp.float32
    ) + jnp.einsum("tf,df->td", shared_dup, shared_up, preferred_element_type=jnp.float32)
    shared_part = lax.psum_scatter(
        shared_term.astype(jnp.bfloat16), "tensor", scatter_dimension=1, tiled=True
    ).astype(jnp.float32)
    arrived = lax.all_to_all(outgoing, "expert", split_axis=1, concat_axis=1, tiled=True)
    arrived = arrived.reshape(local_count, slot_count, feature_cols)
    partial_hidden = jnp.einsum(
        "esd,efd->esf", arrived, down_weight, preferred_element_type=jnp.float32
    )
    up_full = up_saved.astype(jnp.float32)
    hidden_grad = lax.psum(partial_hidden.astype(jnp.bfloat16), "tensor").astype(jnp.float32)
    active, slope_term = silu_parts(gate_saved.astype(jnp.float32))
    d_gate = (hidden_grad * up_full * slope_term).astype(jnp.bfloat16)
    d_up = (hidden_grad * active).astype(jnp.bfloat16)
    score_rows = jnp.sum(up_full * d_up.astype(jnp.float32), axis=2).astype(jnp.bfloat16)
    expert_grad = jnp.einsum(
        "esf,edf->esd", d_gate, gate_weight, preferred_element_type=jnp.float32
    ) + jnp.einsum("esf,edf->esd", d_up, up_weight, preferred_element_type=jnp.float32)
    expert_grad = expert_grad.astype(jnp.bfloat16)
    back_grad, back_score = (
        lax.all_to_all(
            expert_grad.reshape(local_count, groups, capacity * feature_cols),
            "expert",
            split_axis=1,
            concat_axis=1,
            tiled=True,
        ),
        lax.all_to_all(
            score_rows.reshape(local_count, groups, capacity),
            "expert",
            split_axis=1,
            concat_axis=1,
            tiled=True,
        ),
    )
    returned_rows = back_grad.reshape(column_total, feature_cols)
    returned_scores = back_score.reshape(column_total).astype(jnp.float32)
    kept_value = kept_mask.astype(jnp.float32)
    probs_rows = jnp.repeat(router_probs, route_width, axis=0)
    onehot_float = onehot.astype(jnp.float32)
    gate_value = jnp.sum(onehot_float * probs_rows, axis=1)
    route_weight = (gate_value * kept_value).reshape(token_rows, route_width)
    combine_weight = jnp.sum(jnp.where(column_match, route_weight[:, :, None], 0.0), axis=1)
    routed_part = jnp.dot(
        combine_weight,
        returned_rows.astype(jnp.float32),
        precision=lax.Precision.HIGHEST,
        preferred_element_type=jnp.float32,
    )
    safe_column = jnp.maximum(column_id, 0)
    route_score = returned_scores[safe_column] * kept_value
    prob_grad = jnp.sum(
        (onehot_float * route_score[:, None]).reshape(token_rows, route_width, expert_total), axis=1
    )
    gate_total = jnp.sum((gate_value * route_score).reshape(token_rows, route_width), axis=1)
    logit_grad = (router_probs * (prob_grad - gate_total[:, None])).astype(jnp.bfloat16)
    router_part = jnp.einsum(
        "te,de->td", logit_grad, router_weight, preferred_element_type=jnp.float32
    )
    return (shared_part + routed_part + router_part).astype(jnp.bfloat16)


F32, BF16 = jnp.float32, jnp.bfloat16
LAST = (((1,), (1,)), ((), ()))
FIRST = (((0,), (0,)), ((), ()))
TOP_ROWS = 64
INFO_BLOCKS = 7


def call(kernel, megabytes, out_shape, scratch_shapes=(), scalars=0, far=0):
    def run(*operands):
        near = len(operands) - scalars - far
        memory = [pltpu.SMEM] * scalars + [pltpu.VMEM] * near + [pl.ANY] * far
        return pl.pallas_call(
            kernel,
            in_specs=[pl.BlockSpec(memory_space=m) for m in memory],
            out_specs=jax.tree.map(lambda _: pl.BlockSpec(memory_space=pltpu.VMEM), out_shape),
            out_shape=out_shape,
            scratch_shapes=scratch_shapes,
            compiler_params=pltpu.CompilerParams(vmem_limit_bytes=megabytes * 1024 * 1024),
            cost_estimate=pl.CostEstimate(flops=1000, bytes_accessed=1000, transcendentals=0),
        )(*operands)

    return run


def sum_kernel(groups, *refs):
    count = sum(groups)
    at = 0
    for out_ref, size in zip(refs[count:], groups):
        total = refs[at][...].astype(F32)
        for ref in refs[at + 1 : at + size]:
            total = total + ref[...].astype(F32)
        out_ref[...] = total.astype(BF16)
        at += size


def sums(*groups):
    return call(
        functools.partial(sum_kernel, [len(g) for g in groups]),
        2,
        [jax.ShapeDtypeStruct(g[0].shape, BF16) for g in groups],
    )(*[a for g in groups for a in g])


def halves_kernel(fore_ref, back_ref, top_ref, bottom_ref):
    top_ref[...] = fore_ref[0:TOP_ROWS, :]
    bottom_ref[...] = back_ref[TOP_ROWS:, :]


def halves_of(fore, back):
    rows, cols = fore.shape
    return call(
        halves_kernel,
        2,
        [
            jax.ShapeDtypeStruct((TOP_ROWS, cols), BF16),
            jax.ShapeDtypeStruct((rows - TOP_ROWS, cols), BF16),
        ],
    )(fore, back)


def join_kernel(near_f_ref, top_ref, near_b_ref, bottom_ref, fore_ref, back_ref):
    top = near_f_ref[0:TOP_ROWS, :].astype(F32) + top_ref[...].astype(F32)
    fore_ref[0:TOP_ROWS, :] = top.astype(BF16)
    fore_ref[TOP_ROWS:, :] = near_f_ref[TOP_ROWS:, :]
    back_ref[0:TOP_ROWS, :] = near_b_ref[0:TOP_ROWS, :]
    bottom = near_b_ref[TOP_ROWS:, :].astype(F32) + bottom_ref[...].astype(F32)
    back_ref[TOP_ROWS:, :] = bottom.astype(BF16)


def join(near_f, top, near_b, bottom):
    shape = jax.ShapeDtypeStruct(near_f.shape, BF16)
    return call(join_kernel, 2, [shape, shape])(near_f, top, near_b, bottom)


def attach_kernel(fore_ref, meta_f_ref, back_ref, meta_b_ref, fore_out, back_out):
    rows = fore_ref.shape[0]
    for ref, meta_ref, out_ref in (
        (fore_ref, meta_f_ref, fore_out),
        (back_ref, meta_b_ref, back_out),
    ):
        out_ref[0:rows, :] = ref[...]
        out_ref[rows:, :] = meta_ref[...]


def attach(fore, meta_f, back, meta_b):
    rows, cols = fore.shape
    shape = jax.ShapeDtypeStruct((rows + 8, cols), BF16)
    return call(attach_kernel, 2, [shape, shape])(fore, meta_f, back, meta_b)


def payload_kernel(
    capacity, ids_hbm, probs_hbm, grad_hbm, out_ref, meta_ref, ids_ref, probs_ref, sems
):
    expert_total, rows = probs_ref.shape
    cols = grad_hbm.shape[1]
    copies = [
        pltpu.make_async_copy(ids_hbm, ids_ref, sems.at[0]),
        pltpu.make_async_copy(probs_hbm, probs_ref, sems.at[1]),
        pltpu.make_async_copy(grad_hbm, out_ref.at[0:rows, :], sems.at[2]),
    ]
    for copy in copies:
        copy.start()
    experts = lax.broadcasted_iota(jnp.int32, (expert_total, rows), 0)
    row_at = lax.broadcasted_iota(jnp.int32, (rows, rows), 0)
    col_at = lax.broadcasted_iota(jnp.int32, (rows, rows), 1)
    lower = jnp.where(row_at < col_at, 1.0, 0.0).astype(BF16)
    copies[0].wait()
    ids = ids_ref[...]
    member = jnp.zeros((expert_total, rows), F32)
    for k in range(ids.shape[0]):
        member = member + jnp.where(ids[k : k + 1, :] == experts, 1.0, 0.0)
    before = jnp.dot(member.astype(BF16), lower, preferred_element_type=F32)
    slot = jnp.where((member > 0.5) & (before < capacity), before, -1.0)
    copies[1].wait()
    probs = probs_ref[...]
    high = probs.astype(BF16).astype(F32)
    parts = [slot, high, probs - high]
    pieces = [a[8 * i : 8 * i + 8] for a in parts for i in range(expert_total // 8)]
    pieces.append(jnp.zeros((8, cols - len(pieces) * rows), F32))
    meta = jnp.concatenate(pieces, axis=1).astype(BF16)
    out_ref[rows : rows + 8, :] = meta
    meta_ref[...] = meta
    copies[2].wait()


def payload_of(ids_t, probs_t, grad, capacity):
    rows, cols = grad.shape
    return call(
        functools.partial(payload_kernel, capacity),
        60,
        [
            jax.ShapeDtypeStruct((rows + 8, cols), BF16),
            jax.ShapeDtypeStruct((8, cols), BF16),
        ],
        [
            pltpu.VMEM(ids_t.shape, jnp.int32),
            pltpu.VMEM(probs_t.shape, F32),
            pltpu.SemaphoreType.DMA((3,)),
        ],
        0,
        3,
    )(ids_t, probs_t, grad)


def hidden_kernel(halves, tiles, capacity, steps, info_ref, *refs):
    block_refs = refs[: len(halves)]
    weight_ref, placed_ref = refs[len(halves)], refs[-1]
    out_refs = refs[len(halves) + 1 : -1]
    core, tile, row = info_ref[0], info_ref[1], info_ref[2]
    blocks, at = [], 0
    while at < len(halves):
        size = 2 if halves[at] else 1
        blocks.append(block_refs[at : at + size])
        at += size
    rows = 128
    units = weight_ref.shape[1]

    def pick(meta, kind, which):
        value = meta[:, kind * tiles * rows : (kind * tiles + 1) * rows]
        for i in range(1, tiles):
            at_lane = (kind * tiles + i) * rows
            value = jnp.where(tile == i, meta[:, at_lane : at_lane + rows], value)
        line = lax.broadcasted_iota(jnp.int32, (8, rows), 0)
        return jnp.sum(jnp.where(line == which, value, 0.0), axis=0, keepdims=True)

    slot_at = lax.broadcasted_iota(jnp.int32, (capacity, rows), 0).astype(F32)
    for step in steps:
        expert = 1 - core if step == 0 else core
        for b, block in enumerate(blocks):
            last = block[-1]
            meta = last[last.shape[0] - 8 :, :].astype(F32)
            match = jnp.where(slot_at == pick(meta, 0, row + expert), 1.0, 0.0).astype(BF16)
            if len(block) == 1:
                data = block[0][0:rows, :]
            else:
                data = jnp.concatenate([block[0][...], block[1][0 : rows - TOP_ROWS, :]], axis=0)
            placed = jnp.dot(match, data, preferred_element_type=F32)
            placed_ref[step, b * capacity : (b + 1) * capacity, :] = placed.astype(BF16)
            if step == 1:
                lines = [pick(meta, 0, row), pick(meta, 0, row + 1)]
                lines += [pick(meta, 1, row) + pick(meta, 2, row)]
                lines += [pick(meta, 1, row + 1) + pick(meta, 2, row + 1)]
                lines += [jnp.zeros((4, rows), F32)]
                out_refs[-1][8 * b : 8 * b + 8, :] = jnp.concatenate(lines, axis=0)
        out_ref = out_refs[steps.index(step)]
        for n in range(0, units, 256):
            value = lax.dot_general(
                placed_ref[step],
                weight_ref[expert, n : n + 256, :],
                LAST,
                preferred_element_type=F32,
            )
            out_ref[:, n : n + 256] = value.astype(BF16)


def hidden_part(info, blocks, down_weight, tiles, capacity, steps):
    local_count, hidden_units, cols = down_weight.shape
    flat, halves = [], []
    for block in blocks:
        pair = isinstance(block, tuple)
        flat += list(block) if pair else [block]
        halves += [pair, pair] if pair else [False]
    count = len(blocks)
    shape = (count * capacity, hidden_units)
    return call(
        functools.partial(hidden_kernel, halves, tiles, capacity, steps),
        10,
        [jax.ShapeDtypeStruct(shape, BF16)] * len(steps)
        + [jax.ShapeDtypeStruct((8 * count, 128), F32)] * (1 in steps),
        [pltpu.VMEM((2, count * capacity, cols), BF16)],
        1,
    )(info, *flat, down_weight)


def grad_kernel(counts, chunk, split, tiles, capacity, info_ref, *refs):
    groups = len(counts)
    total = sum(counts)
    hidden_refs = refs[: 3 * groups]
    gate_ref, up_ref, gate_w_ref, up_w_ref = refs[3 * groups : 3 * groups + 4]
    out_refs = refs[3 * groups + 4 : -2]
    dgate_ref, dup_ref = refs[-2:]
    core, tile, row = info_ref[0], info_ref[1], info_ref[2]
    rows = 128
    cols = gate_w_ref.shape[1]
    line = lax.broadcasted_iota(jnp.int32, (8, rows), 0)
    slot_at = lax.broadcasted_iota(jnp.int32, (capacity, rows), 0).astype(F32)
    combine, scores = [], []
    b = 0
    for g in range(groups):
        full_ref, pair_ref, meta_ref = hidden_refs[3 * g : 3 * g + 3]
        for i in range(counts[g]):
            span = slice(i * capacity, (i + 1) * capacity)
            store = slice(b * capacity, (b + 1) * capacity)
            saved = pl.ds(pl.multiple_of(info_ref[INFO_BLOCKS + chunk[b]] * capacity, capacity), capacity)
            lines = meta_ref[8 * i : 8 * i + 8, :]
            score_rows = jnp.zeros((8, rows), F32)
            stacked = []
            for e in range(2):
                hidden = jnp.where(core == e, full_ref[span, :], pair_ref[span, :]).astype(F32)
                gate = gate_ref[e, saved, :].astype(F32)
                up = up_ref[e, saved, :].astype(F32)
                active, slope_term = silu_parts(gate)
                dup = hidden * active
                match = slot_at == lines[e : e + 1, :]
                weight = jnp.sum(
                    jnp.where(match, lines[2 + e : 3 + e, :], 0.0), axis=1, keepdims=True
                )
                dgate_ref[e, store, :] = (hidden * up * slope_term * weight).astype(BF16)
                dup_ref[e, store, :] = (dup * weight).astype(BF16)
                score = jnp.sum(up * dup.astype(BF16).astype(F32), axis=1, keepdims=True)
                score = score.astype(BF16).astype(F32)
                token_score = jnp.sum(jnp.where(match, score, 0.0), axis=0, keepdims=True)
                score_rows = score_rows + jnp.where(line == row + e, token_score, 0.0)
                stacked.append(jnp.where(match, 1.0, 0.0).astype(BF16))
            combine.append(jnp.concatenate(stacked, axis=0))
            scores.append(score_rows)
            b += 1
    for n in range(0, cols, 1280):
        grads = []
        for e in range(2):
            value = lax.dot_general(
                dgate_ref[e], gate_w_ref[e, n : n + 1280, :], LAST, preferred_element_type=F32
            )
            value = value + lax.dot_general(
                dup_ref[e], up_w_ref[e, n : n + 1280, :], LAST, preferred_element_type=F32
            )
            grads.append(value.astype(BF16))
        for b in range(total):
            span = slice(b * capacity, (b + 1) * capacity)
            pile = jnp.concatenate([g[span] for g in grads], axis=0)
            value = lax.dot_general(combine[b], pile, FIRST, preferred_element_type=F32)
            if n == 0:
                lanes = [jnp.where(tile == i, scores[b], 0.0) for i in range(tiles)]
                lanes = jnp.concatenate(lanes + [jnp.zeros((8, 1280 - tiles * rows), F32)], axis=1)
            else:
                lanes = jnp.zeros((8, 1280), F32)
            if split:
                out_refs[2 * b][:, n : n + 1280] = value[:TOP_ROWS].astype(BF16)
                low = jnp.concatenate([value[TOP_ROWS:], lanes], axis=0)
                out_refs[2 * b + 1][:, n : n + 1280] = low.astype(BF16)
            else:
                out_refs[b][:, n : n + 1280] = jnp.concatenate([value, lanes], axis=0).astype(BF16)


def grad_part(info, parts, saved, weights, counts, chunk, split, tiles, capacity):
    local_count, cols, hidden_units = weights[0].shape
    total = sum(counts)
    heights = [TOP_ROWS, 136 - TOP_ROWS] * total if split else [136] * total
    return call(
        functools.partial(grad_kernel, counts, chunk, split, tiles, capacity),
        14,
        [jax.ShapeDtypeStruct((h, cols), BF16) for h in heights],
        [
            pltpu.VMEM((2, total * capacity, hidden_units), BF16),
            pltpu.VMEM((2, total * capacity, hidden_units), BF16),
        ],
        1,
    )(info, *parts, *saved, *weights)


def shared_spans(info_ref, cols):
    here = info_ref[3]
    return [
        pl.ds(pl.multiple_of(jnp.bitwise_xor(here, q) * cols, cols), cols) for q in range(4)
    ]


def shared_inner_kernel(info_ref, *refs):
    token_refs, (gate_ref, up_ref, active_ref, slope_ref) = refs[0:4], refs[4:]
    rows, cols = token_refs[0].shape
    units = gate_ref.shape[1]
    spans = shared_spans(info_ref, cols)
    gate_pre = jnp.zeros((rows, units), F32)
    up_pre = jnp.zeros((rows, units), F32)
    for q in range(4):
        token = token_refs[q][...]
        gate_pre = gate_pre + jnp.dot(token, gate_ref[spans[q], :], preferred_element_type=F32)
        up_pre = up_pre + jnp.dot(token, up_ref[spans[q], :], preferred_element_type=F32)
    active, slope_term = silu_parts(gate_pre)
    active_ref[...] = active
    slope_ref[...] = up_pre * slope_term


def shared_inner(info, token_blocks, shared_gate, shared_up):
    shape = jax.ShapeDtypeStruct((token_blocks[0].shape[0], shared_gate.shape[1]), F32)
    return call(shared_inner_kernel, 8, [shape, shape], (), 1)(
        info, *token_blocks, shared_gate, shared_up
    )


def shared_slopes_kernel(info_ref, *refs):
    grad_refs, (down_ref, active_ref, slope_ref, dgate_ref, dup_ref) = refs[0:4], refs[4:]
    rows, cols = grad_refs[0].shape
    spans = shared_spans(info_ref, cols)
    hidden_pre = jnp.zeros((rows, down_ref.shape[0]), F32)
    for q in range(4):
        hidden_pre = hidden_pre + lax.dot_general(
            grad_refs[q][...], down_ref[:, spans[q]], LAST, preferred_element_type=F32
        )
    dgate_ref[...] = (hidden_pre * slope_ref[...]).astype(BF16)
    dup_ref[...] = (hidden_pre * active_ref[...]).astype(BF16)


def shared_slopes(info, grad_blocks, shared_down, active, slope):
    shape = jax.ShapeDtypeStruct(active.shape, BF16)
    return call(shared_slopes_kernel, 8, [shape, shape], (), 1)(
        info, *grad_blocks, shared_down, active, slope
    )


def shared_terms_kernel(which, info_ref, dgate_ref, dup_ref, gate_ref, up_ref, *out_refs):
    cols = out_refs[0].shape[1]
    spans = shared_spans(info_ref, cols)
    dgate, dup = dgate_ref[...], dup_ref[...]
    for out_ref, q in zip(out_refs, which):
        term = lax.dot_general(dgate, gate_ref[spans[q], :], LAST, preferred_element_type=F32)
        term = term + lax.dot_general(dup, up_ref[spans[q], :], LAST, preferred_element_type=F32)
        out_ref[...] = term.astype(BF16)


def shared_terms(info, dgate, dup, shared_gate, shared_up, cols, which):
    shape = jax.ShapeDtypeStruct((dgate.shape[0], cols), BF16)
    kernel = functools.partial(shared_terms_kernel, which)
    return call(kernel, 8, [shape] * len(which), (), 1)(info, dgate, dup, shared_gate, shared_up)


def ring_place(position):
    position = position % 8
    return jnp.where(position < 4, 2 * position, 15 - 2 * position)


def per_device_ring(
    tokens,
    out_grad,
    expert_ids,
    router_probs,
    router_weight,
    gate_weight,
    up_weight,
    down_weight,
    gate_saved,
    up_saved,
    shared_gate,
    shared_up,
    shared_down,
):
    slot_count = gate_saved.shape[1]
    capacity = slot_count // 8
    rows, cols = tokens.shape
    expert_total = router_probs.shape[1]
    tiles = expert_total // 8
    order = [0, 2, 4, 6, 7, 5, 3, 1]
    ahead = [(order[i], order[(i + 1) % 8]) for i in range(8)]
    behind = [(order[i], order[(i - 1) % 8]) for i in range(8)]
    x_pairs = [(i, i ^ 2) for i in range(4)]
    core_pairs = [(i, i ^ 1) for i in range(4)]
    me = lax.axis_index("expert")
    place = jnp.where(me % 2 == 0, me // 2, 7 - me // 2)
    here = lax.axis_index("tensor")
    first = me * 2
    base = [here % 2, first // 8, first % 8]
    tie = lax.optimization_barrier

    def swap_x(a):
        return lax.ppermute(a, "tensor", x_pairs)

    def swap_core(a):
        return lax.ppermute(a, "tensor", core_pairs)

    def ring(fore, back):
        return lax.ppermute(fore, "expert", ahead), lax.ppermute(back, "expert", behind)

    def hidden(blocks, steps=(0, 1)):
        return hidden_part(info, blocks, down_weight, tiles, capacity, steps)

    def grads(saved, weights, *parts):
        chunk = sum((part[0] for part in parts), ())
        return grad_part(
            info,
            [a for part in parts for a in part[1:]],
            saved,
            weights,
            [len(part[0]) for part in parts],
            chunk,
            chunk == (4,),
            tiles,
            capacity,
        )

    numbers = base + [here] + [ring_place(place + d) for d in range(-3, 5)]
    info = jnp.stack([jnp.asarray(n, jnp.int32) for n in numbers])
    payload, meta = payload_of(expert_ids.T, router_probs.T, out_grad, capacity)

    fore, back = ring(out_grad, out_grad)
    meta_f, meta_b = ring(meta, meta)
    grad_x = swap_x(out_grad)
    fore, back, grad_x, meta_f, meta_b, info = tie((fore, back, grad_x, meta_f, meta_b, info))
    fore1, back1 = attach(fore, meta_f, back, meta_b)

    fore, back = ring(fore1, back1)
    tok_x = swap_x(tokens)
    other1, mine1, meta1 = hidden([payload, fore1, back1])
    fore2, back2, other1, mine1 = tie((fore, back, other1, mine1))

    fore, back = ring(fore2, back2)
    (chip1,) = sums((mine1, swap_core(other1)))
    fore2, tok_x = tie((fore2, tok_x))
    other2, mine2, meta2 = hidden([fore2, back2])
    (chip2,) = sums((mine2, swap_core(other2)))
    fore3, back3, chip1, chip2 = tie((fore, back, chip1, chip2))

    top, bottom = ring(*halves_of(fore3, back3))
    far2 = swap_x(chip2)
    other3, mine3, meta3 = hidden([fore3, back3])
    tok_both = swap_core(tok_x)
    tok_core = swap_core(tokens)
    top, bottom, chip2, other3, mine3, tok_core, tok_both, out_grad = tie(
        (top, bottom, chip2, other3, mine3, tok_core, tok_both, out_grad)
    )

    (other4,) = hidden([(top, bottom)], (0,))
    top, bottom, other4, other3, far2 = tie((top, bottom, other4, other3, far2))
    swapped4 = swap_core(other4)
    mine4, meta4 = hidden([(top, bottom)], (1,))
    swapped3 = swap_core(other3)
    (chip4,) = sums((mine4, swapped4))
    chip4, swapped3, mine3, tok_in = tie((chip4, swapped3, mine3, tokens))
    far4 = swap_x(chip4)
    (chip3,) = sums((mine3, swapped3))
    far3 = swap_x(chip3)
    chip3, tok_in = tie((chip3, tok_in))
    active, slope = shared_inner(
        info, [tok_in, tok_core, tok_x, tok_both], shared_gate, shared_up
    )
    active, slope, chip2, far2 = tie((active, slope, chip2, far2))
    (full2,) = sums((chip2, far2))
    pair2 = swap_core(full2)
    far4, full2, active = tie((far4, full2, active))
    (full4,) = sums((chip4, far4))
    pair4 = swap_core(full4)
    saved = (gate_saved, up_saved)
    weights = (gate_weight, up_weight)
    top, bottom = grads(saved, weights, ((4,), full4, pair4, meta4))

    top, bottom, pair2, full2, far3, out_grad, chip1 = tie(
        (top, bottom, pair2, full2, far3, out_grad, chip1)
    )
    fore, back = ring(top, bottom)
    grad_core = swap_core(out_grad)
    far1 = swap_x(chip1)
    (full3,) = sums((chip3, far3))
    pair3 = swap_core(full3)
    near_b3, near_f3, near_b2, near_f2 = grads(
        saved, weights, ((-3, 3), full3, pair3, meta3), ((-2, 2), full2, pair2, meta2)
    )
    fore, back, near_f3, near_b3, near_f2, near_b2, grad_core, grad_in = tie(
        (fore, back, near_f3, near_b3, near_f2, near_b2, grad_core, out_grad)
    )

    fore, back = join(near_f3, fore, near_b3, back)
    fore, back = ring(fore, back)
    grad_both = swap_core(grad_x)
    grad_in, far1 = tie((grad_in, far1))
    dgate, dup = shared_slopes(
        info, [grad_in, grad_core, grad_x, grad_both], shared_down, active, slope
    )
    term3, term2 = shared_terms(info, dgate, dup, shared_gate, shared_up, cols, (3, 2))
    swapped = swap_core(term3)
    term3, dgate, dup = tie((term3, dgate, dup))
    term1, term0 = shared_terms(info, dgate, dup, shared_gate, shared_up, cols, (1, 0))
    fore, back, term1, term0, swapped, chip1, far1 = tie(
        (fore, back, term1, term0, swapped, chip1, far1)
    )

    fore, back, far = sums((near_f2, fore), (near_b2, back), (term2, swapped))
    fore, back = ring(fore, back)
    shared_far = swap_x(far)
    near = swap_core(term1)
    (full1,) = sums((chip1, far1))
    pair1 = swap_core(full1)
    near0, near_b1, near_f1 = grads(saved, weights, ((0, -1, 1), full1, pair1, meta1))
    fore, back, near, near0, near_b1, near_f1 = tie(
        (fore, back, near, near0, near_b1, near_f1)
    )

    fore, back = sums((near_f1, fore), (near_b1, back))
    fore, back = ring(fore, back)
    total = near0.astype(F32) + fore.astype(F32) + back.astype(F32)
    shared_part = term0.astype(F32) + near.astype(F32) + shared_far.astype(F32)
    prob_grad = jnp.concatenate(
        [total[rows:, i * rows : (i + 1) * rows] for i in range(tiles)], axis=0
    ).T
    gate_total = jnp.sum(router_probs * prob_grad, axis=1, keepdims=True)
    logit_grad = (router_probs * (prob_grad - gate_total)).astype(BF16)
    router_part = jnp.einsum("te,de->td", logit_grad, router_weight, preferred_element_type=F32)
    return (shared_part + total[:rows] + router_part).astype(BF16)


def per_device(*args):
    tokens, router_probs, gate_weight, gate_saved = args[0], args[3], args[5], args[8]
    rows, cols = tokens.shape
    expert_total = router_probs.shape[1]
    ring = (
        lax.axis_size("expert") == 8
        and lax.axis_size("tensor") == 4
        and gate_weight.shape[0] == 2
        and gate_saved.shape[1] == 8 * 64
        and gate_saved.shape[2] % 256 == 0
        and rows == 128
        and expert_total == 16
        and cols % 256 == 0
        and cols >= 6 * rows
    )
    return (per_device_ring if ring else per_device_wide)(*args)


def solution(mesh):

    return jax.shard_map(
        per_device,
        mesh=mesh,
        in_specs=(
            P("expert", "tensor"),
            P("expert", "tensor"),
            P("expert", None),
            P("expert", None),
            P("tensor", None),
            P("expert", "tensor", None),
            P("expert", "tensor", None),
            P("expert", None, "tensor"),
            P("expert", None, None),
            P("expert", None, None),
            P(None, "tensor"),
            P(None, "tensor"),
            P("tensor", None),
        ),
        out_specs=P("expert", "tensor"),
        check_vma=False,
    )
```

```python
import functools

import jax
import jax.numpy as jnp
from jax import lax
from jax.experimental import pallas as pl
from jax.experimental.pallas import tpu as pltpu
from jax.sharding import PartitionSpec as P


def silu_parts(preact):
    sigmoid_value = jax.nn.sigmoid(preact)
    return (preact * sigmoid_value, sigmoid_value * (1.0 + preact * (1.0 - sigmoid_value)))


def per_device_wide(
    tokens,
    out_grad,
    expert_ids,
    router_probs,
    router_weight,
    gate_weight,
    up_weight,
    down_weight,
    gate_saved,
    up_saved,
    shared_gate,
    shared_up,
    shared_down,
):
    groups = lax.axis_size("expert")
    local_count, slot_count, hidden_units = gate_saved.shape
    capacity = slot_count // groups
    token_rows, route_width = expert_ids.shape
    expert_total = router_probs.shape[1]
    feature_cols = tokens.shape[1]
    column_total = local_count * groups * capacity
    flat_ids = expert_ids.reshape(-1)
    onehot = (flat_ids[:, None] == jnp.arange(expert_total, dtype=jnp.int32)[None, :]).astype(
        jnp.int32
    )
    slot_index = jnp.sum((jnp.cumsum(onehot, axis=0) - onehot) * onehot, axis=1)
    kept_mask = slot_index < capacity
    owner_group = flat_ids // local_count
    local_expert = flat_ids % local_count
    column_id = jnp.where(
        kept_mask, local_expert * (groups * capacity) + owner_group * capacity + slot_index, -1
    )
    column_grid = column_id.reshape(token_rows, route_width)
    column_match = (
        column_grid[:, :, None] == jnp.arange(column_total, dtype=jnp.int32)[None, None, :]
    )
    placement = jnp.sum(column_match.astype(jnp.float32), axis=1).astype(jnp.bfloat16)
    sectioning = jnp.einsum(
        "tc,td->cd", placement, out_grad, preferred_element_type=jnp.float32
    ).astype(jnp.bfloat16)
    outgoing = sectioning.reshape(local_count, groups, capacity * feature_cols)
    token_piece = lax.all_gather(tokens, "tensor", axis=1, tiled=True)
    grad_piece = lax.all_gather(out_grad, "tensor", axis=1, tiled=True)
    gate_pre = jnp.dot(token_piece, shared_gate, preferred_element_type=jnp.float32)
    up_pre = jnp.dot(token_piece, shared_up, preferred_element_type=jnp.float32)
    hidden_pre = jnp.einsum(
        "tc,fc->tf", grad_piece, shared_down, preferred_element_type=jnp.float32
    )
    active, slope_term = silu_parts(gate_pre)
    shared_dgate = (hidden_pre * up_pre * slope_term).astype(jnp.bfloat16)
    shared_dup = (hidden_pre * active).astype(jnp.bfloat16)
    shared_term = jnp.einsum(
        "tf,df->td", shared_dgate, shared_gate, preferred_element_type=jnp.float32
    ) + jnp.einsum("tf,df->td", shared_dup, shared_up, preferred_element_type=jnp.float32)
    shared_part = lax.psum_scatter(
        shared_term.astype(jnp.bfloat16), "tensor", scatter_dimension=1, tiled=True
    ).astype(jnp.float32)
    arrived = lax.all_to_all(outgoing, "expert", split_axis=1, concat_axis=1, tiled=True)
    arrived = arrived.reshape(local_count, slot_count, feature_cols)
    partial_hidden = jnp.einsum(
        "esd,efd->esf", arrived, down_weight, preferred_element_type=jnp.float32
    )
    up_full = up_saved.astype(jnp.float32)
    hidden_grad = lax.psum(partial_hidden.astype(jnp.bfloat16), "tensor").astype(jnp.float32)
    active, slope_term = silu_parts(gate_saved.astype(jnp.float32))
    d_gate = (hidden_grad * up_full * slope_term).astype(jnp.bfloat16)
    d_up = (hidden_grad * active).astype(jnp.bfloat16)
    score_rows = jnp.sum(up_full * d_up.astype(jnp.float32), axis=2).astype(jnp.bfloat16)
    expert_grad = jnp.einsum(
        "esf,edf->esd", d_gate, gate_weight, preferred_element_type=jnp.float32
    ) + jnp.einsum("esf,edf->esd", d_up, up_weight, preferred_element_type=jnp.float32)
    expert_grad = expert_grad.astype(jnp.bfloat16)
    back_grad, back_score = (
        lax.all_to_all(
            expert_grad.reshape(local_count, groups, capacity * feature_cols),
            "expert",
            split_axis=1,
            concat_axis=1,
            tiled=True,
        ),
        lax.all_to_all(
            score_rows.reshape(local_count, groups, capacity),
            "expert",
            split_axis=1,
            concat_axis=1,
            tiled=True,
        ),
    )
    returned_rows = back_grad.reshape(column_total, feature_cols)
    returned_scores = back_score.reshape(column_total).astype(jnp.float32)
    kept_value = kept_mask.astype(jnp.float32)
    probs_rows = jnp.repeat(router_probs, route_width, axis=0)
    onehot_float = onehot.astype(jnp.float32)
    gate_value = jnp.sum(onehot_float * probs_rows, axis=1)
    route_weight = (gate_value * kept_value).reshape(token_rows, route_width)
    combine_weight = jnp.sum(jnp.where(column_match, route_weight[:, :, None], 0.0), axis=1)
    routed_part = jnp.dot(
        combine_weight,
        returned_rows.astype(jnp.float32),
        precision=lax.Precision.HIGHEST,
        preferred_element_type=jnp.float32,
    )
    safe_column = jnp.maximum(column_id, 0)
    route_score = returned_scores[safe_column] * kept_value
    prob_grad = jnp.sum(
        (onehot_float * route_score[:, None]).reshape(token_rows, route_width, expert_total), axis=1
    )
    gate_total = jnp.sum((gate_value * route_score).reshape(token_rows, route_width), axis=1)
    logit_grad = (router_probs * (prob_grad - gate_total[:, None])).astype(jnp.bfloat16)
    router_part = jnp.einsum(
        "te,de->td", logit_grad, router_weight, preferred_element_type=jnp.float32
    )
    return (shared_part + routed_part + router_part).astype(jnp.bfloat16)


F32, BF16 = jnp.float32, jnp.bfloat16
LAST = (((1,), (1,)), ((), ()))
FIRST = (((0,), (0,)), ((), ()))
TOP_ROWS = 64
INFO_BLOCKS = 7


def call(kernel, megabytes, out_shape, scratch_shapes=(), scalars=0, far=0):
    def run(*operands):
        near = len(operands) - scalars - far
        memory = [pltpu.SMEM] * scalars + [pltpu.VMEM] * near + [pl.ANY] * far
        return pl.pallas_call(
            kernel,
            in_specs=[pl.BlockSpec(memory_space=m) for m in memory],
            out_specs=jax.tree.map(lambda _: pl.BlockSpec(memory_space=pltpu.VMEM), out_shape),
            out_shape=out_shape,
            scratch_shapes=scratch_shapes,
            compiler_params=pltpu.CompilerParams(vmem_limit_bytes=megabytes * 1024 * 1024),
            cost_estimate=pl.CostEstimate(flops=1000, bytes_accessed=1000, transcendentals=0),
        )(*operands)

    return run


def sum_kernel(groups, *refs):
    count = sum(groups)
    at = 0
    for out_ref, size in zip(refs[count:], groups):
        total = refs[at][...].astype(F32)
        for ref in refs[at + 1 : at + size]:
            total = total + ref[...].astype(F32)
        out_ref[...] = total.astype(BF16)
        at += size


def sums(*groups):
    return call(
        functools.partial(sum_kernel, [len(g) for g in groups]),
        2,
        [jax.ShapeDtypeStruct(g[0].shape, BF16) for g in groups],
    )(*[a for g in groups for a in g])


def halves_kernel(fore_ref, back_ref, top_ref, bottom_ref):
    top_ref[...] = fore_ref[0:TOP_ROWS, :]
    bottom_ref[...] = back_ref[TOP_ROWS:, :]


def halves_of(fore, back):
    rows, cols = fore.shape
    return call(
        halves_kernel,
        2,
        [
            jax.ShapeDtypeStruct((TOP_ROWS, cols), BF16),
            jax.ShapeDtypeStruct((rows - TOP_ROWS, cols), BF16),
        ],
    )(fore, back)


def join_kernel(near_f_ref, top_ref, near_b_ref, bottom_ref, fore_ref, back_ref):
    top = near_f_ref[0:TOP_ROWS, :].astype(F32) + top_ref[...].astype(F32)
    fore_ref[0:TOP_ROWS, :] = top.astype(BF16)
    fore_ref[TOP_ROWS:, :] = near_f_ref[TOP_ROWS:, :]
    back_ref[0:TOP_ROWS, :] = near_b_ref[0:TOP_ROWS, :]
    bottom = near_b_ref[TOP_ROWS:, :].astype(F32) + bottom_ref[...].astype(F32)
    back_ref[TOP_ROWS:, :] = bottom.astype(BF16)


def join(near_f, top, near_b, bottom):
    shape = jax.ShapeDtypeStruct(near_f.shape, BF16)
    return call(join_kernel, 2, [shape, shape])(near_f, top, near_b, bottom)


def attach_kernel(fore_ref, meta_f_ref, back_ref, meta_b_ref, fore_out, back_out):
    rows = fore_ref.shape[0]
    for ref, meta_ref, out_ref in (
        (fore_ref, meta_f_ref, fore_out),
        (back_ref, meta_b_ref, back_out),
    ):
        out_ref[0:rows, :] = ref[...]
        out_ref[rows:, :] = meta_ref[...]


def attach(fore, meta_f, back, meta_b):
    rows, cols = fore.shape
    shape = jax.ShapeDtypeStruct((rows + 8, cols), BF16)
    return call(attach_kernel, 2, [shape, shape])(fore, meta_f, back, meta_b)


def payload_kernel(
    capacity, ids_hbm, probs_hbm, grad_hbm, out_ref, meta_ref, ids_ref, probs_ref, sems
):
    expert_total, rows = probs_ref.shape
    cols = grad_hbm.shape[1]
    copies = [
        pltpu.make_async_copy(ids_hbm, ids_ref, sems.at[0]),
        pltpu.make_async_copy(probs_hbm, probs_ref, sems.at[1]),
        pltpu.make_async_copy(grad_hbm, out_ref.at[0:rows, :], sems.at[2]),
    ]
    for copy in copies:
        copy.start()
    experts = lax.broadcasted_iota(jnp.int32, (expert_total, rows), 0)
    row_at = lax.broadcasted_iota(jnp.int32, (rows, rows), 0)
    col_at = lax.broadcasted_iota(jnp.int32, (rows, rows), 1)
    lower = jnp.where(row_at < col_at, 1.0, 0.0).astype(BF16)
    copies[0].wait()
    ids = ids_ref[...]
    member = jnp.zeros((expert_total, rows), F32)
    for k in range(ids.shape[0]):
        member = member + jnp.where(ids[k : k + 1, :] == experts, 1.0, 0.0)
    before = jnp.dot(member.astype(BF16), lower, preferred_element_type=F32)
    slot = jnp.where((member > 0.5) & (before < capacity), before, -1.0)
    copies[1].wait()
    probs = probs_ref[...]
    high = probs.astype(BF16).astype(F32)
    parts = [slot, high, probs - high]
    pieces = [a[8 * i : 8 * i + 8] for a in parts for i in range(expert_total // 8)]
    pieces.append(jnp.zeros((8, cols - len(pieces) * rows), F32))
    meta = jnp.concatenate(pieces, axis=1).astype(BF16)
    out_ref[rows : rows + 8, :] = meta
    meta_ref[...] = meta
    copies[2].wait()


def payload_of(ids_t, probs_t, grad, capacity):
    rows, cols = grad.shape
    return call(
        functools.partial(payload_kernel, capacity),
        60,
        [
            jax.ShapeDtypeStruct((rows + 8, cols), BF16),
            jax.ShapeDtypeStruct((8, cols), BF16),
        ],
        [
            pltpu.VMEM(ids_t.shape, jnp.int32),
            pltpu.VMEM(probs_t.shape, F32),
            pltpu.SemaphoreType.DMA((3,)),
        ],
        0,
        3,
    )(ids_t, probs_t, grad)


def hidden_kernel(halves, tiles, capacity, steps, info_ref, *refs):
    block_refs = refs[: len(halves)]
    weight_ref, placed_ref = refs[len(halves)], refs[-1]
    out_refs = refs[len(halves) + 1 : -1]
    core, tile, row = info_ref[0], info_ref[1], info_ref[2]
    blocks, at = [], 0
    while at < len(halves):
        size = 2 if halves[at] else 1
        blocks.append(block_refs[at : at + size])
        at += size
    rows = 128
    units = weight_ref.shape[1]

    def pick(meta, kind, which):
        value = meta[:, kind * tiles * rows : (kind * tiles + 1) * rows]
        for i in range(1, tiles):
            at_lane = (kind * tiles + i) * rows
            value = jnp.where(tile == i, meta[:, at_lane : at_lane + rows], value)
        line = lax.broadcasted_iota(jnp.int32, (8, rows), 0)
        return jnp.sum(jnp.where(line == which, value, 0.0), axis=0, keepdims=True)

    slot_at = lax.broadcasted_iota(jnp.int32, (capacity, rows), 0).astype(F32)
    for step in steps:
        expert = 1 - core if step == 0 else core
        for b, block in enumerate(blocks):
            last = block[-1]
            meta = last[last.shape[0] - 8 :, :].astype(F32)
            match = jnp.where(slot_at == pick(meta, 0, row + expert), 1.0, 0.0).astype(BF16)
            if len(block) == 1:
                data = block[0][0:rows, :]
            else:
                data = jnp.concatenate([block[0][...], block[1][0 : rows - TOP_ROWS, :]], axis=0)
            placed = jnp.dot(match, data, preferred_element_type=F32)
            placed_ref[step, b * capacity : (b + 1) * capacity, :] = placed.astype(BF16)
            if step == 1:
                lines = [pick(meta, 0, row), pick(meta, 0, row + 1)]
                lines += [pick(meta, 1, row) + pick(meta, 2, row)]
                lines += [pick(meta, 1, row + 1) + pick(meta, 2, row + 1)]
                lines += [jnp.zeros((4, rows), F32)]
                out_refs[-1][8 * b : 8 * b + 8, :] = jnp.concatenate(lines, axis=0)
        out_ref = out_refs[steps.index(step)]
        for n in range(0, units, 256):
            value = lax.dot_general(
                placed_ref[step],
                weight_ref[expert, n : n + 256, :],
                LAST,
                preferred_element_type=F32,
            )
            out_ref[:, n : n + 256] = value.astype(BF16)


def hidden_part(info, blocks, down_weight, tiles, capacity, steps):
    local_count, hidden_units, cols = down_weight.shape
    flat, halves = [], []
    for block in blocks:
        pair = isinstance(block, tuple)
        flat += list(block) if pair else [block]
        halves += [pair, pair] if pair else [False]
    count = len(blocks)
    shape = (count * capacity, hidden_units)
    return call(
        functools.partial(hidden_kernel, halves, tiles, capacity, steps),
        10,
        [jax.ShapeDtypeStruct(shape, BF16)] * len(steps)
        + [jax.ShapeDtypeStruct((8 * count, 128), F32)] * (1 in steps),
        [pltpu.VMEM((2, count * capacity, cols), BF16)],
        1,
    )(info, *flat, down_weight)


def grad_kernel(counts, chunk, split, tiles, capacity, info_ref, *refs):
    groups = len(counts)
    total = sum(counts)
    hidden_refs = refs[: 3 * groups]
    gate_ref, up_ref, gate_w_ref, up_w_ref = refs[3 * groups : 3 * groups + 4]
    out_refs = refs[3 * groups + 4 : -2]
    dgate_ref, dup_ref = refs[-2:]
    core, tile, row = info_ref[0], info_ref[1], info_ref[2]
    rows = 128
    cols = gate_w_ref.shape[1]
    line = lax.broadcasted_iota(jnp.int32, (8, rows), 0)
    slot_at = lax.broadcasted_iota(jnp.int32, (capacity, rows), 0).astype(F32)
    combine, scores = [], []
    b = 0
    for g in range(groups):
        full_ref, pair_ref, meta_ref = hidden_refs[3 * g : 3 * g + 3]
        for i in range(counts[g]):
            span = slice(i * capacity, (i + 1) * capacity)
            store = slice(b * capacity, (b + 1) * capacity)
            saved = pl.ds(pl.multiple_of(info_ref[INFO_BLOCKS + chunk[b]] * capacity, capacity), capacity)
            lines = meta_ref[8 * i : 8 * i + 8, :]
            score_rows = jnp.zeros((8, rows), F32)
            stacked = []
            for e in range(2):
                hidden = jnp.where(core == e, full_ref[span, :], pair_ref[span, :]).astype(F32)
                gate = gate_ref[e, saved, :].astype(F32)
                up = up_ref[e, saved, :].astype(F32)
                active, slope_term = silu_parts(gate)
                dup = hidden * active
                match = slot_at == lines[e : e + 1, :]
                weight = jnp.sum(
                    jnp.where(match, lines[2 + e : 3 + e, :], 0.0), axis=1, keepdims=True
                )
                dgate_ref[e, store, :] = (hidden * up * slope_term * weight).astype(BF16)
                dup_ref[e, store, :] = (dup * weight).astype(BF16)
                score = jnp.sum(up * dup.astype(BF16).astype(F32), axis=1, keepdims=True)
                score = score.astype(BF16).astype(F32)
                token_score = jnp.sum(jnp.where(match, score, 0.0), axis=0, keepdims=True)
                score_rows = score_rows + jnp.where(line == row + e, token_score, 0.0)
                stacked.append(jnp.where(match, 1.0, 0.0).astype(BF16))
            combine.append(jnp.concatenate(stacked, axis=0))
            scores.append(score_rows)
            b += 1
    for n in range(0, cols, 1280):
        grads = []
        for e in range(2):
            value = lax.dot_general(
                dgate_ref[e], gate_w_ref[e, n : n + 1280, :], LAST, preferred_element_type=F32
            )
            value = value + lax.dot_general(
                dup_ref[e], up_w_ref[e, n : n + 1280, :], LAST, preferred_element_type=F32
            )
            grads.append(value.astype(BF16))
        for b in range(total):
            span = slice(b * capacity, (b + 1) * capacity)
            pile = jnp.concatenate([g[span] for g in grads], axis=0)
            value = lax.dot_general(combine[b], pile, FIRST, preferred_element_type=F32)
            if n == 0:
                lanes = [jnp.where(tile == i, scores[b], 0.0) for i in range(tiles)]
                lanes = jnp.concatenate(lanes + [jnp.zeros((8, 1280 - tiles * rows), F32)], axis=1)
            else:
                lanes = jnp.zeros((8, 1280), F32)
            if split:
                out_refs[2 * b][:, n : n + 1280] = value[:TOP_ROWS].astype(BF16)
                low = jnp.concatenate([value[TOP_ROWS:], lanes], axis=0)
                out_refs[2 * b + 1][:, n : n + 1280] = low.astype(BF16)
            else:
                out_refs[b][:, n : n + 1280] = jnp.concatenate([value, lanes], axis=0).astype(BF16)


def grad_part(info, parts, saved, weights, counts, chunk, split, tiles, capacity):
    local_count, cols, hidden_units = weights[0].shape
    total = sum(counts)
    heights = [TOP_ROWS, 136 - TOP_ROWS] * total if split else [136] * total
    return call(
        functools.partial(grad_kernel, counts, chunk, split, tiles, capacity),
        14,
        [jax.ShapeDtypeStruct((h, cols), BF16) for h in heights],
        [
            pltpu.VMEM((2, total * capacity, hidden_units), BF16),
            pltpu.VMEM((2, total * capacity, hidden_units), BF16),
        ],
        1,
    )(info, *parts, *saved, *weights)


def shared_spans(info_ref, cols):
    here = info_ref[3]
    return [
        pl.ds(pl.multiple_of(jnp.bitwise_xor(here, q) * cols, cols), cols) for q in range(4)
    ]


def shared_inner_kernel(info_ref, *refs):
    token_refs, (gate_ref, up_ref, active_ref, slope_ref) = refs[0:4], refs[4:]
    rows, cols = token_refs[0].shape
    units = gate_ref.shape[1]
    spans = shared_spans(info_ref, cols)
    gate_pre = jnp.zeros((rows, units), F32)
    up_pre = jnp.zeros((rows, units), F32)
    for q in range(4):
        token = token_refs[q][...]
        gate_pre = gate_pre + jnp.dot(token, gate_ref[spans[q], :], preferred_element_type=F32)
        up_pre = up_pre + jnp.dot(token, up_ref[spans[q], :], preferred_element_type=F32)
    active, slope_term = silu_parts(gate_pre)
    active_ref[...] = active
    slope_ref[...] = up_pre * slope_term


def shared_inner(info, token_blocks, shared_gate, shared_up):
    shape = jax.ShapeDtypeStruct((token_blocks[0].shape[0], shared_gate.shape[1]), F32)
    return call(shared_inner_kernel, 8, [shape, shape], (), 1)(
        info, *token_blocks, shared_gate, shared_up
    )


def shared_slopes_kernel(info_ref, *refs):
    grad_refs, (down_ref, active_ref, slope_ref, dgate_ref, dup_ref) = refs[0:4], refs[4:]
    rows, cols = grad_refs[0].shape
    spans = shared_spans(info_ref, cols)
    hidden_pre = jnp.zeros((rows, down_ref.shape[0]), F32)
    for q in range(4):
        hidden_pre = hidden_pre + lax.dot_general(
            grad_refs[q][...], down_ref[:, spans[q]], LAST, preferred_element_type=F32
        )
    dgate_ref[...] = (hidden_pre * slope_ref[...]).astype(BF16)
    dup_ref[...] = (hidden_pre * active_ref[...]).astype(BF16)


def shared_slopes(info, grad_blocks, shared_down, active, slope):
    shape = jax.ShapeDtypeStruct(active.shape, BF16)
    return call(shared_slopes_kernel, 8, [shape, shape], (), 1)(
        info, *grad_blocks, shared_down, active, slope
    )


def shared_terms_kernel(which, info_ref, dgate_ref, dup_ref, gate_ref, up_ref, *out_refs):
    cols = out_refs[0].shape[1]
    spans = shared_spans(info_ref, cols)
    dgate, dup = dgate_ref[...], dup_ref[...]
    for out_ref, q in zip(out_refs, which):
        term = lax.dot_general(dgate, gate_ref[spans[q], :], LAST, preferred_element_type=F32)
        term = term + lax.dot_general(dup, up_ref[spans[q], :], LAST, preferred_element_type=F32)
        out_ref[...] = term.astype(BF16)


def shared_terms(info, dgate, dup, shared_gate, shared_up, cols, which):
    shape = jax.ShapeDtypeStruct((dgate.shape[0], cols), BF16)
    kernel = functools.partial(shared_terms_kernel, which)
    return call(kernel, 8, [shape] * len(which), (), 1)(info, dgate, dup, shared_gate, shared_up)


def ring_place(position):
    position = position % 8
    return jnp.where(position < 4, 2 * position, 15 - 2 * position)


def per_device_ring(
    tokens,
    out_grad,
    expert_ids,
    router_probs,
    router_weight,
    gate_weight,
    up_weight,
    down_weight,
    gate_saved,
    up_saved,
    shared_gate,
    shared_up,
    shared_down,
):
    slot_count = gate_saved.shape[1]
    capacity = slot_count // 8
    rows, cols = tokens.shape
    expert_total = router_probs.shape[1]
    tiles = expert_total // 8
    order = [0, 2, 4, 6, 7, 5, 3, 1]
    ahead = [(order[i], order[(i + 1) % 8]) for i in range(8)]
    behind = [(order[i], order[(i - 1) % 8]) for i in range(8)]
    x_pairs = [(i, i ^ 2) for i in range(4)]
    core_pairs = [(i, i ^ 1) for i in range(4)]
    me = lax.axis_index("expert")
    place = jnp.where(me % 2 == 0, me // 2, 7 - me // 2)
    here = lax.axis_index("tensor")
    first = me * 2
    base = [here % 2, first // 8, first % 8]
    tie = lax.optimization_barrier

    def swap_x(a):
        return lax.ppermute(a, "tensor", x_pairs)

    def swap_core(a):
        return lax.ppermute(a, "tensor", core_pairs)

    def ring(fore, back):
        return lax.ppermute(fore, "expert", ahead), lax.ppermute(back, "expert", behind)

    def hidden(blocks, steps=(0, 1)):
        return hidden_part(info, blocks, down_weight, tiles, capacity, steps)

    def grads(saved, weights, *parts):
        chunk = sum((part[0] for part in parts), ())
        return grad_part(
            info,
            [a for part in parts for a in part[1:]],
            saved,
            weights,
            [len(part[0]) for part in parts],
            chunk,
            chunk == (4,),
            tiles,
            capacity,
        )

    numbers = base + [here] + [ring_place(place + d) for d in range(-3, 5)]
    info = jnp.stack([jnp.asarray(n, jnp.int32) for n in numbers])
    payload, meta = payload_of(expert_ids.T, router_probs.T, out_grad, capacity)

    fore, back = ring(out_grad, out_grad)
    meta_f, meta_b = ring(meta, meta)
    grad_x = swap_x(out_grad)
    fore, back, grad_x, meta_f, meta_b, info = tie((fore, back, grad_x, meta_f, meta_b, info))
    fore1, back1 = attach(fore, meta_f, back, meta_b)

    fore, back = ring(fore1, back1)
    tok_x = swap_x(tokens)
    other1, mine1, meta1 = hidden([payload, fore1, back1])
    fore2, back2, other1, mine1 = tie((fore, back, other1, mine1))

    fore, back = ring(fore2, back2)
    (chip1,) = sums((mine1, swap_core(other1)))
    fore2, tok_x = tie((fore2, tok_x))
    other2, mine2, meta2 = hidden([fore2, back2])
    (chip2,) = sums((mine2, swap_core(other2)))
    fore3, back3, chip1, chip2 = tie((fore, back, chip1, chip2))

    top, bottom = ring(*halves_of(fore3, back3))
    far2 = swap_x(chip2)
    other3, mine3, meta3 = hidden([fore3, back3])
    tok_both = swap_core(tok_x)
    tok_core = swap_core(tokens)
    top, bottom, chip2, other3, mine3, out_grad = tie(
        (top, bottom, chip2, other3, mine3, out_grad)
    )

    (other4,) = hidden([(top, bottom)], (0,))
    top, bottom, other4, other3, far2, tok_core, tok_both = tie(
        (top, bottom, other4, other3, far2, tok_core, tok_both)
    )
    swapped4 = swap_core(other4)
    mine4, meta4 = hidden([(top, bottom)], (1,))
    swapped3 = swap_core(other3)
    (chip4,) = sums((mine4, swapped4))
    chip4, swapped3, mine3, tok_in = tie((chip4, swapped3, mine3, tokens))
    far4 = swap_x(chip4)
    (chip3,) = sums((mine3, swapped3))
    far3 = swap_x(chip3)
    chip3, tok_in = tie((chip3, tok_in))
    active, slope = shared_inner(
        info, [tok_in, tok_core, tok_x, tok_both], shared_gate, shared_up
    )
    active, slope, chip2, far2 = tie((active, slope, chip2, far2))
    (full2,) = sums((chip2, far2))
    pair2 = swap_core(full2)
    far4, full2, active = tie((far4, full2, active))
    (full4,) = sums((chip4, far4))
    pair4 = swap_core(full4)
    saved = (gate_saved, up_saved)
    weights = (gate_weight, up_weight)
    top, bottom = grads(saved, weights, ((4,), full4, pair4, meta4))

    top, bottom, pair2, full2, far3, out_grad, chip1 = tie(
        (top, bottom, pair2, full2, far3, out_grad, chip1)
    )
    fore, back = ring(top, bottom)
    grad_core = swap_core(out_grad)
    far1 = swap_x(chip1)
    (full3,) = sums((chip3, far3))
    pair3 = swap_core(full3)
    near_b3, near_f3, near_b2, near_f2 = grads(
        saved, weights, ((-3, 3), full3, pair3, meta3), ((-2, 2), full2, pair2, meta2)
    )
    fore, back, near_f3, near_b3, near_f2, near_b2, grad_core, grad_in = tie(
        (fore, back, near_f3, near_b3, near_f2, near_b2, grad_core, out_grad)
    )

    fore, back = join(near_f3, fore, near_b3, back)
    fore, back = ring(fore, back)
    grad_both = swap_core(grad_x)
    grad_in, far1 = tie((grad_in, far1))
    dgate, dup = shared_slopes(
        info, [grad_in, grad_core, grad_x, grad_both], shared_down, active, slope
    )
    term3, term2 = shared_terms(info, dgate, dup, shared_gate, shared_up, cols, (3, 2))
    swapped = swap_core(term3)
    term3, dgate, dup = tie((term3, dgate, dup))
    term1, term0 = shared_terms(info, dgate, dup, shared_gate, shared_up, cols, (1, 0))
    fore, back, term1, term0, swapped, chip1, far1 = tie(
        (fore, back, term1, term0, swapped, chip1, far1)
    )

    fore, back, far = sums((near_f2, fore), (near_b2, back), (term2, swapped))
    fore, back = ring(fore, back)
    shared_far = swap_x(far)
    near = swap_core(term1)
    (full1,) = sums((chip1, far1))
    pair1 = swap_core(full1)
    near0, near_b1, near_f1 = grads(saved, weights, ((0, -1, 1), full1, pair1, meta1))
    fore, back, near, near0, near_b1, near_f1 = tie(
        (fore, back, near, near0, near_b1, near_f1)
    )

    fore, back = sums((near_f1, fore), (near_b1, back))
    fore, back = ring(fore, back)
    total = near0.astype(F32) + fore.astype(F32) + back.astype(F32)
    shared_part = term0.astype(F32) + near.astype(F32) + shared_far.astype(F32)
    prob_grad = jnp.concatenate(
        [total[rows:, i * rows : (i + 1) * rows] for i in range(tiles)], axis=0
    ).T
    gate_total = jnp.sum(router_probs * prob_grad, axis=1, keepdims=True)
    logit_grad = (router_probs * (prob_grad - gate_total)).astype(BF16)
    router_part = jnp.einsum("te,de->td", logit_grad, router_weight, preferred_element_type=F32)
    return (shared_part + total[:rows] + router_part).astype(BF16)


def per_device(*args):
    tokens, router_probs, gate_weight, gate_saved = args[0], args[3], args[5], args[8]
    rows, cols = tokens.shape
    expert_total = router_probs.shape[1]
    ring = (
        lax.axis_size("expert") == 8
        and lax.axis_size("tensor") == 4
        and gate_weight.shape[0] == 2
        and gate_saved.shape[1] == 8 * 64
        and gate_saved.shape[2] % 256 == 0
        and rows == 128
        and expert_total == 16
        and cols % 256 == 0
        and cols >= 6 * rows
    )
    return (per_device_ring if ring else per_device_wide)(*args)


def solution(mesh):

    return jax.shard_map(
        per_device,
        mesh=mesh,
        in_specs=(
            P("expert", "tensor"),
            P("expert", "tensor"),
            P("expert", None),
            P("expert", None),
            P("tensor", None),
            P("expert", "tensor", None),
            P("expert", "tensor", None),
            P("expert", None, "tensor"),
            P("expert", None, None),
            P("expert", None, None),
            P(None, "tensor"),
            P(None, "tensor"),
            P("tensor", None),
        ),
        out_specs=P("expert", "tensor"),
        check_vma=False,
    )
```
